32 devices in a mesh: dp: 8 (over y, x, core), tensor: 4 (over z).
Axes of the slice: x: 2, y: 2, z: 4, core: 2. Of those that a mesh axis runs over, the one named last changes fastest.
Arguments:
- activations: bfloat16 [16384, 1536], P('dp'), may hold values from -6 to 6
- cotangent: bfloat16 [16384, 1536], P('dp'), may hold values from -11 to 11
- in_weight: float32 [1536, 2, 3072], P('dp', None, 'tensor'), may hold values from -0.15947199 to 0.15947199
- in_first: float32 [1536, 2, 3072], P('dp', None, 'tensor'), may hold values from -64 to 64
- in_second: float32 [1536, 2, 3072], P('dp', None, 'tensor'), may hold values from 491.52 to 1966.08
- step_weight: float32 [1536, 48], P('dp', 'tensor'), may hold values from -0.15625 to 0.15625
- step_first: float32 [1536, 48], P('dp', 'tensor'), may hold values from -64 to 64
- step_second: float32 [1536, 48], P('dp', 'tensor'), may hold values from 491.52 to 1966.08
- out_weight: float32 [3072, 1536], P('tensor', 'dp'), may hold values from -0.109375 to 0.109375
- out_first: float32 [3072, 1536], P('tensor', 'dp'), may hold values from -64 to 64
- out_second: float32 [3072, 1536], P('tensor', 'dp'), may hold values from 491.52 to 1966.08
- state_weight: float32 [1536, 256], P(('dp', 'tensor')), may hold values from -0.15625 to 0.15625
- state_first: float32 [1536, 256], P(('dp', 'tensor')), may hold values from -64 to 64
- state_second: float32 [1536, 256], P(('dp', 'tensor')), may hold values from 491.52 to 1966.08
- conv_weight: float32 [4, 3328], P(None, ('dp', 'tensor')), may hold values from -3 to 3
- conv_first: float32 [4, 3328], P(None, ('dp', 'tensor')), may hold values from -80 to 80
- conv_second: float32 [4, 3328], P(None, ('dp', 'tensor')), may hold values from 819.2 to 3276.8
- conv_bias: float32 [3328], P(('dp', 'tensor')), may hold values from -3 to 3
- bias_first: float32 [3328], P(('dp', 'tensor')), may hold values from -80 to 80
- bias_second: float32 [3328], P(('dp', 'tensor')), may hold values from 819.2 to 3276.8
- gain_vector: float32 [4608], P(('dp', 'tensor')), may hold values from 0.5 to 1.5
- gains_first: float32 [4608], P(('dp', 'tensor')), may hold values from -80 to 80
- gains_second: float32 [4608], P(('dp', 'tensor')), may hold values from 819.2 to 3276.8
- head_params: float32 [3, 48], replicated, may hold values from -6 to 1.5, as said below
- head_first: float32 [3, 48], replicated, may hold values from -80 to 80
- head_second: float32 [3, 48], replicated, may hold values from 819.2 to 3276.8
Outputs:
- block_output: bfloat16 [16384, 1536], P('dp')
- input_grad: float32 [16384, 1536], P('dp')
- in_updated: float32 [1536, 2, 3072], P('dp', None, 'tensor')
- in_moment: float32 [1536, 2, 3072], P('dp', None, 'tensor')
- in_square: float32 [1536, 2, 3072], P('dp', None, 'tensor')
- step_updated: float32 [1536, 48], P('dp', 'tensor')
- step_moment: float32 [1536, 48], P('dp', 'tensor')
- step_square: float32 [1536, 48], P('dp', 'tensor')
- out_updated: float32 [3072, 1536], P('tensor', 'dp')
- out_moment: float32 [3072, 1536], P('tensor', 'dp')
- out_square: float32 [3072, 1536], P('tensor', 'dp')
- state_updated: float32 [1536, 256], P(('dp', 'tensor'))
- state_moment: float32 [1536, 256], P(('dp', 'tensor'))
- state_square: float32 [1536, 256], P(('dp', 'tensor'))
- conv_updated: float32 [4, 3328], P(None, ('dp', 'tensor'))
- conv_moment: float32 [4, 3328], P(None, ('dp', 'tensor'))
- conv_square: float32 [4, 3328], P(None, ('dp', 'tensor'))
- bias_updated: float32 [3328], P(('dp', 'tensor'))
- bias_moment: float32 [3328], P(('dp', 'tensor'))
- bias_square: float32 [3328], P(('dp', 'tensor'))
- gains_updated: float32 [4608], P(('dp', 'tensor'))
- gains_moment: float32 [4608], P(('dp', 'tensor'))
- gains_square: float32 [4608], P(('dp', 'tensor'))
- head_updated: float32 [3, 48], replicated
- head_moment: float32 [3, 48], replicated
- head_square: float32 [3, 48], replicated
The draws below stay inside these ranges and needn't reach their ends.
Inputs may be any that keep to these rules, and one draw needn't show every extreme that they name: `head_params`: row 0 the logarithms of the decay rates, row 1 the biases of the step sizes, row 2 the skip factors.
All inputs are finite; a program needn't handle non-finite values.
Results may differ from the reference program's by a relative error of at most 0.03.
Values may be sent and summed in bfloat16 or wider, within the bound.
A program may use at most 256 MiB of HBM per device.

```python
import math
import jax
import jax.numpy as jnp
from jax import lax

D = 1536
HEADS = 48
STATE = 128
KCONV = 4
SPAN = 256
LENGTH = 1024
STEP = 5
INNER = 3072
CONV = 3328
TOKENS = 16384


def draw_cotangent(key, part):
    key = jax.random.fold_in(key, 11)
    position = jnp.arange(TOKENS, dtype=jnp.float32)[:, None] / TOKENS
    noise = jnp.clip(jax.random.normal(key, (TOKENS, D), jnp.float32), -6.0, 6.0)
    factor = 0.6 + 1.2 * position
    return (noise * factor).astype(jnp.bfloat16)


def draw_in_weight(key, part):
    key = jax.random.fold_in(key, 12)
    column = jnp.arange(INNER, dtype=jnp.float32)[None, None, :] / INNER
    noise = jnp.clip(jax.random.normal(key, (D, 2, INNER), jnp.float32), -5.0, 5.0)
    factor = 0.75 + 0.5 * column
    return (noise * factor / math.sqrt(D)).astype(jnp.float32)


def draw_head_params(key, part):
    key = jax.random.fold_in(key, 13)
    keys = jax.random.split(key, 3)
    logs = jax.random.uniform(keys[0], (HEADS,), jnp.float32, -1.0, 1.5)
    biases = jax.random.uniform(keys[1], (HEADS,), jnp.float32, -6.0, -2.0)
    skips = jax.random.uniform(keys[2], (HEADS,), jnp.float32, 0.5, 1.5)
    return jnp.stack([logs, biases, skips]).astype(jnp.float32)


def steps_of(stream_key, extent, shards, low, largest):
    def one(dim, shards_of):
        draws = jax.random.uniform(jax.random.fold_in(jax.random.fold_in(stream_key, 6), dim), (shards_of,), jnp.float32, low / len(shards), largest / len(shards))
        return jnp.repeat(jnp.exp(draws), extent[dim] // shards_of).reshape((-1,) + (1,) * (len(extent) - dim - 1))

    level = one(*shards[0])
    for cut in shards[1:]:
        level = level * one(*cut)
    return level


def centred(key, shape, width, bound, shards=(), kind=jnp.bfloat16):
    entries = width * jax.random.normal(key, shape, jnp.float32)
    if shards:
        entries = entries * steps_of(key, shape, shards, -0.22, 0.18)
    return jnp.clip(entries, -bound, bound).astype(kind)


def setup_inputs(seed: int = 0) -> dict:
    arg_keys = jax.random.split(jax.random.key(seed), 27)
    return {
        "activations": centred(arg_keys[0], (TOKENS, D), 1.0, 6.0, ((0, 8),)),
        "cotangent": draw_cotangent(jax.random.fold_in(arg_keys[26], 71), 0),
        "in_weight": draw_in_weight(jax.random.fold_in(arg_keys[26], 71), 0),
        "in_first": centred(arg_keys[3], (D, 2, INNER), (0.08 * TOKENS ** 0.5), 64.0, ((0, 8), (2, 4)), jnp.float32),
        "in_second": jnp.clip(jnp.exp(math.log(1966.08) - 1.3862944 * jax.random.uniform(arg_keys[4], (D, 2, INNER), jnp.float32) ** steps_of(arg_keys[4], (D, 2, INNER), ((0, 8), (2, 4)), -0.2, 0.2)), 491.52, 1966.08),
        "step_weight": centred(arg_keys[5], (D, HEADS), D ** -0.5, 0.15625, ((0, 8), (1, 4)), jnp.float32),
        "step_first": centred(arg_keys[6], (D, HEADS), (0.08 * TOKENS ** 0.5), 64.0, ((0, 8), (1, 4)), jnp.float32),
        "step_second": jnp.clip(jnp.exp(math.log(1966.08) - 1.3862944 * jax.random.uniform(arg_keys[7], (D, HEADS), jnp.float32) ** steps_of(arg_keys[7], (D, HEADS), ((0, 8), (1, 4)), -0.2, 0.2)), 491.52, 1966.08),
        "out_weight": centred(arg_keys[8], (INNER, D), INNER ** -0.5, 0.109375, ((0, 4), (1, 8)), jnp.float32),
        "out_first": centred(arg_keys[9], (INNER, D), (0.08 * TOKENS ** 0.5), 64.0, ((0, 4), (1, 8)), jnp.float32),
        "out_second": jnp.clip(jnp.exp(math.log(1966.08) - 1.3862944 * jax.random.uniform(arg_keys[10], (INNER, D), jnp.float32) ** steps_of(arg_keys[10], (INNER, D), ((0, 4), (1, 8)), -0.2, 0.2)), 491.52, 1966.08),
        "state_weight": centred(arg_keys[11], (D, 2 * STATE), D ** -0.5, 0.15625, ((0, 32),), jnp.float32),
        "state_first": centred(arg_keys[12], (D, 2 * STATE), (0.08 * TOKENS ** 0.5), 64.0, ((0, 32),), jnp.float32),
        "state_second": jnp.clip(jnp.exp(math.log(1966.08) - 1.3862944 * jax.random.uniform(arg_keys[13], (D, 2 * STATE), jnp.float32) ** steps_of(arg_keys[13], (D, 2 * STATE), ((0, 32),), -0.2, 0.2)), 491.52, 1966.08),
        "conv_weight": centred(arg_keys[14], (KCONV, CONV), KCONV ** -0.5, 3.0, ((1, 32),), jnp.float32),
        "conv_first": centred(arg_keys[15], (KCONV, CONV), (0.11 * TOKENS ** 0.5), 80.0, ((1, 32),), jnp.float32),
        "conv_second": jnp.clip(jnp.exp(math.log(3276.8) - 1.3862944 * jax.random.uniform(arg_keys[16], (KCONV, CONV), jnp.float32) ** steps_of(arg_keys[16], (KCONV, CONV), ((1, 32),), -0.2, 0.2)), 819.2, 3276.8),
        "conv_bias": centred(arg_keys[17], (CONV,), 0.5, 3.0, ((0, 32),), jnp.float32),
        "bias_first": centred(arg_keys[18], (CONV,), (0.11 * TOKENS ** 0.5), 80.0, ((0, 32),), jnp.float32),
        "bias_second": jnp.clip(jnp.exp(math.log(3276.8) - 1.3862944 * jax.random.uniform(arg_keys[19], (CONV,), jnp.float32) ** steps_of(arg_keys[19], (CONV,), ((0, 32),), -0.2, 0.2)), 819.2, 3276.8),
        "gain_vector": jnp.clip(1.0 + 0.1 * jax.random.normal(arg_keys[20], (D + INNER,), jnp.float32), 0.5, 1.5),
        "gains_first": centred(arg_keys[21], (D + INNER,), (0.11 * TOKENS ** 0.5), 80.0, ((0, 32),), jnp.float32),
        "gains_second": jnp.clip(jnp.exp(math.log(3276.8) - 1.3862944 * jax.random.uniform(arg_keys[22], (D + INNER,), jnp.float32) ** steps_of(arg_keys[22], (D + INNER,), ((0, 32),), -0.2, 0.2)), 819.2, 3276.8),
        "head_params": draw_head_params(jax.random.fold_in(arg_keys[26], 71), 0),
        "head_first": centred(arg_keys[24], (3, HEADS), (0.11 * TOKENS ** 0.5), 80.0, (), jnp.float32),
        "head_second": jnp.clip(jnp.exp(jax.random.uniform(arg_keys[25], (3, HEADS), jnp.float32, math.log(819.2), math.log(3276.8))), 819.2, 3276.8),
    }


HIGHEST = lax.Precision.HIGHEST
NORM_EPSILON = 1e-05
FIRST_DECAY = 0.9
SECOND_DECAY = 0.95
ADAM_EPSILON = 1e-08
WEIGHT_DECAY = 0.1
RATE_MATRIX = 0.05
RATE_OUTPUT = 0.04
RATE_CONV = 1.0
RATE_VECTOR = 0.5
RATE_HEADS = 2.0

@jax.custom_vjp
def low(v):
    return lax.optimization_barrier(v.astype(jnp.bfloat16)).astype(jnp.float32)

@jax.custom_vjp
def low_back(v):
    return v

def low_keep(v):
    return (low(v), None)

def low_pass(kept, grad):
    return (grad,)

def back_keep(v):
    return (v, None)

def back_low(kept, grad):
    return (low(grad),)
low.defvjp(low_keep, low_pass)
low_back.defvjp(back_keep, back_low)

def matmul(operand, factor):
    return jnp.dot(operand, factor, precision=HIGHEST, preferred_element_type=jnp.float32)

def causal_conv(values, kernel, offsets):
    length = values.shape[0]
    tap_count = kernel.shape[0]
    padded = jnp.pad(values, ((tap_count - 1, 0), (0, 0)))
    result = offsets[None, :] + kernel[0][None, :] * padded[0:length]
    for shift_tap in range(1, tap_count):
        result = result + kernel[shift_tap][None, :] * padded[shift_tap:shift_tap + length]
    return result

def state_space(values, step_sizes, decay_rates, inputs_b, inputs_c):
    length, head_count, head_width = values.shape
    block_count = length // SPAN
    causal_mask = lax.broadcasted_iota(jnp.int32, (SPAN, SPAN), 0) >= lax.broadcasted_iota(jnp.int32, (SPAN, SPAN), 1)

    def one_block(carry_state, block_piece):
        block_values, block_steps, block_b, block_c = block_piece
        decays = (block_steps * decay_rates[None, :]).T
        totals = jnp.cumsum(decays, axis=1)
        decay_gaps = jnp.where(causal_mask[None, :, :], totals[:, :, None] - totals[:, None, :], -10000.0)
        intersection = jnp.dot(block_c, block_b.T, precision=HIGHEST)
        mixing = jnp.exp(decay_gaps) * intersection[None, :, :] * block_steps.T[:, None, :]
        within = jnp.einsum('hts,shp->thp', mixing, block_values, precision=HIGHEST)
        carried = jnp.exp(totals).T[:, :, None] * jnp.einsum('tn,hpn->thp', block_c, carry_state, precision=HIGHEST)
        block_ends = totals[:, -1]
        weights = (jnp.exp(block_ends[:, None] - totals) * block_steps.T).T
        fresh_state = jnp.einsum('shp,sn->hpn', weights[:, :, None] * block_values, block_b, precision=HIGHEST)
        return (jnp.exp(block_ends)[:, None, None] * carry_state + fresh_state, within + carried)
    pieces = (values.reshape(block_count, SPAN, head_count, head_width), step_sizes.reshape(block_count, SPAN, head_count), inputs_b.reshape(block_count, SPAN, inputs_b.shape[1]), inputs_c.reshape(block_count, SPAN, inputs_c.shape[1]))
    initial = jnp.zeros((head_count, head_width, inputs_b.shape[1]), jnp.float32)
    _, outputs = lax.scan(jax.checkpoint(one_block), initial, pieces)
    return outputs.reshape(length, head_count, head_width)

def mix_sequence(gate_in, value_in, state_in, step_in, kernel, offsets, head_table, gain_row):
    length = gate_in.shape[0]
    inner_width = value_in.shape[1]
    head_count = head_table.shape[1]
    states = state_in.shape[1] // 2
    active = jax.nn.silu(causal_conv(jnp.concatenate([value_in, state_in], 1), kernel, offsets))
    channels = active[:, :inner_width].reshape(length, head_count, inner_width // head_count)
    step_sizes = jax.nn.softplus(step_in + head_table[1][None, :])
    decay_rates = -jnp.exp(head_table[0])
    output = state_space(channels, step_sizes, decay_rates, active[:, inner_width:inner_width + states], active[:, inner_width + states:])
    output = output + head_table[2][None, :, None] * channels
    gated_out = output.reshape(length, inner_width) * jax.nn.silu(gate_in)
    return (gated_out * gain_row[None, :], lax.optimization_barrier(jnp.sum(gated_out * gated_out, axis=1, keepdims=True)))

def block_forward(sequence, in_weight, step_weight, out_weight, state_weight, conv_weight, conv_bias, gain_vector, head_params):
    normed = low(sequence * lax.rsqrt(lax.optimization_barrier(jnp.mean(sequence * sequence, axis=1, keepdims=True)) + NORM_EPSILON) * gain_vector[None, :D])
    gate_value = low_back(matmul(normed, in_weight.reshape(D, 2 * INNER)))
    state_in = low_back(matmul(normed, state_weight))
    step_in = low_back(matmul(normed, step_weight))
    gated_out, squares = mix_sequence(gate_value[:, :INNER], gate_value[:, INNER:], state_in, step_in, conv_weight, conv_bias, head_params, gain_vector[D:])
    norm_scale = lax.rsqrt(squares / INNER + NORM_EPSILON)
    branch = low_back(matmul(low(gated_out), out_weight))
    return sequence + norm_scale * branch

def forward(values, in_weight, step_weight, out_weight, state_weight, conv_weight, conv_bias, gain_vector, head_params):
    in_low = low(in_weight)
    step_low = low(step_weight)
    out_low = low(out_weight)
    state_low = low(state_weight)

    def scan_step(carry_value, sequence):
        return (carry_value, block_forward(sequence, in_low, step_low, out_low, state_low, conv_weight, conv_bias, gain_vector, head_params))
    _, outputs = lax.scan(jax.checkpoint(scan_step), jnp.zeros((), jnp.float32), values.reshape(-1, LENGTH, D))
    return outputs.reshape(-1, D)

def adamw_update(weight, gradient, moment, square, step_rate, decay_rate):
    moment = FIRST_DECAY * moment + (1.0 - FIRST_DECAY) * gradient
    square = SECOND_DECAY * square + (1.0 - SECOND_DECAY) * gradient * gradient
    first_fix = 1.0 - FIRST_DECAY ** STEP
    second_fix = 1.0 - SECOND_DECAY ** STEP
    update = moment / first_fix / (jnp.sqrt(square / second_fix) + ADAM_EPSILON)
    return (weight - step_rate * (update + decay_rate * weight), moment, square)

def reference(activations, cotangent, in_weight, in_first, in_second, step_weight, step_first, step_second, out_weight, out_first, out_second, state_weight, state_first, state_second, conv_weight, conv_first, conv_second, conv_bias, bias_first, bias_second, gain_vector, gains_first, gains_second, head_params, head_first, head_second):
    block_values, pullback = jax.vjp(forward, activations.astype(jnp.float32), in_weight, step_weight, out_weight, state_weight, conv_weight, conv_bias, gain_vector, head_params)
    gradients = pullback(cotangent.astype(jnp.float32))
    in_new = adamw_update(in_weight, gradients[1], in_first, in_second, RATE_MATRIX, WEIGHT_DECAY)
    step_new = adamw_update(step_weight, gradients[2], step_first, step_second, RATE_MATRIX, WEIGHT_DECAY)
    out_new = adamw_update(out_weight, gradients[3], out_first, out_second, RATE_OUTPUT, WEIGHT_DECAY)
    state_new = adamw_update(state_weight, gradients[4], state_first, state_second, RATE_MATRIX, WEIGHT_DECAY)
    conv_new = adamw_update(conv_weight, gradients[5], conv_first, conv_second, RATE_CONV, 0.0)
    bias_new = adamw_update(conv_bias, gradients[6], bias_first, bias_second, RATE_VECTOR, 0.0)
    gains_new = adamw_update(gain_vector, gradients[7], gains_first, gains_second, RATE_VECTOR, 0.0)
    head_new = adamw_update(head_params, gradients[8], head_first, head_second, RATE_HEADS, 0.0)
    return (block_values.astype(jnp.bfloat16), gradients[0], in_new[0], in_new[1], in_new[2], step_new[0], step_new[1], step_new[2], out_new[0], out_new[1], out_new[2], state_new[0], state_new[1], state_new[2], conv_new[0], conv_new[1], conv_new[2], bias_new[0], bias_new[1], bias_new[2], gains_new[0], gains_new[1], gains_new[2], head_new[0], head_new[1], head_new[2])
```

```python
import functools

import jax
import jax.numpy as jnp
from jax import lax
from jax.experimental import pallas as pl
from jax.experimental.pallas import tpu as pltpu
from jax.sharding import PartitionSpec as P

F32 = jnp.float32
BF16 = jnp.bfloat16
MESH = pl.DeviceIdType.MESH

SPAN = 256
LENGTH = 1024
STEP = 5
LANES = 128
LOG2E = 1.4426950408889634
NORM_EPSILON = 1e-05
FIRST_DECAY = 0.9
SECOND_DECAY = 0.95
ADAM_EPSILON = 1e-08
WEIGHT_DECAY = 0.1
RATE_MATRIX = 0.05
RATE_OUTPUT = 0.04
RATE_CONV = 1.0
RATE_VECTOR = 0.5
RATE_HEADS = 2.0
MIXER_VMEM = 63 * 1024 * 1024


def mm(a, b):
    return lax.dot_general(a, b, (((1,), (0,)), ((), ())), preferred_element_type=F32)


def mm_nt(a, b):
    return lax.dot_general(a, b, (((1,), (1,)), ((), ())), preferred_element_type=F32)


def mm_exact(a, b):
    return lax.dot_general(
        a, b, (((1,), (0,)), ((), ())), preferred_element_type=F32, precision=lax.Precision.HIGHEST
    )


def sigmoid(v):
    return 1.0 / (1.0 + jnp.exp(-v))


def softplus(v):
    return jnp.maximum(v, 0.0) + jnp.log1p(jnp.exp(-jnp.abs(v)))


def split_low(v):
    high = v.astype(BF16)
    return high, (v - high.astype(F32)).astype(BF16)


def head_marks(head_width, channels):
    head = lax.broadcasted_iota(jnp.int32, (LANES, channels), 0)
    channel = lax.broadcasted_iota(jnp.int32, (LANES, channels), 1)
    inside = (channel >= head * head_width) & (channel < (head + 1) * head_width)
    return inside.astype(F32).astype(BF16)


def head_marks_t(head_width, channels):
    head = lax.broadcasted_iota(jnp.int32, (channels, LANES), 1)
    channel = lax.broadcasted_iota(jnp.int32, (channels, LANES), 0)
    inside = (channel >= head * head_width) & (channel < (head + 1) * head_width)
    return inside.astype(F32).astype(BF16)


def spread(v, marks2):
    high, low = split_low(v)
    return mm(jnp.concatenate([high, low], 1), marks2)


def gather_heads(v, marks_t2):
    high, low = split_low(v)
    return mm(jnp.concatenate([high, low], 1), marks_t2)


def causal_ones(lower):
    row = lax.broadcasted_iota(jnp.int32, (SPAN, SPAN), 0)
    col = lax.broadcasted_iota(jnp.int32, (SPAN, SPAN), 1)
    keep = row >= col if lower else row <= col
    return keep.astype(F32)


def lane_masks():
    lane = lax.broadcasted_iota(jnp.int32, (1, LANES), 1)
    first = (lane < LANES // 2).astype(F32)
    return first, 1.0 - first


def sds(shape, dtype):
    return jax.ShapeDtypeStruct(shape, dtype)


def axis_bits(size):
    count = size.bit_length() - 1
    order = list(range(1, count)) + [0]
    other = [order[1], order[0]] + order[2:] if count >= 3 else order
    return order, other


def flipped(index, mask):
    result = index
    bit = 1
    while bit <= mask:
        if mask & bit:
            result = result + bit * (1 - 2 * ((index // bit) % 2))
        bit *= 2
    return result


def gather_weights(
    w_own, st_own, sm_own, w_full, st_full, sm_full, local_sem, z_send, z_recv, send_sem, recv_sem,
    *, dp, tp, cut
):
    me = lax.axis_index("dp")
    tensor = lax.axis_index("tensor")
    rows, width = w_own.shape
    count = dp.bit_length() - 1

    barrier = pltpu.get_barrier_semaphore()
    for b in range(count):
        pl.semaphore_signal(
            barrier, inc=1, device_id=(flipped(me, 1 << b), tensor), device_id_type=MESH
        )
    for k in range(1, tp):
        pl.semaphore_signal(barrier, inc=1, device_id=(me, flipped(tensor, k)), device_id_type=MESH)
    pl.semaphore_wait(barrier, count + tp - 1)

    order, other = axis_bits(dp)
    row_of = lambda mask: pl.multiple_of(flipped(me, mask) * rows, 16)
    left, right = pl.ds(0, cut), pl.ds(cut, width - cut)

    def weight_part(columns):
        def source(mask):
            if mask == 0:
                return w_own.at[:, columns]
            return w_full.at[pl.ds(row_of(mask), rows), columns]

        return source, lambda mask: w_full.at[pl.ds(row_of(mask), rows), columns]

    state_part = (lambda mask: st_full.at[flipped(me, mask)],) * 2
    small_part = (lambda mask: sm_full.at[flipped(me, mask)],) * 2
    kinds = (
        (order, weight_part(left)),
        (other, weight_part(right)),
        (order, state_part),
        (other, small_part),
    )

    def full_mask(bits, packed):
        return sum(1 << bits[j] for j in range(count) if packed >> j & 1)

    def move(kind, packed, j):
        bits, (source, target) = kinds[kind]
        mask = full_mask(bits, packed)
        slot = packed | (1 << j)
        return pltpu.make_async_remote_copy(
            src_ref=source(mask),
            dst_ref=target(mask),
            send_sem=send_sem.at[kind, slot],
            recv_sem=recv_sem.at[kind, slot],
            device_id=(flipped(me, 1 << bits[j]), tensor),
            device_id_type=MESH,
        )

    started = []

    def start(kind, packed, j):
        copy = move(kind, packed, j)
        copy.start()
        started.append(copy)

    zs = []
    for k in range(1, tp):
        for which, (own, full) in enumerate(((st_own, st_full), (sm_own, sm_full))):
            copy = pltpu.make_async_remote_copy(
                src_ref=own,
                dst_ref=full.at[me, tensor],
                send_sem=z_send.at[which, k],
                recv_sem=z_recv.at[which, k],
                device_id=(me, flipped(tensor, k)),
                device_id_type=MESH,
            )
            copy.start()
            zs.append(copy)
    for j in range(count):
        for kind in (0, 1):
            start(kind, 0, j)
    locals_ = [
        pltpu.make_async_copy(w_own, w_full.at[pl.ds(row_of(0), rows)], local_sem.at[0]),
        pltpu.make_async_copy(st_own, st_full.at[me, tensor], local_sem.at[1]),
        pltpu.make_async_copy(sm_own, sm_full.at[me, tensor], local_sem.at[2]),
    ]
    for copy in locals_:
        copy.start()
    for copy in locals_:
        copy.wait()
    for copy in zs:
        copy.wait()
    for j in range(count):
        for kind in (3, 2):
            start(kind, 0, j)
    for packed in range(1, dp):
        top = packed.bit_length() - 1
        for kind in (0, 1, 3, 2):
            move(kind, packed & ~(1 << top), top).wait_recv()
            for j in range(top + 1, count):
                start(kind, packed, j)
    for copy in started:
        copy.wait_send()


def run_gather(w_own, st_own, sm_own, dp, tp):
    rows, width = w_own.shape
    cut = width // 2 // LANES * LANES
    hbm = pl.BlockSpec(memory_space=pl.ANY)
    return pl.pallas_call(
        functools.partial(gather_weights, dp=dp, tp=tp, cut=cut),
        in_specs=[hbm] * 3,
        out_specs=(hbm,) * 3,
        out_shape=(
            sds((dp * rows, width), BF16),
            sds((dp, tp) + st_own.shape, BF16),
            sds((dp, tp) + sm_own.shape, F32),
        ),
        scratch_shapes=[
            pltpu.SemaphoreType.DMA((3,)),
            pltpu.SemaphoreType.DMA((2, tp)),
            pltpu.SemaphoreType.DMA((2, tp)),
            pltpu.SemaphoreType.DMA((4, dp)),
            pltpu.SemaphoreType.DMA((4, dp)),
        ],
        compiler_params=pltpu.CompilerParams(collective_id=1, has_side_effects=True),
        name="gather_weights",
    )(w_own, st_own, sm_own)


def add_low(a, b):
    return (a.astype(F32) + b.astype(F32)).astype(BF16)


HALF = SPAN // 2


def forward_step(f, x, c, w_v, ws_v, pv, saved, state_v, ext, stage, stats, sizes):
    inner, head_width, heads = sizes
    cin_s, pre_s, gate_s, y_s, sp_s, state_s = saved
    states = ws_v.shape[1] // 2
    conv = inner + 2 * states

    x = x[...].astype(F32)
    inv = lax.rsqrt(jnp.mean(x * x, axis=1, keepdims=True) + NORM_EPSILON)
    normed = (x * inv * pv[0:1, :]).astype(BF16)

    step_in = mm(normed, w_v[:, 2 * inner : 2 * inner + LANES])
    sp_s[f] = step_in
    ext[8:, 0:inner] = mm(normed, w_v[:, inner : 2 * inner])
    ext[8:, inner:conv] = mm(normed, ws_v[...])
    gate = mm(normed, w_v[:, 0:inner]).astype(BF16)
    gate_s[f] = gate
    gate = gate.astype(F32)
    cin_s[f] = ext[8:, :].astype(BF16)
    pre = pv[6:7, 0:conv]
    for tap in range(4):
        pre = pre + pv[2 + tap : 3 + tap, 0:conv] * ext[5 + tap : 5 + tap + SPAN, :]
    ext[0:8, :] = ext[SPAN : SPAN + 8, :]
    pre = pre.astype(BF16)
    pre_s[f] = pre
    pre = pre.astype(F32)
    act = pre * sigmoid(pre)

    rate = pv[7:8, 0:LANES]
    dt = softplus(step_in + pv[7:8, LANES : 2 * LANES])
    total = mm_exact(causal_ones(True), dt * rate)
    total2 = total * LOG2E
    total2_t = jnp.transpose(total2)
    marks = head_marks(head_width, inner)
    marks2 = jnp.concatenate([marks, marks], 0)
    end = total[SPAN - 1 : SPAN, :]
    xc = act[:, 0:inner]
    bmat = act[:, inner : inner + states].astype(BF16)
    cmat = act[:, inner + states :].astype(BF16)
    xd = (xc * spread(dt, marks2)).astype(BF16)
    weighted = (xd.astype(F32) * spread(jnp.exp(end - total), marks2)).astype(BF16)

    state = state_v[...]
    state_low = state.astype(BF16)
    state_s[f] = state_low
    carried = spread(jnp.exp(total), marks2) * mm(cmat, state_low)
    keep = spread(jnp.broadcast_to(jnp.exp(end), (8, LANES)), marks2)[0:1, :]
    state_v[...] = keep * state + mm(jnp.transpose(bmat), weighted)

    inter = mm_nt(cmat, bmat) * causal_ones(True)
    first, second = lane_masks()
    skip = pv[1:2, inner : 2 * inner]
    parts = []
    for pair in range(heads // 2):
        lanes = slice(pair * LANES, (pair + 1) * LANES)
        xp = xd[:, lanes].astype(F32)
        within = None
        for side, mask in ((0, first), (1, second)):
            h = 2 * pair + side
            gap = jnp.minimum(total2[:, h : h + 1] - total2_t[h : h + 1, :], 0.0)
            mixing = (jnp.exp2(gap) * inter).astype(BF16)
            term = mm(mixing, (xp * mask).astype(BF16))
            within = term if within is None else within + term
        parts.append(within)
    y = jnp.concatenate(parts, 1) + carried
    y_s[f] = y
    y = y + skip * xc
    gated = y * gate * sigmoid(gate)
    squares = jnp.sum(gated * gated, axis=1, keepdims=True)
    lowered = (gated * pv[1:2, 0:inner]).astype(BF16)
    out = mm_nt(lowered, w_v[:, 2 * inner + LANES :])
    stage[...] = out.astype(BF16).reshape(stage.shape)
    dots = jnp.sum(c[...].astype(F32) * out, axis=1, keepdims=True)
    lane = lax.broadcasted_iota(jnp.int32, (SPAN, LANES), 1)
    both = jnp.where(lane == 0, squares, jnp.where(lane == 1, dots, 0.0))
    stats[...] = jnp.transpose(both)[0:8, :]


def backward_step(
    f, x, c, w_v, ws_v, pv, totals, saved, dst_v, dext, small, grads, lowered_v, turned, put, stage, sizes, norm_width
):
    inner, head_width, heads = sizes
    cin_s, pre_s, gate_s, y_s, sp_s, state_s = saved
    states = ws_v.shape[1] // 2
    conv = inner + 2 * states
    put_grads, put_lowered, put_branch, put_normed = put

    sums = jnp.transpose(jnp.concatenate([totals] * (LANES // 8), 0))
    scale = lax.rsqrt(sums[:, 0:1] / norm_width + NORM_EPSILON)
    bg = (scale * c[...].astype(F32)).astype(BF16)
    squares_grad = (-0.5 / norm_width) * sums[:, 1:2] * scale * scale * scale
    low_grad = mm(bg, w_v[:, 2 * inner + LANES :])

    pre = pre_s[f].astype(F32)
    sig_pre = sigmoid(pre)
    act = pre * sig_pre
    xc = act[:, 0:inner]
    bmat = act[:, inner : inner + states].astype(BF16)
    cmat = act[:, inner + states :].astype(BF16)

    skip = pv[1:2, inner : 2 * inner]
    gate = gate_s[f].astype(F32)
    sig = sigmoid(gate)
    y_scan = y_s[f]
    y = y_scan + skip * xc
    silu_gate = gate * sig
    gated = y * silu_gate
    gain = pv[1:2, 0:inner]
    lowered_v[...] = (gated * gain).astype(BF16)
    put_lowered.start()
    gated_grad = low_grad * gain + 2.0 * gated * squares_grad
    small[1:2, 0:inner] += jnp.sum(low_grad * gated, axis=0, keepdims=True)
    y_grad = gated_grad * silu_gate
    grads[:, 0:inner] = (gated_grad * y * sig * (1.0 + gate * (1.0 - sig))).astype(BF16)
    small[1:2, inner : 2 * inner] += jnp.sum(y_grad * xc, axis=0, keepdims=True)

    turned[...] = jnp.transpose(bg)
    put_branch.start()

    rate = pv[7:8, 0:LANES]
    step_pre = sp_s[f] + pv[7:8, LANES : 2 * LANES]
    dt = softplus(step_pre)
    total = mm_exact(causal_ones(True), dt * rate)
    total2 = total * LOG2E
    total2_t = jnp.transpose(total2)
    marks = head_marks(head_width, inner)
    marks2 = jnp.concatenate([marks, marks], 0)
    marks_t = head_marks_t(head_width, inner)
    marks_t2 = jnp.concatenate([marks_t, marks_t], 0)
    end = total[SPAN - 1 : SPAN, :]
    dt_wide = spread(dt, marks2)
    xd = (xc * dt_wide).astype(BF16)
    xd_wide = xd.astype(F32)
    end_wide = spread(jnp.exp(end - total), marks2)

    yb = y_grad.astype(BF16)
    yb_wide = yb.astype(F32)
    state_low = state_s[f]
    dst = dst_v[...]
    dst_low = dst.astype(BF16)
    carried_grad = (yb_wide * spread(jnp.exp(total), marks2)).astype(BF16)
    c_grad = mm_nt(carried_grad, state_low)
    b_state = mm(bmat, dst_low) * end_wide
    b_grad = mm_nt((xd_wide * end_wide).astype(BF16), dst_low)
    keep = spread(jnp.broadcast_to(jnp.exp(end), (8, LANES)), marks2)[0:1, :]
    end_row = jnp.sum(xd_wide * b_state, axis=0, keepdims=True) + keep * jnp.sum(
        dst * state_low.astype(F32), axis=0, keepdims=True
    )
    dst_v[...] = keep * dst + mm(jnp.transpose(cmat), carried_grad)

    causal = causal_ones(True)
    inter = mm_nt(cmat, bmat) * causal
    first, second = lane_masks()
    inter_grad = jnp.zeros((SPAN, SPAN), F32)
    yb_t = jnp.transpose(yb)
    parts = []
    for pair in range(heads // 2):
        lanes = slice(pair * LANES, (pair + 1) * LANES)
        xp = xd[:, lanes]
        yp = yb_wide[:, lanes]
        for side, mask in ((0, first), (1, second)):
            h = 2 * pair + side
            gap = jnp.minimum(total2[:, h : h + 1] - total2_t[h : h + 1, :], 0.0)
            fade = jnp.exp2(gap)
            mixing = (fade * inter).astype(BF16)
            inter_grad = inter_grad + mm_nt((yp * mask).astype(BF16), xp) * fade
            parts.append(mm(yb_t[h * head_width : (h + 1) * head_width, :], mixing))
    xd_grad = jnp.transpose(jnp.concatenate(parts, 0)) + b_state
    inter_low = (inter_grad * causal).astype(BF16)
    c_grad = c_grad + mm(inter_low, bmat)
    b_grad = b_grad + mm(jnp.transpose(inter_low), cmat)

    rows = gather_heads(yb_wide * y_scan - xd_wide * xd_grad, marks_t2)
    end_sum = gather_heads(jnp.broadcast_to(end_row, (8, inner)), marks_t2)[0:1, :]
    decay_grad = mm_exact(causal_ones(False), rows) + end_sum
    dt_grad = decay_grad * rate + gather_heads(xc * xd_grad, marks_t2)
    small[7:8, 0:LANES] += jnp.sum(decay_grad * dt, axis=0, keepdims=True) * rate
    step_grad = dt_grad * sigmoid(step_pre)
    small[7:8, LANES : 2 * LANES] += jnp.sum(step_grad, axis=0, keepdims=True)
    grads[:, conv + inner :] = step_grad.astype(BF16)

    x_grad = xd_grad * dt_wide + skip * y_grad
    act_grad = jnp.concatenate([x_grad, b_grad, c_grad], 1)
    pre = pre_s[f].astype(F32)
    sig_pre = sigmoid(pre)
    pre_grad = act_grad * sig_pre * (1.0 + pre * (1.0 - sig_pre))
    dext[0:SPAN, :] = pre_grad
    small[6:7, 0:conv] += jnp.sum(pre_grad, axis=0, keepdims=True)
    conv_in = cin_s[f].astype(F32)
    conv_grad = None
    for tap in range(4):
        shifted = dext[3 - tap : 3 - tap + SPAN, :]
        term = pv[2 + tap : 3 + tap, 0:conv] * shifted
        conv_grad = term if conv_grad is None else conv_grad + term
        small[2 + tap : 3 + tap, 0:conv] += jnp.sum(conv_in * shifted, axis=0, keepdims=True)
    dext[SPAN:, :] = dext[0:8, :]
    grads[:, inner : inner + conv] = conv_grad.astype(BF16)

    normed_grad = mm_nt(grads[:, 0 : 2 * inner], w_v[:, 0 : 2 * inner])
    normed_grad = normed_grad + mm_nt(grads[:, 2 * inner : inner + conv], ws_v[...])
    normed_grad = normed_grad + mm_nt(
        grads[:, inner + conv :], w_v[:, 2 * inner : 2 * inner + LANES]
    )
    x = x[...].astype(F32)
    inv = lax.rsqrt(jnp.mean(x * x, axis=1, keepdims=True) + NORM_EPSILON)
    scaled_x = x * inv
    small[0:1, :] += jnp.sum(normed_grad * scaled_x, axis=0, keepdims=True)
    scaled = normed_grad * pv[0:1, :]
    inner_mean = jnp.mean(x * scaled, axis=1, keepdims=True)
    part = inv * scaled - x * (inv * inv * inv * inner_mean)
    stage[...] = part.astype(BF16).reshape(stage.shape)

    put_branch.wait()
    turned[...] = jnp.transpose((scaled_x * pv[0:1, :]).astype(BF16))
    put_normed.start()
    put_grads.start()


def mixer(
    x_hbm,
    c_hbm,
    w_hbm,
    ws_hbm,
    pv,
    edge,
    across,
    mine,
    rs1,
    rs2,
    grads_hbm,
    lowered_hbm,
    branch_hbm,
    normed_hbm,
    own,
    vectors,
    head_sums,
    totals,
    w_v,
    ws_v,
    xbuf,
    cbuf,
    cin_s,
    pre_s,
    gate_s,
    y_s,
    sp_s,
    state_s,
    state_v,
    dst_v,
    ext,
    wgrad,
    tiles,
    small,
    grads,
    lowered_v,
    turned,
    stage,
    landed,
    mine_v,
    pair,
    total_v,
    rsv,
    stat_own,
    stat_in,
    small1,
    small2,
    small3,
    w_sem,
    load_sem,
    edge_send,
    edge_recv,
    across_send,
    across_recv,
    keep_sem,
    mine_sem,
    pump_sem,
    stat_send,
    stat_recv,
    rs1_send,
    rs1_recv,
    rs2_send,
    rs2_recv,
    rs_sem,
    put_sem,
    tile_sem,
    sm_send,
    sm_recv,
    *,
    dp,
    tp,
    sizes,
    norm_width,
):
    me = lax.axis_index("dp")
    z = lax.axis_index("tensor")
    inner, head_width, heads = sizes
    tokens, depth = x_hbm.shape
    blocks = tokens // SPAN
    per = LENGTH // SPAN
    sequences = blocks // per
    cycle = 2 * per
    pieces = 2 * blocks
    half = dp // 2
    rows = depth // dp
    conv = inner + ws_hbm.shape[1]
    wide = inner + conv + LANES
    saved = (cin_s, pre_s, gate_s, y_s, sp_s, state_s)
    parity = lax.rem(me, 2)
    chip = me // 2
    sibling = me + 1 - 2 * parity
    is_middle = (z == 1) | (z == 2)
    is_end = (z == 0) | (z == 3)
    edge_peer = flipped(z, 1)
    across_peer = 3 - z

    barrier = pltpu.get_barrier_semaphore()
    greet = [(sibling, z)]
    greet += [(2 * lax.rem(chip + k, half) + parity, z) for k in range(1, half)]
    greet += [(me, flipped(z, k)) for k in range(1, tp)]
    for device in greet:
        pl.semaphore_signal(barrier, inc=1, device_id=device, device_id_type=MESH)

    loads_w = [
        pltpu.make_async_copy(w_hbm, w_v, w_sem.at[0]),
        pltpu.make_async_copy(ws_hbm, ws_v, w_sem.at[1]),
    ]
    for copy in loads_w:
        copy.start()

    def block_of(n):
        s, r = n // cycle, lax.rem(n, cycle)
        back = r // per
        pos = lax.rem(r, per)
        return per * s + (1 - back) * pos + back * (per - 1 - pos)

    def slot_of(n):
        return blocks * (lax.rem(n, cycle) // per) + block_of(n)

    def loads(n):
        slot = lax.rem(n, 2)
        at = pl.multiple_of(block_of(n) * SPAN, SPAN)
        return [
            pltpu.make_async_copy(x_hbm.at[pl.ds(at, SPAN)], xbuf.at[slot], load_sem.at[0, slot]),
            pltpu.make_async_copy(c_hbm.at[pl.ds(at, SPAN)], cbuf.at[slot], load_sem.at[1, slot]),
        ]

    def next_block(n):
        for copy in loads(n):
            copy.wait()

        @pl.when(n + 1 < pieces)
        def _():
            for copy in loads(n + 1):
                copy.start()

    def edge_copy(n, h, source):
        slot = slot_of(n)
        return pltpu.make_async_remote_copy(
            src_ref=source,
            dst_ref=edge.at[slot, h],
            send_sem=edge_send.at[slot, h],
            recv_sem=edge_recv.at[slot, h],
            device_id=(me, edge_peer),
            device_id_type=MESH,
        )

    def inward(n, h):
        return edge_copy(n, h, mine.at[slot_of(n), h])

    def outward(n, h):
        return edge_copy(n, h, total_v.at[lax.rem(n, 2), h])

    def kept(n, h):
        slot = slot_of(n)
        return pltpu.make_async_copy(total_v.at[lax.rem(n, 2), h], edge.at[slot, h], keep_sem.at[slot, h])

    def across_copy(n, h):
        slot = slot_of(n)
        return pltpu.make_async_remote_copy(
            src_ref=pair.at[lax.rem(n, 2), h],
            dst_ref=across.at[slot, h],
            send_sem=across_send.at[slot, h],
            recv_sem=across_recv.at[slot, h],
            device_id=(me, across_peer),
            device_id_type=MESH,
        )

    def landing(source, n, h):
        return pltpu.make_async_copy(source.at[slot_of(n), h], landed.at[h], pump_sem.at[h])

    def mine_load(n):
        return pltpu.make_async_copy(mine.at[slot_of(n)], mine_v, pump_sem.at[2])

    def store_piece(n):
        return pltpu.make_async_copy(stage, mine.at[slot_of(n)], mine_sem.at[0])

    def in_groups(apart, arrived, load, place, send):
        for group in ((0,), (1,)) if apart else ((0, 1),):
            for h in group:
                arrived(h)
            for h in group:
                load(h).start()
            for h in group:
                load(h).wait()
            for h in group:
                place(h)
                send(h)

    def combine(n, apart=False):
        mine_load(n).start()

        @pl.when(n >= 2)
        def _():
            for h in (0, 1):
                across_copy(n - 2, h).wait_send()

        mine_load(n).wait()
        slot = lax.rem(n, 2)

        def place(h):
            pair[slot, h] = add_low(mine_v[h], landed[h])

        in_groups(
            apart,
            lambda h: inward(n, h).wait_recv(),
            lambda h: landing(edge, n, h),
            place,
            lambda h: across_copy(n, h).start(),
        )

    def finish(n, apart=False):
        @pl.when(n >= 2)
        def _():
            for h in (0, 1):
                outward(n - 2, h).wait_send()
                kept(n - 2, h).wait()

        slot = lax.rem(n, 2)

        def place(h):
            total_v[slot, h] = add_low(pair[slot, h], landed[h])

        def send(h):
            outward(n, h).start()
            kept(n, h).start()

        in_groups(
            apart,
            lambda h: across_copy(n, h).wait_recv(),
            lambda h: landing(across, n, h),
            place,
            send,
        )

    def combined(n):
        return jnp.maximum(2 * n - 3, 0) // 3

    def sent(n):
        paced = combined(n) + 2 + lax.rem(n, cycle) // per
        return jnp.where(n == pieces - 1, pieces, jnp.where(n < 0, 0, jnp.minimum(n + 1, paced)))

    def pump(n):
        @pl.when(is_end)
        def _():
            @pl.loop(sent(n - 1), sent(n))
            def _(k):
                for h in (0, 1):
                    inward(k, h).start()

        @pl.when(is_middle & (combined(n - 2) > combined(n - 3)))
        def _():
            finish(combined(n - 2) - 1)

        @pl.when(is_middle & (combined(n) > combined(n - 1)))
        def _():
            combine(combined(n) - 1)

    def advance(n, apart=False):
        @pl.when(is_middle)
        def _():
            combine(n, apart)
            finish(n - 1, apart)

    def puts(b, which):
        pairs = (
            (grads, grads_hbm),
            (lowered_v, lowered_hbm),
            (turned, branch_hbm),
            (turned, normed_hbm),
        )
        return [
            pltpu.make_async_copy(pairs[k][0], pairs[k][1].at[b], put_sem.at[k]) for k in which
        ]

    def stat_copy(s, k):
        return pltpu.make_async_remote_copy(
            src_ref=stat_own.at[s],
            dst_ref=stat_in.at[s, k - 1],
            send_sem=stat_send.at[s, k - 1],
            recv_sem=stat_recv.at[s, k - 1],
            device_id=(me, flipped(z, k)),
            device_id_type=MESH,
        )

    for copy in loads(0):
        copy.start()
    small[...] = jnp.zeros_like(small)
    pl.semaphore_wait(barrier, len(greet))
    for copy in loads_w:
        copy.wait()

    @pl.loop(0, sequences)
    def _(s):
        first_n = s * cycle
        ext[0:8, :] = jnp.zeros((8, conv), F32)
        state_v[...] = jnp.zeros_like(state_v)

        @pl.loop(0, per)
        def _(f):
            n = first_n + f
            next_block(n)
            slot = lax.rem(n, 2)
            forward_step(
                f,
                xbuf.at[slot],
                cbuf.at[slot],
                w_v,
                ws_v,
                pv,
                saved,
                state_v,
                ext,
                stage,
                stat_own.at[s, f],
                sizes,
            )

            store_piece(n).start()

            @pl.when(f == per - 1)
            def _():
                for k in range(1, tp):
                    stat_copy(s, k).start()

            store_piece(n).wait()
            pump(n)

        for k in range(1, tp):
            stat_copy(s, k).wait()
        ext[SPAN:, :] = jnp.zeros((8, conv), F32)
        dst_v[...] = jnp.zeros_like(dst_v)
        totals[s] = (stat_own[s] + stat_in[s, 0]) + (stat_in[s, 1] + stat_in[s, 2])

        @pl.loop(0, per)
        def _(j):
            n = first_n + per + j
            f = per - 1 - j
            b = per * s + f
            next_block(n)

            @pl.when(b != per - 1)
            def _():
                for copy in puts(b, (0, 1, 3)):
                    copy.wait()

            slot = lax.rem(n, 2)
            backward_step(
                f,
                xbuf.at[slot],
                cbuf.at[slot],
                w_v,
                ws_v,
                pv,
                totals[s, f],
                saved,
                dst_v,
                ext,
                small,
                grads,
                lowered_v,
                turned,
                puts(b, range(4)),
                stage,
                sizes,
                norm_width,
            )
            store_piece(n).start()
            store_piece(n).wait()
            pump(n)

    def to_sibling(q):
        at = pl.multiple_of((2 * q + 1 - parity) * rows, 16)
        return pltpu.make_async_remote_copy(
            src_ref=wgrad.at[pl.ds(at, rows)],
            dst_ref=rs1.at[q],
            send_sem=rs1_send.at[q],
            recv_sem=rs1_recv.at[q],
            device_id=(sibling, z),
            device_id_type=MESH,
        )

    def to_owner(k):
        q = lax.rem(chip + k, half)
        at = pl.multiple_of((2 * q + parity) * rows, 16)
        return pltpu.make_async_remote_copy(
            src_ref=wgrad.at[pl.ds(at, rows)],
            dst_ref=rs2.at[chip],
            send_sem=rs2_send.at[k],
            recv_sem=rs2_recv.at[k],
            device_id=(2 * q + parity, z),
            device_id_type=MESH,
        )

    def small_copy(source, target, index, device):
        return pltpu.make_async_remote_copy(
            src_ref=source,
            dst_ref=target,
            send_sem=sm_send.at[index],
            recv_sem=sm_recv.at[index],
            device_id=device,
            device_id_type=MESH,
        )

    def fetch(source):
        copy = pltpu.make_async_copy(source, rsv, rs_sem.at[0])
        copy.start()
        copy.wait()
        return rsv[...].astype(F32)

    def left_operand(source):
        return [
            pltpu.make_async_copy(source.at[b], w_v.at[:, pl.ds(b * SPAN, SPAN)], tile_sem.at[2 + b])
            for b in range(blocks)
        ]

    def tile_load(source, at, size, slot):
        return pltpu.make_async_copy(
            source.at[:, :, pl.ds(at, size)], tiles.at[slot, :, :, pl.ds(0, size)], tile_sem.at[slot]
        )

    def products(source, width, place):
        whole = width // 256

        @pl.loop(0, whole)
        def _(t):
            slot = lax.rem(t, 2)
            at = pl.multiple_of(t * 256, 256)
            tile_load(source, at, 256, slot).wait()

            @pl.when(t + 1 < whole)
            def _():
                tile_load(source, pl.multiple_of(at + 256, 256), 256, 1 - slot).start()

            right = tiles[slot].reshape(tokens, 256)
            wgrad[:, pl.ds(pl.multiple_of(place + at, 128), 256)] = mm(
                w_v[:, 0:tokens], right
            ).astype(BF16)

    for copy in puts(per * (sequences - 1), (0, 1, 3)):
        copy.wait()
    for copy in left_operand(normed_hbm):
        copy.start()
    tile_load(grads_hbm, 0, 256, 0).start()
    for copy in left_operand(normed_hbm):
        copy.wait()
    products(grads_hbm, wide, 0)
    rest = wide % 256
    last = tile_load(grads_hbm, wide - rest, rest, 0)
    last.start()
    last.wait()
    wgrad[:, wide - rest : wide] = mm(
        w_v[:, 0:tokens], tiles[0].reshape(tokens, 256)[:, 0:rest]
    ).astype(BF16)
    for copy in left_operand(branch_hbm):
        copy.start()
    tile_load(lowered_hbm, 0, 256, 0).start()

    head = (2 * (pieces - 1) - 3) // 3

    @pl.when(is_middle)
    def _():
        for n in range((2 * (pieces - 3) - 3) // 3, head - 1):
            finish(n)

    advance(head)
    for copy in left_operand(branch_hbm):
        copy.wait()
    products(lowered_hbm, inner, wide)

    @pl.loop(0, half)
    def _(q):
        to_sibling(q).start()

    first_small = small_copy(small, small1, 0, (sibling, z))
    first_small.start()
    spread_over = pieces - 1 - head
    early = head + 1 + max(spread_over // 3, 0)
    for n in range(head + 1, early):
        advance(n)
    first_small.wait()
    small2[chip] = small[...] + small1[...]
    second_small = [
        small_copy(
            small2.at[chip], small2.at[chip], k, (2 * lax.rem(chip + k, half) + parity, z)
        )
        for k in range(1, half)
    ]
    for copy in second_small:
        copy.start()

    @pl.loop(1, half)
    def _(k):
        q = lax.rem(chip + k, half)
        to_sibling(q).wait_recv()
        at = pl.multiple_of((2 * q + parity) * rows, 16)
        wgrad[pl.ds(at, rows), :] = (
            wgrad[pl.ds(at, rows), :].astype(F32) + fetch(rs1.at[q])
        ).astype(BF16)
        to_owner(k).start()

    late = max(early, pieces - 2)
    for n in range(early, late):
        advance(n)
    to_sibling(chip).wait_recv()
    own[...] = wgrad[pl.ds(pl.multiple_of(me * rows, 16), rows), :].astype(F32) + fetch(
        rs1.at[chip]
    )
    for copy in second_small:
        copy.wait()
    total = small2[0]
    for q in range(1, half):
        total = total + small2[q]
    small3[z] = total
    third_small = [
        small_copy(small3.at[z], small3.at[z], half + k, (me, flipped(z, k)))
        for k in range(1, tp)
    ]
    for copy in third_small:
        copy.start()
    for n in range(late, pieces - 1):
        advance(n, True)

    @pl.loop(1, half)
    def _(k):
        to_owner(k).wait_recv()
        own[...] += fetch(rs2.at[lax.rem(chip + half - k, half)])

    advance(pieces - 1, True)
    for copy in third_small:
        copy.wait()
    vectors[...] = jnp.zeros_like(vectors)
    both = conv - inner
    shared = small3[0, 2:7, inner:conv]
    before = small3[0, 0:1, :]
    for k in range(1, tp):
        shared = shared + small3[k, 2:7, inner:conv]
        before = before + small3[k, 0:1, :]
    for k in range(tp):
        vectors[0:5, k * inner : (k + 1) * inner] = small3[k, 2:7, 0:inner]
        vectors[5:6, depth + k * inner : depth + (k + 1) * inner] = small3[k, 1:2, 0:inner]
        head_sums[k, 0:1, :] = small3[k, 7:8, 0:LANES]
        head_sums[k, 1:2, :] = small3[k, 7:8, LANES : 2 * LANES]
        marks_t = head_marks_t(head_width, inner)
        skips = gather_heads(
            jnp.broadcast_to(small3[k, 1:2, inner : 2 * inner], (8, inner)),
            jnp.concatenate([marks_t, marks_t], 0),
        )
        head_sums[k, 2:8, :] = skips[2:8, :]
    vectors[0:5, tp * inner : tp * inner + both] = shared
    vectors[5:6, 0:depth] = before

    @pl.when(is_middle)
    def _():
        finish(pieces - 1, True)

    @pl.loop(0, half)
    def _(q):
        to_sibling(q).wait_send()

    @pl.loop(1, half)
    def _(k):
        to_owner(k).wait_send()

    @pl.when(is_middle)
    def _():
        for n in (pieces - 2, pieces - 1):
            for h in (0, 1):
                across_copy(n, h).wait_send()
                outward(n, h).wait_send()
                kept(n, h).wait()

    @pl.when(is_end)
    def _():
        @pl.loop(0, pieces)
        def _(n):
            for h in (0, 1):
                inward(n, h).wait_send()
                outward(n, h).wait_recv()


def finalize(x_ref, c_ref, out_ref, in_ref, totals_ref, block_ref, grad_ref, *, norm_width):
    sums = jnp.transpose(jnp.concatenate([totals_ref[0, 0]] * (LANES // 8), 0))
    scale = lax.rsqrt(sums[:, 0:1] / norm_width + NORM_EPSILON)
    shape = x_ref.shape
    branch = out_ref[0].reshape(shape).astype(F32)
    block_ref[...] = (x_ref[...].astype(F32) + scale * branch).astype(BF16)
    grad_ref[...] = in_ref[0].reshape(shape).astype(F32) + c_ref[...].astype(F32)


def run_finalize(x, c, sums, totals, norm_width):
    tokens, depth = x.shape
    blocks = tokens // SPAN
    per = LENGTH // SPAN
    rows = pl.BlockSpec((SPAN, depth), lambda b: (b, 0))
    return pl.pallas_call(
        functools.partial(finalize, norm_width=norm_width),
        grid=(blocks,),
        in_specs=[
            rows,
            rows,
            pl.BlockSpec((1, 2, HALF, depth), lambda b: (b, 0, 0, 0)),
            pl.BlockSpec((1, 2, HALF, depth), lambda b: (blocks + b, 0, 0, 0)),
            pl.BlockSpec((1, 1, 8, SPAN), lambda b: (b // per, b % per, 0, 0)),
        ],
        out_specs=(rows, rows),
        out_shape=(sds((tokens, depth), BF16), sds((tokens, depth), F32)),
        compiler_params=pltpu.CompilerParams(vmem_limit_bytes=32 * 1024 * 1024),
        cost_estimate=pl.CostEstimate(
            flops=6 * tokens * depth, bytes_accessed=14 * tokens * depth, transcendentals=0
        ),
        name="finalize",
    )(x, c, sums, sums, totals)


def run_mixer(x, c, w, ws, pv, dp, tp, sizes, norm_width):
    inner, head_width, heads = sizes
    tokens, depth = x.shape
    conv_states = ws.shape[1]
    conv = inner + conv_states
    states = conv_states // 2
    wide = inner + conv + LANES
    width = w.shape[1]
    blocks = tokens // SPAN
    per = LENGTH // SPAN
    sequences = blocks // per
    pieces = 2 * blocks
    half = dp // 2
    rows = depth // dp
    hbm = pl.BlockSpec(memory_space=pl.ANY)
    vmem = pl.BlockSpec(memory_space=pltpu.VMEM)
    dma = pltpu.SemaphoreType.DMA
    piece = (2, HALF, depth)
    rows_of_x = (SPAN, depth)
    flops = tokens * (6 * depth * (2 * inner + conv) + 6 * depth * inner + 80 * heads * SPAN * 64)
    return pl.pallas_call(
        functools.partial(mixer, dp=dp, tp=tp, sizes=sizes, norm_width=norm_width),
        in_specs=[hbm] * 4 + [vmem],
        out_specs=(hbm,) * 9 + (vmem,) * 4,
        out_shape=(
            sds((pieces,) + piece, BF16),
            sds((pieces,) + piece, BF16),
            sds((pieces,) + piece, BF16),
            sds((half, rows, wide + inner), BF16),
            sds((half, rows, wide + inner), BF16),
            sds((blocks, SPAN, wide), BF16),
            sds((blocks, SPAN, inner), BF16),
            sds((blocks, depth, SPAN), BF16),
            sds((blocks, depth, SPAN), BF16),
            sds((rows, wide + inner), F32),
            sds((8, tp * inner + depth), F32),
            sds((tp, 8, LANES), F32),
            sds((sequences, per, 8, SPAN), F32),
        ),
        scratch_shapes=[
            pltpu.VMEM((depth, width), BF16),
            pltpu.VMEM((depth, conv_states), BF16),
            pltpu.VMEM((2,) + rows_of_x, BF16),
            pltpu.VMEM((2,) + rows_of_x, BF16),
            pltpu.VMEM((per, SPAN, conv), BF16),
            pltpu.VMEM((per, SPAN, conv), BF16),
            pltpu.VMEM((per, SPAN, inner), BF16),
            pltpu.VMEM((per, SPAN, inner), F32),
            pltpu.VMEM((per, SPAN, LANES), F32),
            pltpu.VMEM((per, states, inner), BF16),
            pltpu.VMEM((states, inner), F32),
            pltpu.VMEM((states, inner), F32),
            pltpu.VMEM((SPAN + 8, conv), F32),
            pltpu.VMEM((depth, wide + inner), BF16),
            pltpu.VMEM((2, blocks, SPAN, 256), BF16),
            pltpu.VMEM((8, depth), F32),
            pltpu.VMEM((SPAN, wide), BF16),
            pltpu.VMEM((SPAN, inner), BF16),
            pltpu.VMEM((depth, SPAN), BF16),
            pltpu.VMEM(piece, BF16),
            pltpu.VMEM(piece, BF16),
            pltpu.VMEM(piece, BF16),
            pltpu.VMEM((2,) + piece, BF16),
            pltpu.VMEM((2,) + piece, BF16),
            pltpu.VMEM((rows, wide + inner), BF16),
            pltpu.VMEM((sequences, per, 8, SPAN), F32),
            pltpu.VMEM((sequences, tp - 1, per, 8, SPAN), F32),
            pltpu.VMEM((8, depth), F32),
            pltpu.VMEM((half, 8, depth), F32),
            pltpu.VMEM((tp, 8, depth), F32),
            dma((2,)),
            dma((2, 2)),
            dma((pieces, 2)),
            dma((pieces, 2)),
            dma((pieces, 2)),
            dma((pieces, 2)),
            dma((pieces, 2)),
            dma((1,)),
            dma((3,)),
            dma((sequences, tp - 1)),
            dma((sequences, tp - 1)),
            dma((half,)),
            dma((half,)),
            dma((half,)),
            dma((half,)),
            dma((1,)),
            dma((4,)),
            dma((2 + blocks,)),
            dma((half + tp,)),
            dma((half + tp,)),
        ],
        compiler_params=pltpu.CompilerParams(
            collective_id=2, has_side_effects=True, vmem_limit_bytes=MIXER_VMEM
        ),
        cost_estimate=pl.CostEstimate(flops=flops, bytes_accessed=60_000_000, transcendentals=0),
        name="mixer",
    )(x, c, w, ws, pv)


def adamw_update(weight, gradient, moment, square, step_rate, decay_rate):
    moment = FIRST_DECAY * moment + (1.0 - FIRST_DECAY) * gradient
    square = SECOND_DECAY * square + (1.0 - SECOND_DECAY) * gradient * gradient
    first_fix = 1.0 - FIRST_DECAY**STEP
    second_fix = 1.0 - SECOND_DECAY**STEP
    update = moment / first_fix / (jnp.sqrt(square / second_fix) + ADAM_EPSILON)
    return (weight - step_rate * (update + decay_rate * weight), moment, square)


def swap(values, mask, tp):
    return lax.ppermute(values, "tensor", [(i, i ^ mask) for i in range(tp)])


def pad_to(values, size):
    return jnp.pad(values, [(0, 0)] * (values.ndim - 1) + [(0, size - values.shape[-1])])


def shards(
    dp,
    tp,
    activations,
    cotangent,
    in_weight,
    in_first,
    in_second,
    step_weight,
    step_first,
    step_second,
    out_weight,
    out_first,
    out_second,
    state_weight,
    state_first,
    state_second,
    conv_weight,
    conv_first,
    conv_second,
    conv_bias,
    bias_first,
    bias_second,
    gain_vector,
    gains_first,
    gains_second,
    head_params,
    head_first,
    head_second,
):
    dp_rank = lax.axis_index("dp")
    rank = lax.axis_index("tensor")
    tokens, depth = activations.shape
    shard_rows, _, inner = in_weight.shape
    norm_width = inner * tp
    heads = step_weight.shape[1]
    head_width = inner // heads
    state_rows, conv_states = state_weight.shape
    conv = inner + conv_states
    taps, conv_own = conv_weight.shape
    gains_own = gain_vector.shape[0]
    sizes = (inner, head_width, heads)

    w_own = jnp.concatenate(
        [
            in_weight.reshape(shard_rows, 2 * inner).astype(BF16),
            pad_to(step_weight.astype(BF16), LANES),
            out_weight.astype(BF16).T,
        ],
        1,
    )
    padded_rows = -(-state_rows // 16) * 16
    st_own = jnp.pad(state_weight.astype(BF16), ((0, padded_rows - state_rows), (0, 0)))
    flat = jnp.concatenate([conv_weight.reshape(-1), conv_bias, gain_vector])
    sm_own = pad_to(flat, -(-flat.shape[0] // 1024) * 1024).reshape(-1, LANES)
    w, st_full, sm_full = run_gather(w_own, st_own, sm_own, dp, tp)
    ws = st_full[:, :, :state_rows].reshape(depth, conv_states)
    small = sm_full.reshape(dp * tp, -1)
    kernel_full = (
        small[:, : taps * conv_own].reshape(-1, taps, conv_own).transpose(1, 0, 2).reshape(taps, -1)
    )
    offsets_full = small[:, taps * conv_own : (taps + 1) * conv_own].reshape(-1)
    gains_full = small[:, (taps + 1) * conv_own : (taps + 1) * conv_own + gains_own].reshape(-1)
    start = rank * inner
    conv_rows = jnp.concatenate([kernel_full, offsets_full[None, :]], 0)
    conv_local = jnp.concatenate(
        [lax.dynamic_slice_in_dim(conv_rows, start, inner, 1), conv_rows[:, norm_width:]], 1
    )
    head_local = lax.dynamic_slice_in_dim(head_params, rank * heads, heads, 1)
    gain_local = lax.dynamic_slice_in_dim(gains_full, depth + start, inner, 0)
    pv = jnp.concatenate(
        [
            gains_full[None, :depth],
            pad_to(jnp.concatenate([gain_local, jnp.repeat(head_local[2], head_width)]), depth)[
                None, :
            ],
            pad_to(conv_local, depth),
            pad_to(
                jnp.concatenate(
                    [pad_to(-jnp.exp(head_local[0]), LANES), pad_to(head_local[1], LANES)]
                ),
                depth,
            )[None, :],
        ],
        0,
    )

    sums, _, _, _, _, _, _, _, _, own, vectors, head_sums, totals = run_mixer(
        activations, cotangent, w, ws, pv, dp, tp, sizes, norm_width
    )
    block_output, input_grad = run_finalize(activations, cotangent, sums, totals, norm_width)

    in_owned = own[:, : 2 * inner].reshape(shard_rows, 2, inner)
    state_part = own[:, 2 * inner : inner + conv]
    step_owned = own[:, inner + conv : inner + conv + heads].T
    out_owned = own[:, inner + conv + LANES :].T
    state_owned = lax.dynamic_slice_in_dim(state_part, rank * state_rows, state_rows, 0)
    for k in range(1, tp):
        theirs = lax.dynamic_slice_in_dim(state_part, (rank ^ k) * state_rows, state_rows, 0)
        state_owned = state_owned + swap(theirs, k, tp)

    head_grad = head_sums[:, :3, :heads].transpose(1, 0, 2).reshape(3, tp * heads)
    device = dp_rank * tp + rank
    conv_owned = lax.dynamic_slice(vectors, (0, device * conv_own), (taps + 1, conv_own))
    gains_owned = lax.dynamic_slice(vectors, (taps + 1, device * gains_own), (1, gains_own))[0]

    in_new = adamw_update(in_weight, in_owned, in_first, in_second, RATE_MATRIX, WEIGHT_DECAY)
    step_new = adamw_update(
        step_weight.T, step_owned, step_first.T, step_second.T, RATE_MATRIX, WEIGHT_DECAY
    )
    step_new = tuple(value.T for value in step_new)
    out_new = adamw_update(out_weight, out_owned, out_first, out_second, RATE_OUTPUT, WEIGHT_DECAY)
    state_new = adamw_update(
        state_weight, state_owned, state_first, state_second, RATE_MATRIX, WEIGHT_DECAY
    )
    conv_new = adamw_update(conv_weight, conv_owned[:taps], conv_first, conv_second, RATE_CONV, 0.0)
    bias_new = adamw_update(conv_bias, conv_owned[taps], bias_first, bias_second, RATE_VECTOR, 0.0)
    gains_new = adamw_update(gain_vector, gains_owned, gains_first, gains_second, RATE_VECTOR, 0.0)
    head_new = adamw_update(head_params, head_grad, head_first, head_second, RATE_HEADS, 0.0)
    return (
        (block_output, input_grad)
        + in_new
        + step_new
        + out_new
        + state_new
        + conv_new
        + bias_new
        + gains_new
        + head_new
    )


def solution(mesh):
    both = ("dp", "tensor")
    rows = P("dp", None)
    projection = P("dp", None, "tensor")
    step = P("dp", "tensor")
    out = P("tensor", "dp")
    state = P(both, None)
    taps = P(None, both)
    vector = P(both)
    parameters = sum(
        ((spec,) * 3 for spec in (projection, step, out, state, taps, vector, vector, P())), ()
    )
    return jax.shard_map(
        functools.partial(shards, mesh.shape["dp"], mesh.shape["tensor"]),
        mesh=mesh,
        in_specs=(rows, rows) + parameters,
        out_specs=(rows, rows) + parameters,
        check_vma=False,
    )
```

```python
import functools

import jax
import jax.numpy as jnp
from jax import lax
from jax.experimental import pallas as pl
from jax.experimental.pallas import tpu as pltpu
from jax.sharding import PartitionSpec as P

F32 = jnp.float32
BF16 = jnp.bfloat16
MESH = pl.DeviceIdType.MESH

SPAN = 256
LENGTH = 1024
STEP = 5
LANES = 128
LOG2E = 1.4426950408889634
NORM_EPSILON = 1e-05
FIRST_DECAY = 0.9
SECOND_DECAY = 0.95
ADAM_EPSILON = 1e-08
WEIGHT_DECAY = 0.1
RATE_MATRIX = 0.05
RATE_OUTPUT = 0.04
RATE_CONV = 1.0
RATE_VECTOR = 0.5
RATE_HEADS = 2.0
MIXER_VMEM = 63 * 1024 * 1024


def mm(a, b):
    return lax.dot_general(a, b, (((1,), (0,)), ((), ())), preferred_element_type=F32)


def mm_nt(a, b):
    return lax.dot_general(a, b, (((1,), (1,)), ((), ())), preferred_element_type=F32)


def mm_exact(a, b):
    return lax.dot_general(
        a, b, (((1,), (0,)), ((), ())), preferred_element_type=F32, precision=lax.Precision.HIGHEST
    )


def sigmoid(v):
    return 1.0 / (1.0 + jnp.exp(-v))


def softplus(v):
    return jnp.maximum(v, 0.0) + jnp.log1p(jnp.exp(-jnp.abs(v)))


def split_low(v):
    high = v.astype(BF16)
    return high, (v - high.astype(F32)).astype(BF16)


def head_marks(head_width, channels):
    head = lax.broadcasted_iota(jnp.int32, (LANES, channels), 0)
    channel = lax.broadcasted_iota(jnp.int32, (LANES, channels), 1)
    inside = (channel >= head * head_width) & (channel < (head + 1) * head_width)
    return inside.astype(F32).astype(BF16)


def head_marks_t(head_width, channels):
    head = lax.broadcasted_iota(jnp.int32, (channels, LANES), 1)
    channel = lax.broadcasted_iota(jnp.int32, (channels, LANES), 0)
    inside = (channel >= head * head_width) & (channel < (head + 1) * head_width)
    return inside.astype(F32).astype(BF16)


def spread(v, marks2):
    high, low = split_low(v)
    return mm(jnp.concatenate([high, low], 1), marks2)


def gather_heads(v, marks_t2):
    high, low = split_low(v)
    return mm(jnp.concatenate([high, low], 1), marks_t2)


def causal_ones(lower):
    row = lax.broadcasted_iota(jnp.int32, (SPAN, SPAN), 0)
    col = lax.broadcasted_iota(jnp.int32, (SPAN, SPAN), 1)
    keep = row >= col if lower else row <= col
    return keep.astype(F32)


def lane_masks():
    lane = lax.broadcasted_iota(jnp.int32, (1, LANES), 1)
    first = (lane < LANES // 2).astype(F32)
    return first, 1.0 - first


def sds(shape, dtype):
    return jax.ShapeDtypeStruct(shape, dtype)


def axis_bits(size):
    count = size.bit_length() - 1
    order = list(range(1, count)) + [0]
    other = [order[1], order[0]] + order[2:] if count >= 3 else order
    return order, other


def flipped(index, mask):
    result = index
    bit = 1
    while bit <= mask:
        if mask & bit:
            result = result + bit * (1 - 2 * ((index // bit) % 2))
        bit *= 2
    return result


def gather_weights(
    w_own, st_own, sm_own, w_full, st_full, sm_full, local_sem, z_send, z_recv, send_sem, recv_sem,
    *, dp, tp, cut
):
    me = lax.axis_index("dp")
    tensor = lax.axis_index("tensor")
    rows, width = w_own.shape
    count = dp.bit_length() - 1

    barrier = pltpu.get_barrier_semaphore()
    for b in range(count):
        pl.semaphore_signal(
            barrier, inc=1, device_id=(flipped(me, 1 << b), tensor), device_id_type=MESH
        )
    for k in range(1, tp):
        pl.semaphore_signal(barrier, inc=1, device_id=(me, flipped(tensor, k)), device_id_type=MESH)
    pl.semaphore_wait(barrier, count + tp - 1)

    order, other = axis_bits(dp)
    row_of = lambda mask: pl.multiple_of(flipped(me, mask) * rows, 16)
    left, right = pl.ds(0, cut), pl.ds(cut, width - cut)

    def weight_part(columns):
        def source(mask):
            if mask == 0:
                return w_own.at[:, columns]
            return w_full.at[pl.ds(row_of(mask), rows), columns]

        return source, lambda mask: w_full.at[pl.ds(row_of(mask), rows), columns]

    state_part = (lambda mask: st_full.at[flipped(me, mask)],) * 2
    small_part = (lambda mask: sm_full.at[flipped(me, mask)],) * 2
    kinds = (
        (order, weight_part(left)),
        (other, weight_part(right)),
        (order, state_part),
        (other, small_part),
    )

    def full_mask(bits, packed):
        return sum(1 << bits[j] for j in range(count) if packed >> j & 1)

    def move(kind, packed, j):
        bits, (source, target) = kinds[kind]
        mask = full_mask(bits, packed)
        slot = packed | (1 << j)
        return pltpu.make_async_remote_copy(
            src_ref=source(mask),
            dst_ref=target(mask),
            send_sem=send_sem.at[kind, slot],
            recv_sem=recv_sem.at[kind, slot],
            device_id=(flipped(me, 1 << bits[j]), tensor),
            device_id_type=MESH,
        )

    started = []

    def start(kind, packed, j):
        copy = move(kind, packed, j)
        copy.start()
        started.append(copy)

    zs = []
    for k in range(1, tp):
        for which, (own, full) in enumerate(((st_own, st_full), (sm_own, sm_full))):
            copy = pltpu.make_async_remote_copy(
                src_ref=own,
                dst_ref=full.at[me, tensor],
                send_sem=z_send.at[which, k],
                recv_sem=z_recv.at[which, k],
                device_id=(me, flipped(tensor, k)),
                device_id_type=MESH,
            )
            copy.start()
            zs.append(copy)
    for j in range(count):
        for kind in (0, 1):
            start(kind, 0, j)
    locals_ = [
        pltpu.make_async_copy(w_own, w_full.at[pl.ds(row_of(0), rows)], local_sem.at[0]),
        pltpu.make_async_copy(st_own, st_full.at[me, tensor], local_sem.at[1]),
        pltpu.make_async_copy(sm_own, sm_full.at[me, tensor], local_sem.at[2]),
    ]
    for copy in locals_:
        copy.start()
    for copy in locals_:
        copy.wait()
    for copy in zs:
        copy.wait()
    for j in range(count):
        for kind in (3, 2):
            start(kind, 0, j)
    for packed in range(1, dp):
        top = packed.bit_length() - 1
        for kind in (0, 1, 3, 2):
            move(kind, packed & ~(1 << top), top).wait_recv()
            for j in range(top + 1, count):
                start(kind, packed, j)
    for copy in started:
        copy.wait_send()


def run_gather(w_own, st_own, sm_own, dp, tp):
    rows, width = w_own.shape
    cut = width // 2 // LANES * LANES
    hbm = pl.BlockSpec(memory_space=pl.ANY)
    return pl.pallas_call(
        functools.partial(gather_weights, dp=dp, tp=tp, cut=cut),
        in_specs=[hbm] * 3,
        out_specs=(hbm,) * 3,
        out_shape=(
            sds((dp * rows, width), BF16),
            sds((dp, tp) + st_own.shape, BF16),
            sds((dp, tp) + sm_own.shape, F32),
        ),
        scratch_shapes=[
            pltpu.SemaphoreType.DMA((3,)),
            pltpu.SemaphoreType.DMA((2, tp)),
            pltpu.SemaphoreType.DMA((2, tp)),
            pltpu.SemaphoreType.DMA((4, dp)),
            pltpu.SemaphoreType.DMA((4, dp)),
        ],
        compiler_params=pltpu.CompilerParams(collective_id=1, has_side_effects=True),
        name="gather_weights",
    )(w_own, st_own, sm_own)


def add_low(a, b):
    return (a.astype(F32) + b.astype(F32)).astype(BF16)


HALF = SPAN // 2


def forward_step(f, x, c, w_v, ws_v, pv, saved, state_v, ext, stage, stats, sizes):
    inner, head_width, heads = sizes
    cin_s, pre_s, gate_s, y_s, sp_s, state_s = saved
    states = ws_v.shape[1] // 2
    conv = inner + 2 * states

    x = x[...].astype(F32)
    inv = lax.rsqrt(jnp.mean(x * x, axis=1, keepdims=True) + NORM_EPSILON)
    normed = (x * inv * pv[0:1, :]).astype(BF16)

    step_in = mm(normed, w_v[:, 2 * inner : 2 * inner + LANES])
    sp_s[f] = step_in
    ext[8:, 0:inner] = mm(normed, w_v[:, inner : 2 * inner])
    ext[8:, inner:conv] = mm(normed, ws_v[...])
    gate = mm(normed, w_v[:, 0:inner]).astype(BF16)
    gate_s[f] = gate
    gate = gate.astype(F32)
    cin_s[f] = ext[8:, :].astype(BF16)
    pre = pv[6:7, 0:conv]
    for tap in range(4):
        pre = pre + pv[2 + tap : 3 + tap, 0:conv] * ext[5 + tap : 5 + tap + SPAN, :]
    ext[0:8, :] = ext[SPAN : SPAN + 8, :]
    pre = pre.astype(BF16)
    pre_s[f] = pre
    pre = pre.astype(F32)
    act = pre * sigmoid(pre)

    rate = pv[7:8, 0:LANES]
    dt = softplus(step_in + pv[7:8, LANES : 2 * LANES])
    total = mm_exact(causal_ones(True), dt * rate)
    total2 = total * LOG2E
    total2_t = jnp.transpose(total2)
    marks = head_marks(head_width, inner)
    marks2 = jnp.concatenate([marks, marks], 0)
    end = total[SPAN - 1 : SPAN, :]
    xc = act[:, 0:inner]
    bmat = act[:, inner : inner + states].astype(BF16)
    cmat = act[:, inner + states :].astype(BF16)
    xd = (xc * spread(dt, marks2)).astype(BF16)
    weighted = (xd.astype(F32) * spread(jnp.exp(end - total), marks2)).astype(BF16)

    state = state_v[...]
    state_low = state.astype(BF16)
    state_s[f] = state_low
    carried = spread(jnp.exp(total), marks2) * mm(cmat, state_low)
    keep = spread(jnp.broadcast_to(jnp.exp(end), (8, LANES)), marks2)[0:1, :]
    state_v[...] = keep * state + mm(jnp.transpose(bmat), weighted)

    inter = mm_nt(cmat, bmat) * causal_ones(True)
    first, second = lane_masks()
    skip = pv[1:2, inner : 2 * inner]
    parts = []
    for pair in range(heads // 2):
        lanes = slice(pair * LANES, (pair + 1) * LANES)
        xp = xd[:, lanes].astype(F32)
        within = None
        for side, mask in ((0, first), (1, second)):
            h = 2 * pair + side
            gap = jnp.minimum(total2[:, h : h + 1] - total2_t[h : h + 1, :], 0.0)
            mixing = (jnp.exp2(gap) * inter).astype(BF16)
            term = mm(mixing, (xp * mask).astype(BF16))
            within = term if within is None else within + term
        parts.append(within)
    y = jnp.concatenate(parts, 1) + carried
    y_s[f] = y
    y = y + skip * xc
    gated = y * gate * sigmoid(gate)
    squares = jnp.sum(gated * gated, axis=1, keepdims=True)
    lowered = (gated * pv[1:2, 0:inner]).astype(BF16)
    out = mm_nt(lowered, w_v[:, 2 * inner + LANES :])
    stage[...] = out.astype(BF16).reshape(stage.shape)
    dots = jnp.sum(c[...].astype(F32) * out, axis=1, keepdims=True)
    lane = lax.broadcasted_iota(jnp.int32, (SPAN, LANES), 1)
    both = jnp.where(lane == 0, squares, jnp.where(lane == 1, dots, 0.0))
    stats[...] = jnp.transpose(both)[0:8, :]


def backward_step(
    f, x, c, w_v, ws_v, pv, totals, saved, dst_v, dext, small, grads, lowered_v, turned, put, between, stage, sizes, norm_width
):
    inner, head_width, heads = sizes
    cin_s, pre_s, gate_s, y_s, sp_s, state_s = saved
    states = ws_v.shape[1] // 2
    conv = inner + 2 * states
    put_grads, put_lowered, put_branch, put_normed = put

    sums = jnp.transpose(jnp.concatenate([totals] * (LANES // 8), 0))
    scale = lax.rsqrt(sums[:, 0:1] / norm_width + NORM_EPSILON)
    bg = (scale * c[...].astype(F32)).astype(BF16)
    squares_grad = (-0.5 / norm_width) * sums[:, 1:2] * scale * scale * scale
    low_grad = mm(bg, w_v[:, 2 * inner + LANES :])

    pre = pre_s[f].astype(F32)
    sig_pre = sigmoid(pre)
    act = pre * sig_pre
    xc = act[:, 0:inner]
    bmat = act[:, inner : inner + states].astype(BF16)
    cmat = act[:, inner + states :].astype(BF16)

    skip = pv[1:2, inner : 2 * inner]
    gate = gate_s[f].astype(F32)
    sig = sigmoid(gate)
    y_scan = y_s[f]
    y = y_scan + skip * xc
    silu_gate = gate * sig
    gated = y * silu_gate
    gain = pv[1:2, 0:inner]
    lowered_v[...] = (gated * gain).astype(BF16)
    put_lowered.start()
    gated_grad = low_grad * gain + 2.0 * gated * squares_grad
    small[1:2, 0:inner] += jnp.sum(low_grad * gated, axis=0, keepdims=True)
    y_grad = gated_grad * silu_gate
    grads[:, 0:inner] = (gated_grad * y * sig * (1.0 + gate * (1.0 - sig))).astype(BF16)
    small[1:2, inner : 2 * inner] += jnp.sum(y_grad * xc, axis=0, keepdims=True)

    turned[...] = jnp.transpose(bg)
    put_branch.start()

    rate = pv[7:8, 0:LANES]
    step_pre = sp_s[f] + pv[7:8, LANES : 2 * LANES]
    dt = softplus(step_pre)
    total = mm_exact(causal_ones(True), dt * rate)
    total2 = total * LOG2E
    total2_t = jnp.transpose(total2)
    marks = head_marks(head_width, inner)
    marks2 = jnp.concatenate([marks, marks], 0)
    marks_t = head_marks_t(head_width, inner)
    marks_t2 = jnp.concatenate([marks_t, marks_t], 0)
    end = total[SPAN - 1 : SPAN, :]
    dt_wide = spread(dt, marks2)
    xd = (xc * dt_wide).astype(BF16)
    xd_wide = xd.astype(F32)
    end_wide = spread(jnp.exp(end - total), marks2)

    yb = y_grad.astype(BF16)
    yb_wide = yb.astype(F32)
    state_low = state_s[f]
    dst = dst_v[...]
    dst_low = dst.astype(BF16)
    carried_grad = (yb_wide * spread(jnp.exp(total), marks2)).astype(BF16)
    c_grad = mm_nt(carried_grad, state_low)
    b_state = mm(bmat, dst_low) * end_wide
    b_grad = mm_nt((xd_wide * end_wide).astype(BF16), dst_low)
    keep = spread(jnp.broadcast_to(jnp.exp(end), (8, LANES)), marks2)[0:1, :]
    end_row = jnp.sum(xd_wide * b_state, axis=0, keepdims=True) + keep * jnp.sum(
        dst * state_low.astype(F32), axis=0, keepdims=True
    )
    dst_v[...] = keep * dst + mm(jnp.transpose(cmat), carried_grad)

    causal = causal_ones(True)
    inter = mm_nt(cmat, bmat) * causal
    first, second = lane_masks()
    inter_grad = jnp.zeros((SPAN, SPAN), F32)
    yb_t = jnp.transpose(yb)
    parts = []
    for pair in range(heads // 2):
        lanes = slice(pair * LANES, (pair + 1) * LANES)
        xp = xd[:, lanes]
        yp = yb_wide[:, lanes]
        for side, mask in ((0, first), (1, second)):
            h = 2 * pair + side
            gap = jnp.minimum(total2[:, h : h + 1] - total2_t[h : h + 1, :], 0.0)
            fade = jnp.exp2(gap)
            mixing = (fade * inter).astype(BF16)
            inter_grad = inter_grad + mm_nt((yp * mask).astype(BF16), xp) * fade
            parts.append(mm(yb_t[h * head_width : (h + 1) * head_width, :], mixing))
        if pair == heads // 4:
            between()
    xd_grad = jnp.transpose(jnp.concatenate(parts, 0)) + b_state
    inter_low = (inter_grad * causal).astype(BF16)
    c_grad = c_grad + mm(inter_low, bmat)
    b_grad = b_grad + mm(jnp.transpose(inter_low), cmat)

    rows = gather_heads(yb_wide * y_scan - xd_wide * xd_grad, marks_t2)
    end_sum = gather_heads(jnp.broadcast_to(end_row, (8, inner)), marks_t2)[0:1, :]
    decay_grad = mm_exact(causal_ones(False), rows) + end_sum
    dt_grad = decay_grad * rate + gather_heads(xc * xd_grad, marks_t2)
    small[7:8, 0:LANES] += jnp.sum(decay_grad * dt, axis=0, keepdims=True) * rate
    step_grad = dt_grad * sigmoid(step_pre)
    small[7:8, LANES : 2 * LANES] += jnp.sum(step_grad, axis=0, keepdims=True)
    grads[:, conv + inner :] = step_grad.astype(BF16)

    x_grad = xd_grad * dt_wide + skip * y_grad
    act_grad = jnp.concatenate([x_grad, b_grad, c_grad], 1)
    pre = pre_s[f].astype(F32)
    sig_pre = sigmoid(pre)
    pre_grad = act_grad * sig_pre * (1.0 + pre * (1.0 - sig_pre))
    dext[0:SPAN, :] = pre_grad
    small[6:7, 0:conv] += jnp.sum(pre_grad, axis=0, keepdims=True)
    conv_in = cin_s[f].astype(F32)
    conv_grad = None
    for tap in range(4):
        shifted = dext[3 - tap : 3 - tap + SPAN, :]
        term = pv[2 + tap : 3 + tap, 0:conv] * shifted
        conv_grad = term if conv_grad is None else conv_grad + term
        small[2 + tap : 3 + tap, 0:conv] += jnp.sum(conv_in * shifted, axis=0, keepdims=True)
    dext[SPAN:, :] = dext[0:8, :]
    grads[:, inner : inner + conv] = conv_grad.astype(BF16)

    normed_grad = mm_nt(grads[:, 0 : 2 * inner], w_v[:, 0 : 2 * inner])
    normed_grad = normed_grad + mm_nt(grads[:, 2 * inner : inner + conv], ws_v[...])
    normed_grad = normed_grad + mm_nt(
        grads[:, inner + conv :], w_v[:, 2 * inner : 2 * inner + LANES]
    )
    x = x[...].astype(F32)
    inv = lax.rsqrt(jnp.mean(x * x, axis=1, keepdims=True) + NORM_EPSILON)
    scaled_x = x * inv
    small[0:1, :] += jnp.sum(normed_grad * scaled_x, axis=0, keepdims=True)
    scaled = normed_grad * pv[0:1, :]
    inner_mean = jnp.mean(x * scaled, axis=1, keepdims=True)
    part = inv * scaled - x * (inv * inv * inv * inner_mean)
    stage[...] = part.astype(BF16).reshape(stage.shape)

    put_branch.wait()
    turned[...] = jnp.transpose((scaled_x * pv[0:1, :]).astype(BF16))
    put_normed.start()
    put_grads.start()


def mixer(
    x_hbm,
    c_hbm,
    w_hbm,
    ws_hbm,
    pv,
    edge,
    across,
    mine,
    rs1,
    rs2,
    grads_hbm,
    lowered_hbm,
    branch_hbm,
    normed_hbm,
    own,
    state_sum,
    vectors,
    head_sums,
    totals,
    w_v,
    ws_v,
    xbuf,
    cbuf,
    cin_s,
    pre_s,
    gate_s,
    y_s,
    sp_s,
    state_s,
    state_v,
    dst_v,
    ext,
    wgrad,
    tiles,
    small,
    grads,
    lowered_v,
    turned,
    stage,
    edge_v,
    across_v,
    mine_v,
    pair,
    total_v,
    rsv,
    stat_own,
    stat_in,
    small1,
    small2,
    small3,
    state_in,
    w_sem,
    load_sem,
    edge_send,
    edge_recv,
    across_send,
    across_recv,
    keep_sem,
    mine_sem,
    pump_sem,
    stat_send,
    stat_recv,
    rs1_send,
    rs1_recv,
    rs2_send,
    rs2_recv,
    rs_sem,
    put_sem,
    tile_sem,
    sm_send,
    sm_recv,
    st_send,
    st_recv,
    *,
    dp,
    tp,
    sizes,
    norm_width,
):
    me = lax.axis_index("dp")
    z = lax.axis_index("tensor")
    inner, head_width, heads = sizes
    tokens, depth = x_hbm.shape
    blocks = tokens // SPAN
    per = LENGTH // SPAN
    sequences = blocks // per
    cycle = 2 * per
    pieces = 2 * blocks
    half = dp // 2
    rows = depth // dp
    conv = inner + ws_hbm.shape[1]
    wide = inner + conv + LANES
    saved = (cin_s, pre_s, gate_s, y_s, sp_s, state_s)
    parity = lax.rem(me, 2)
    chip = me // 2
    sibling = me + 1 - 2 * parity
    is_middle = (z == 1) | (z == 2)
    is_end = (z == 0) | (z == 3)
    edge_peer = flipped(z, 1)
    across_peer = 3 - z

    barrier = pltpu.get_barrier_semaphore()
    greet = [(sibling, z)]
    greet += [(2 * lax.rem(chip + k, half) + parity, z) for k in range(1, half)]
    greet += [(me, flipped(z, k)) for k in range(1, tp)]
    for device in greet:
        pl.semaphore_signal(barrier, inc=1, device_id=device, device_id_type=MESH)

    loads_w = [
        pltpu.make_async_copy(w_hbm, w_v, w_sem.at[0]),
        pltpu.make_async_copy(ws_hbm, ws_v, w_sem.at[1]),
    ]
    for copy in loads_w:
        copy.start()

    def block_of(n):
        s, r = n // cycle, lax.rem(n, cycle)
        back = r // per
        pos = lax.rem(r, per)
        return per * s + (1 - back) * pos + back * (per - 1 - pos)

    def slot_of(n):
        return blocks * (lax.rem(n, cycle) // per) + block_of(n)

    def loads(n):
        slot = lax.rem(n, 2)
        at = pl.multiple_of(block_of(n) * SPAN, SPAN)
        return [
            pltpu.make_async_copy(x_hbm.at[pl.ds(at, SPAN)], xbuf.at[slot], load_sem.at[0, slot]),
            pltpu.make_async_copy(c_hbm.at[pl.ds(at, SPAN)], cbuf.at[slot], load_sem.at[1, slot]),
        ]

    def next_block(n):
        for copy in loads(n):
            copy.wait()

        @pl.when(n + 1 < pieces)
        def _():
            for copy in loads(n + 1):
                copy.start()

    def edge_copy(n, h, source):
        slot = slot_of(n)
        return pltpu.make_async_remote_copy(
            src_ref=source,
            dst_ref=edge.at[slot, h],
            send_sem=edge_send.at[slot, h],
            recv_sem=edge_recv.at[slot, h],
            device_id=(me, edge_peer),
            device_id_type=MESH,
        )

    def inward(n, h):
        return edge_copy(n, h, mine.at[slot_of(n), h])

    def outward(n, h):
        return edge_copy(n, h, total_v.at[lax.rem(n, 2), h])

    def kept(n, h):
        slot = slot_of(n)
        return pltpu.make_async_copy(total_v.at[lax.rem(n, 2), h], edge.at[slot, h], keep_sem.at[slot, h])

    def across_copy(n, h):
        slot = slot_of(n)
        return pltpu.make_async_remote_copy(
            src_ref=pair.at[lax.rem(n, 2), h],
            dst_ref=across.at[slot, h],
            send_sem=across_send.at[slot, h],
            recv_sem=across_recv.at[slot, h],
            device_id=(me, across_peer),
            device_id_type=MESH,
        )

    def edge_load(n, h):
        return pltpu.make_async_copy(edge.at[slot_of(n), h], edge_v.at[h], pump_sem.at[0, h])

    def across_load(n, h):
        return pltpu.make_async_copy(across.at[slot_of(n), h], across_v.at[h], pump_sem.at[1, h])

    def mine_load(n, h):
        return pltpu.make_async_copy(mine.at[slot_of(n), h], mine_v.at[h], pump_sem.at[2, h])

    def store_piece(n):
        return pltpu.make_async_copy(stage, mine.at[slot_of(n)], mine_sem.at[0])

    def begin_combine(n, h):
        inward(n, h).wait_recv()
        edge_load(n, h).start()
        mine_load(n, h).start()

    def end_combine(n, h):
        @pl.when(n >= 2)
        def _():
            across_copy(n - 2, h).wait_send()

        edge_load(n, h).wait()
        mine_load(n, h).wait()
        pair[lax.rem(n, 2), h] = add_low(mine_v[h], edge_v[h])
        across_copy(n, h).start()

    def begin_finish(n, h):
        across_copy(n, h).wait_recv()
        across_load(n, h).start()

    def end_finish(n, h):
        @pl.when(n >= 2)
        def _():
            outward(n - 2, h).wait_send()
            kept(n - 2, h).wait()

        across_load(n, h).wait()
        slot = lax.rem(n, 2)
        total_v[slot, h] = add_low(pair[slot, h], across_v[h])
        outward(n, h).start()
        kept(n, h).start()

    ticks = 3 * per + 1

    def made(tick):
        s, q = (tick - 1) // ticks, lax.rem(tick - 1, ticks) + 1
        return cycle * s + jnp.minimum(q, per) + jnp.maximum(q - per - 1, 0) // 2

    def combined(tick):
        return jnp.maximum(3 * tick - 4, 0) // 7

    def finished(tick):
        return combined(jnp.maximum(tick - 4, 0))

    def sent(tick):
        paced = jnp.minimum(made(jnp.maximum(tick, 1)), (3 * tick + 9) // 7)
        return jnp.where(tick == ticks * sequences, pieces, jnp.where(tick < 1, 0, paced))

    def pump(tick):
        @pl.when(is_end)
        def _():
            @pl.loop(sent(tick - 1), sent(tick))
            def _(k):
                for h in (0, 1):
                    inward(k, h).start()

        def middle(count, when, step):
            @pl.when(is_middle & (when >= 1) & (count(when) > count(when - 1)))
            def _():
                for h in (0, 1):
                    step(count(when) - 1, h)

        middle(finished, tick - 1, end_finish)
        middle(combined, tick - 1, end_combine)
        middle(finished, tick, begin_finish)
        middle(combined, tick, begin_combine)

    def combine(n, apart=False):
        for group in ((0,), (1,)) if apart else ((0, 1),):
            for h in group:
                begin_combine(n, h)
            for h in group:
                end_combine(n, h)

    def finish(n, apart=False):
        for group in ((0,), (1,)) if apart else ((0, 1),):
            for h in group:
                begin_finish(n, h)
            for h in group:
                end_finish(n, h)

    def free_stage(n):
        @pl.when(is_middle & (n >= 1))
        def _():
            store_piece(n - 1).wait()

    def keep_piece(n):
        store_piece(n).start()

        @pl.when(is_end)
        def _():
            store_piece(n).wait()

    def puts(b, which):
        pairs = (
            (grads, grads_hbm),
            (lowered_v, lowered_hbm),
            (turned, branch_hbm),
            (turned, normed_hbm),
        )
        return [
            pltpu.make_async_copy(pairs[k][0], pairs[k][1].at[b], put_sem.at[k]) for k in which
        ]

    def stat_copy(s, k):
        return pltpu.make_async_remote_copy(
            src_ref=stat_own.at[s],
            dst_ref=stat_in.at[s, k - 1],
            send_sem=stat_send.at[s, k - 1],
            recv_sem=stat_recv.at[s, k - 1],
            device_id=(me, flipped(z, k)),
            device_id_type=MESH,
        )

    for copy in loads(0):
        copy.start()
    small[...] = jnp.zeros_like(small)
    pl.semaphore_wait(barrier, len(greet))
    for copy in loads_w:
        copy.wait()

    @pl.loop(0, sequences)
    def _(s):
        first_n = s * cycle
        ext[0:8, :] = jnp.zeros((8, conv), F32)
        state_v[...] = jnp.zeros_like(state_v)

        @pl.loop(0, per)
        def _(f):
            n = first_n + f
            next_block(n)
            free_stage(n)
            slot = lax.rem(n, 2)
            forward_step(
                f,
                xbuf.at[slot],
                cbuf.at[slot],
                w_v,
                ws_v,
                pv,
                saved,
                state_v,
                ext,
                stage,
                stat_own.at[s, f],
                sizes,
            )

            keep_piece(n)

            @pl.when(f == per - 1)
            def _():
                for k in range(1, tp):
                    stat_copy(s, k).start()

            pump(ticks * s + 1 + f)

        for k in range(1, tp):
            stat_copy(s, k).wait()
        pump(ticks * s + per + 1)
        ext[SPAN:, :] = jnp.zeros((8, conv), F32)
        dst_v[...] = jnp.zeros_like(dst_v)
        totals[s] = (stat_own[s] + stat_in[s, 0]) + (stat_in[s, 1] + stat_in[s, 2])

        @pl.loop(0, per)
        def _(j):
            n = first_n + per + j
            f = per - 1 - j
            b = per * s + f
            tick = ticks * s + per + 1 + 2 * j
            next_block(n)
            free_stage(n)

            @pl.when(b != per - 1)
            def _():
                for copy in puts(b, (0, 1, 3)):
                    copy.wait()

            slot = lax.rem(n, 2)
            backward_step(
                f,
                xbuf.at[slot],
                cbuf.at[slot],
                w_v,
                ws_v,
                pv,
                totals[s, f],
                saved,
                dst_v,
                ext,
                small,
                grads,
                lowered_v,
                turned,
                puts(b, range(4)),
                lambda: pump(tick + 1),
                stage,
                sizes,
                norm_width,
            )
            keep_piece(n)
            pump(tick + 2)

    def to_sibling(q):
        at = pl.multiple_of((2 * q + 1 - parity) * rows, 16)
        return pltpu.make_async_remote_copy(
            src_ref=wgrad.at[pl.ds(at, rows)],
            dst_ref=rs1.at[q],
            send_sem=rs1_send.at[q],
            recv_sem=rs1_recv.at[q],
            device_id=(sibling, z),
            device_id_type=MESH,
        )

    def to_owner(k):
        q = lax.rem(chip + k, half)
        at = pl.multiple_of((2 * q + parity) * rows, 16)
        return pltpu.make_async_remote_copy(
            src_ref=wgrad.at[pl.ds(at, rows)],
            dst_ref=rs2.at[chip],
            send_sem=rs2_send.at[k],
            recv_sem=rs2_recv.at[k],
            device_id=(2 * q + parity, z),
            device_id_type=MESH,
        )

    def small_copy(source, target, index, device):
        return pltpu.make_async_remote_copy(
            src_ref=source,
            dst_ref=target,
            send_sem=sm_send.at[index],
            recv_sem=sm_recv.at[index],
            device_id=device,
            device_id_type=MESH,
        )

    def fetch(source):
        copy = pltpu.make_async_copy(source, rsv, rs_sem.at[0])
        copy.start()
        copy.wait()
        return rsv[...].astype(F32)

    def left_operand(source):
        return [
            pltpu.make_async_copy(source.at[b], w_v.at[:, pl.ds(b * SPAN, SPAN)], tile_sem.at[2 + b])
            for b in range(blocks)
        ]

    def tile_load(source, at, size, slot):
        return pltpu.make_async_copy(
            source.at[:, :, pl.ds(at, size)], tiles.at[slot, :, :, pl.ds(0, size)], tile_sem.at[slot]
        )

    def products(source, width, place):
        whole = width // 256

        @pl.loop(0, whole)
        def _(t):
            slot = lax.rem(t, 2)
            at = pl.multiple_of(t * 256, 256)
            tile_load(source, at, 256, slot).wait()

            @pl.when(t + 1 < whole)
            def _():
                tile_load(source, pl.multiple_of(at + 256, 256), 256, 1 - slot).start()

            right = tiles[slot].reshape(tokens, 256)
            wgrad[:, pl.ds(pl.multiple_of(place + at, 128), 256)] = mm(
                w_v[:, 0:tokens], right
            ).astype(BF16)

    for copy in puts(per * (sequences - 1), (0, 1, 3)):
        copy.wait()
    last_tick = ticks * sequences
    count = lambda tick: max(3 * tick - 4, 0) // 7
    done_finish, done_combine = count(last_tick - 4), count(last_tick)

    @pl.when(is_middle)
    def _():
        store_piece(pieces - 1).wait()
        for h in (0, 1):
            if count(last_tick - 4) > count(last_tick - 5):
                end_finish(done_finish - 1, h)
            if count(last_tick) > count(last_tick - 1):
                end_combine(done_combine - 1, h)

    for copy in left_operand(normed_hbm):
        copy.start()
    tile_load(grads_hbm, 0, 256, 0).start()
    for copy in left_operand(normed_hbm):
        copy.wait()
    products(grads_hbm, wide, 0)
    rest = wide % 256
    last = tile_load(grads_hbm, wide - rest, rest, 0)
    last.start()
    last.wait()
    wgrad[:, wide - rest : wide] = mm(
        w_v[:, 0:tokens], tiles[0].reshape(tokens, 256)[:, 0:rest]
    ).astype(BF16)
    for copy in left_operand(branch_hbm):
        copy.start()
    tile_load(lowered_hbm, 0, 256, 0).start()

    steps, behind = [], done_finish
    for n in range(done_combine, pieces):
        while behind <= n - 2:
            steps.append((finish, behind))
            behind += 1
        steps.append((combine, n))
    steps += [(finish, n) for n in range(behind, pieces)]

    def drain(upto):
        count = steps.index((combine, upto)) + 1 if upto < pieces else len(steps)

        @pl.when(is_middle)
        def _():
            for step, n in steps[:count]:
                step(n, n >= pieces - 2)

        del steps[:count]

    drain(done_combine)
    for copy in left_operand(branch_hbm):
        copy.wait()
    products(lowered_hbm, inner, wide)

    @pl.loop(0, half)
    def _(q):
        to_sibling(q).start()

    first_small = small_copy(small, small1, 0, (sibling, z))
    first_small.start()
    drain(done_combine + 2)
    first_small.wait()
    small2[chip] = small[...] + small1[...]
    second_small = [
        small_copy(
            small2.at[chip], small2.at[chip], k, (2 * lax.rem(chip + k, half) + parity, z)
        )
        for k in range(1, half)
    ]
    for copy in second_small:
        copy.start()

    @pl.loop(1, half)
    def _(k):
        q = lax.rem(chip + k, half)
        to_sibling(q).wait_recv()
        at = pl.multiple_of((2 * q + parity) * rows, 16)
        wgrad[pl.ds(at, rows), :] = (
            wgrad[pl.ds(at, rows), :].astype(F32) + fetch(rs1.at[q])
        ).astype(BF16)
        to_owner(k).start()

    drain(pieces - 2)
    to_sibling(chip).wait_recv()
    own[...] = wgrad[pl.ds(pl.multiple_of(me * rows, 16), rows), :].astype(F32) + fetch(
        rs1.at[chip]
    )
    for copy in second_small:
        copy.wait()
    total = small2[0]
    for q in range(1, half):
        total = total + small2[q]
    small3[z] = total
    third_small = [
        small_copy(small3.at[z], small3.at[z], half + k, (me, flipped(z, k)))
        for k in range(1, tp)
    ]
    for copy in third_small:
        copy.start()
    drain(pieces - 1)

    @pl.loop(1, half)
    def _(k):
        to_owner(k).wait_recv()
        own[...] += fetch(rs2.at[lax.rem(chip + half - k, half)])

    share = state_sum.shape[0]
    state_columns = pl.ds(2 * inner, conv - inner)

    def state_rows(device):
        return pl.ds(pl.multiple_of(device * share, 8), share)

    state_copies = [
        pltpu.make_async_remote_copy(
            src_ref=own.at[state_rows(flipped(z, k)), state_columns],
            dst_ref=state_in.at[k - 1],
            send_sem=st_send.at[k - 1],
            recv_sem=st_recv.at[k - 1],
            device_id=(me, flipped(z, k)),
            device_id_type=MESH,
        )
        for k in range(1, tp)
    ]
    if share * tp == rows:
        for copy in state_copies:
            copy.start()
    else:
        state_copies = []

    for copy in third_small:
        copy.wait()
    vectors[...] = jnp.zeros_like(vectors)
    both = conv - inner
    shared = small3[0, 2:7, inner:conv]
    before = small3[0, 0:1, :]
    for k in range(1, tp):
        shared = shared + small3[k, 2:7, inner:conv]
        before = before + small3[k, 0:1, :]
    for k in range(tp):
        vectors[0:5, k * inner : (k + 1) * inner] = small3[k, 2:7, 0:inner]
        vectors[5:6, depth + k * inner : depth + (k + 1) * inner] = small3[k, 1:2, 0:inner]
        head_sums[k, 0:1, :] = small3[k, 7:8, 0:LANES]
        head_sums[k, 1:2, :] = small3[k, 7:8, LANES : 2 * LANES]
        marks_t = head_marks_t(head_width, inner)
        skips = gather_heads(
            jnp.broadcast_to(small3[k, 1:2, inner : 2 * inner], (8, inner)),
            jnp.concatenate([marks_t, marks_t], 0),
        )
        head_sums[k, 2:8, :] = skips[2:8, :]
    vectors[0:5, tp * inner : tp * inner + both] = shared
    vectors[5:6, 0:depth] = before

    for copy in state_copies:
        copy.wait()
    if state_copies:
        state_sum[...] = own[state_rows(z), state_columns] + (
            state_in[0] + (state_in[1] + state_in[2])
        )
    else:
        state_sum[...] = jnp.zeros_like(state_sum)
    drain(pieces)

    @pl.loop(0, half)
    def _(q):
        to_sibling(q).wait_send()

    @pl.loop(1, half)
    def _(k):
        to_owner(k).wait_send()

    @pl.when(is_middle)
    def _():
        for n in (pieces - 2, pieces - 1):
            for h in (0, 1):
                across_copy(n, h).wait_send()
                outward(n, h).wait_send()
                kept(n, h).wait()

    @pl.when(is_end)
    def _():
        @pl.loop(0, pieces)
        def _(n):
            for h in (0, 1):
                inward(n, h).wait_send()
                outward(n, h).wait_recv()


def finalize(x_ref, c_ref, out_ref, in_ref, totals_ref, block_ref, grad_ref, *, norm_width):
    sums = jnp.transpose(jnp.concatenate([totals_ref[0, 0]] * (LANES // 8), 0))
    scale = lax.rsqrt(sums[:, 0:1] / norm_width + NORM_EPSILON)
    shape = x_ref.shape
    branch = out_ref[0].reshape(shape).astype(F32)
    block_ref[...] = (x_ref[...].astype(F32) + scale * branch).astype(BF16)
    grad_ref[...] = in_ref[0].reshape(shape).astype(F32) + c_ref[...].astype(F32)


def run_finalize(x, c, sums, totals, norm_width):
    tokens, depth = x.shape
    blocks = tokens // SPAN
    per = LENGTH // SPAN
    rows = pl.BlockSpec((SPAN, depth), lambda b: (b, 0))
    return pl.pallas_call(
        functools.partial(finalize, norm_width=norm_width),
        grid=(blocks,),
        in_specs=[
            rows,
            rows,
            pl.BlockSpec((1, 2, HALF, depth), lambda b: (b, 0, 0, 0)),
            pl.BlockSpec((1, 2, HALF, depth), lambda b: (blocks + b, 0, 0, 0)),
            pl.BlockSpec((1, 1, 8, SPAN), lambda b: (b // per, b % per, 0, 0)),
        ],
        out_specs=(rows, rows),
        out_shape=(sds((tokens, depth), BF16), sds((tokens, depth), F32)),
        compiler_params=pltpu.CompilerParams(vmem_limit_bytes=60 * 1024 * 1024),
        cost_estimate=pl.CostEstimate(
            flops=6 * tokens * depth, bytes_accessed=14 * tokens * depth, transcendentals=0
        ),
        name="finalize",
    )(x, c, sums, sums, totals)


def run_mixer(x, c, w, ws, pv, dp, tp, sizes, norm_width):
    inner, head_width, heads = sizes
    tokens, depth = x.shape
    conv_states = ws.shape[1]
    conv = inner + conv_states
    states = conv_states // 2
    wide = inner + conv + LANES
    width = w.shape[1]
    blocks = tokens // SPAN
    per = LENGTH // SPAN
    sequences = blocks // per
    pieces = 2 * blocks
    half = dp // 2
    rows = depth // dp
    hbm = pl.BlockSpec(memory_space=pl.ANY)
    vmem = pl.BlockSpec(memory_space=pltpu.VMEM)
    dma = pltpu.SemaphoreType.DMA
    piece = (2, HALF, depth)
    rows_of_x = (SPAN, depth)
    share = rows // tp if rows % (8 * tp) == 0 else 8
    flops = tokens * (6 * depth * (2 * inner + conv) + 6 * depth * inner + 80 * heads * SPAN * 64)
    return pl.pallas_call(
        functools.partial(mixer, dp=dp, tp=tp, sizes=sizes, norm_width=norm_width),
        in_specs=[hbm] * 4 + [vmem],
        out_specs=(hbm,) * 9 + (vmem,) * 5,
        out_shape=(
            sds((pieces,) + piece, BF16),
            sds((pieces,) + piece, BF16),
            sds((pieces,) + piece, BF16),
            sds((half, rows, wide + inner), BF16),
            sds((half, rows, wide + inner), BF16),
            sds((blocks, SPAN, wide), BF16),
            sds((blocks, SPAN, inner), BF16),
            sds((blocks, depth, SPAN), BF16),
            sds((blocks, depth, SPAN), BF16),
            sds((rows, wide + inner), F32),
            sds((share, conv_states), F32),
            sds((8, tp * inner + depth), F32),
            sds((tp, 8, LANES), F32),
            sds((sequences, per, 8, SPAN), F32),
        ),
        scratch_shapes=[
            pltpu.VMEM((depth, width), BF16),
            pltpu.VMEM((depth, conv_states), BF16),
            pltpu.VMEM((2,) + rows_of_x, BF16),
            pltpu.VMEM((2,) + rows_of_x, BF16),
            pltpu.VMEM((per, SPAN, conv), BF16),
            pltpu.VMEM((per, SPAN, conv), BF16),
            pltpu.VMEM((per, SPAN, inner), BF16),
            pltpu.VMEM((per, SPAN, inner), F32),
            pltpu.VMEM((per, SPAN, LANES), F32),
            pltpu.VMEM((per, states, inner), BF16),
            pltpu.VMEM((states, inner), F32),
            pltpu.VMEM((states, inner), F32),
            pltpu.VMEM((SPAN + 8, conv), F32),
            pltpu.VMEM((depth, wide + inner), BF16),
            pltpu.VMEM((2, blocks, SPAN, 256), BF16),
            pltpu.VMEM((8, depth), F32),
            pltpu.VMEM((SPAN, wide), BF16),
            pltpu.VMEM((SPAN, inner), BF16),
            pltpu.VMEM((depth, SPAN), BF16),
            pltpu.VMEM(piece, BF16),
            pltpu.VMEM(piece, BF16),
            pltpu.VMEM(piece, BF16),
            pltpu.VMEM(piece, BF16),
            pltpu.VMEM((2,) + piece, BF16),
            pltpu.VMEM((2,) + piece, BF16),
            pltpu.VMEM((rows, wide + inner), BF16),
            pltpu.VMEM((sequences, per, 8, SPAN), F32),
            pltpu.VMEM((sequences, tp - 1, per, 8, SPAN), F32),
            pltpu.VMEM((8, depth), F32),
            pltpu.VMEM((half, 8, depth), F32),
            pltpu.VMEM((tp, 8, depth), F32),
            pltpu.VMEM((tp - 1, share, conv_states), F32),
            dma((2,)),
            dma((2, 2)),
            dma((pieces, 2)),
            dma((pieces, 2)),
            dma((pieces, 2)),
            dma((pieces, 2)),
            dma((pieces, 2)),
            dma((1,)),
            dma((3, 2)),
            dma((sequences, tp - 1)),
            dma((sequences, tp - 1)),
            dma((half,)),
            dma((half,)),
            dma((half,)),
            dma((half,)),
            dma((1,)),
            dma((4,)),
            dma((2 + blocks,)),
            dma((half + tp,)),
            dma((half + tp,)),
            dma((tp - 1,)),
            dma((tp - 1,)),
        ],
        compiler_params=pltpu.CompilerParams(
            collective_id=2, has_side_effects=True, vmem_limit_bytes=MIXER_VMEM
        ),
        cost_estimate=pl.CostEstimate(flops=flops, bytes_accessed=60_000_000, transcendentals=0),
        name="mixer",
    )(x, c, w, ws, pv)


def adamw_update(weight, gradient, moment, square, step_rate, decay_rate):
    moment = FIRST_DECAY * moment + (1.0 - FIRST_DECAY) * gradient
    square = SECOND_DECAY * square + (1.0 - SECOND_DECAY) * gradient * gradient
    first_fix = 1.0 - FIRST_DECAY**STEP
    second_fix = 1.0 - SECOND_DECAY**STEP
    update = moment / first_fix / (jnp.sqrt(square / second_fix) + ADAM_EPSILON)
    return (weight - step_rate * (update + decay_rate * weight), moment, square)


def swap(values, mask, tp):
    return lax.ppermute(values, "tensor", [(i, i ^ mask) for i in range(tp)])


def pad_to(values, size):
    return jnp.pad(values, [(0, 0)] * (values.ndim - 1) + [(0, size - values.shape[-1])])


def shards(
    dp,
    tp,
    activations,
    cotangent,
    in_weight,
    in_first,
    in_second,
    step_weight,
    step_first,
    step_second,
    out_weight,
    out_first,
    out_second,
    state_weight,
    state_first,
    state_second,
    conv_weight,
    conv_first,
    conv_second,
    conv_bias,
    bias_first,
    bias_second,
    gain_vector,
    gains_first,
    gains_second,
    head_params,
    head_first,
    head_second,
):
    dp_rank = lax.axis_index("dp")
    rank = lax.axis_index("tensor")
    tokens, depth = activations.shape
    shard_rows, _, inner = in_weight.shape
    norm_width = inner * tp
    heads = step_weight.shape[1]
    head_width = inner // heads
    state_rows, conv_states = state_weight.shape
    conv = inner + conv_states
    taps, conv_own = conv_weight.shape
    gains_own = gain_vector.shape[0]
    sizes = (inner, head_width, heads)

    w_own = jnp.concatenate(
        [
            in_weight.reshape(shard_rows, 2 * inner).astype(BF16),
            pad_to(step_weight.astype(BF16), LANES),
            out_weight.astype(BF16).T,
        ],
        1,
    )
    padded_rows = -(-state_rows // 16) * 16
    st_own = jnp.pad(state_weight.astype(BF16), ((0, padded_rows - state_rows), (0, 0)))
    flat = jnp.concatenate([conv_weight.reshape(-1), conv_bias, gain_vector])
    sm_own = pad_to(flat, -(-flat.shape[0] // 1024) * 1024).reshape(-1, LANES)
    w, st_full, sm_full = run_gather(w_own, st_own, sm_own, dp, tp)
    ws = st_full[:, :, :state_rows].reshape(depth, conv_states)
    small = sm_full.reshape(dp * tp, -1)
    kernel_full = (
        small[:, : taps * conv_own].reshape(-1, taps, conv_own).transpose(1, 0, 2).reshape(taps, -1)
    )
    offsets_full = small[:, taps * conv_own : (taps + 1) * conv_own].reshape(-1)
    gains_full = small[:, (taps + 1) * conv_own : (taps + 1) * conv_own + gains_own].reshape(-1)
    start = rank * inner
    conv_rows = jnp.concatenate([kernel_full, offsets_full[None, :]], 0)
    conv_local = jnp.concatenate(
        [lax.dynamic_slice_in_dim(conv_rows, start, inner, 1), conv_rows[:, norm_width:]], 1
    )
    head_local = lax.dynamic_slice_in_dim(head_params, rank * heads, heads, 1)
    gain_local = lax.dynamic_slice_in_dim(gains_full, depth + start, inner, 0)
    pv = jnp.concatenate(
        [
            gains_full[None, :depth],
            pad_to(jnp.concatenate([gain_local, jnp.repeat(head_local[2], head_width)]), depth)[
                None, :
            ],
            pad_to(conv_local, depth),
            pad_to(
                jnp.concatenate(
                    [pad_to(-jnp.exp(head_local[0]), LANES), pad_to(head_local[1], LANES)]
                ),
                depth,
            )[None, :],
        ],
        0,
    )

    sums, _, _, _, _, _, _, _, _, own, state_sum, vectors, head_sums, totals = run_mixer(
        activations, cotangent, w, ws, pv, dp, tp, sizes, norm_width
    )
    block_output, input_grad = run_finalize(activations, cotangent, sums, totals, norm_width)

    in_owned = own[:, : 2 * inner].reshape(shard_rows, 2, inner)
    state_part = own[:, 2 * inner : inner + conv]
    step_owned = own[:, inner + conv : inner + conv + heads].T
    out_owned = own[:, inner + conv + LANES :].T
    if state_sum.shape[0] == state_rows:
        state_owned = state_sum
    else:
        state_owned = lax.dynamic_slice_in_dim(state_part, rank * state_rows, state_rows, 0)
        for k in range(1, tp):
            theirs = lax.dynamic_slice_in_dim(state_part, (rank ^ k) * state_rows, state_rows, 0)
            state_owned = state_owned + swap(theirs, k, tp)
    head_grad = head_sums[:, :3, :heads].transpose(1, 0, 2).reshape(3, tp * heads)
    device = dp_rank * tp + rank
    conv_owned = lax.dynamic_slice(vectors, (0, device * conv_own), (taps + 1, conv_own))
    gains_owned = lax.dynamic_slice(vectors, (taps + 1, device * gains_own), (1, gains_own))[0]

    in_new = adamw_update(in_weight, in_owned, in_first, in_second, RATE_MATRIX, WEIGHT_DECAY)
    step_new = adamw_update(
        step_weight.T, step_owned, step_first.T, step_second.T, RATE_MATRIX, WEIGHT_DECAY
    )
    step_new = tuple(value.T for value in step_new)
    out_new = adamw_update(out_weight, out_owned, out_first, out_second, RATE_OUTPUT, WEIGHT_DECAY)
    state_new = adamw_update(
        state_weight, state_owned, state_first, state_second, RATE_MATRIX, WEIGHT_DECAY
    )
    conv_new = adamw_update(conv_weight, conv_owned[:taps], conv_first, conv_second, RATE_CONV, 0.0)
    bias_new = adamw_update(conv_bias, conv_owned[taps], bias_first, bias_second, RATE_VECTOR, 0.0)
    gains_new = adamw_update(gain_vector, gains_owned, gains_first, gains_second, RATE_VECTOR, 0.0)
    head_new = adamw_update(head_params, head_grad, head_first, head_second, RATE_HEADS, 0.0)
    return (
        (block_output, input_grad)
        + in_new
        + step_new
        + out_new
        + state_new
        + conv_new
        + bias_new
        + gains_new
        + head_new
    )


def solution(mesh):
    both = ("dp", "tensor")
    rows = P("dp", None)
    projection = P("dp", None, "tensor")
    step = P("dp", "tensor")
    out = P("tensor", "dp")
    state = P(both, None)
    taps = P(None, both)
    vector = P(both)
    parameters = sum(
        ((spec,) * 3 for spec in (projection, step, out, state, taps, vector, vector, P())), ()
    )
    return jax.shard_map(
        functools.partial(shards, mesh.shape["dp"], mesh.shape["tensor"]),
        mesh=mesh,
        in_specs=(rows, rows) + parameters,
        out_specs=(rows, rows) + parameters,
        check_vma=False,
    )
```

```python
import functools

import jax
import jax.numpy as jnp
from jax import lax
from jax.experimental import pallas as pl
from jax.experimental.pallas import tpu as pltpu
from jax.sharding import PartitionSpec as P

F32 = jnp.float32
BF16 = jnp.bfloat16
MESH = pl.DeviceIdType.MESH

SPAN = 256
LENGTH = 1024
STEP = 5
LANES = 128
LOG2E = 1.4426950408889634
NORM_EPSILON = 1e-05
FIRST_DECAY = 0.9
SECOND_DECAY = 0.95
ADAM_EPSILON = 1e-08
WEIGHT_DECAY = 0.1
RATE_MATRIX = 0.05
RATE_OUTPUT = 0.04
RATE_CONV = 1.0
RATE_VECTOR = 0.5
RATE_HEADS = 2.0
MIXER_VMEM = 63 * 1024 * 1024


def mm(a, b):
    return lax.dot_general(a, b, (((1,), (0,)), ((), ())), preferred_element_type=F32)


def mm_nt(a, b):
    return lax.dot_general(a, b, (((1,), (1,)), ((), ())), preferred_element_type=F32)


def mm_ones(ones, v):
    high, low = split_low(v)
    rest = (v - high.astype(F32) - low.astype(F32)).astype(BF16)
    parts = mm(ones, jnp.concatenate([high, low, rest], 1))
    width = v.shape[1]
    return parts[:, 0:width] + parts[:, width : 2 * width] + parts[:, 2 * width :]


def sigmoid(v):
    return 0.5 * jnp.tanh(0.5 * v) + 0.5


def softplus(v):
    return jnp.maximum(v, 0.0) + jnp.log1p(jnp.exp(-jnp.abs(v)))


def split_low(v):
    high = v.astype(BF16)
    return high, (v - high.astype(F32)).astype(BF16)


def head_marks(head_width, channels):
    head = lax.broadcasted_iota(jnp.int32, (LANES, channels), 0)
    channel = lax.broadcasted_iota(jnp.int32, (LANES, channels), 1)
    inside = (channel >= head * head_width) & (channel < (head + 1) * head_width)
    return inside.astype(F32).astype(BF16)


def head_marks_t(head_width, channels):
    head = lax.broadcasted_iota(jnp.int32, (channels, LANES), 1)
    channel = lax.broadcasted_iota(jnp.int32, (channels, LANES), 0)
    inside = (channel >= head * head_width) & (channel < (head + 1) * head_width)
    return inside.astype(F32).astype(BF16)


def spread(v, marks2):
    high, low = split_low(v)
    return mm(jnp.concatenate([high, low], 1), marks2)


def gather_heads(v, marks_t2):
    high, low = split_low(v)
    return mm(jnp.concatenate([high, low], 1), marks_t2)


def causal_ones(lower):
    row = lax.broadcasted_iota(jnp.int32, (SPAN, SPAN), 0)
    col = lax.broadcasted_iota(jnp.int32, (SPAN, SPAN), 1)
    keep = row >= col if lower else row <= col
    return keep.astype(F32).astype(BF16)


def lane_masks():
    lane = lax.broadcasted_iota(jnp.int32, (1, LANES), 1)
    first = (lane < LANES // 2).astype(F32)
    return first, 1.0 - first


def sds(shape, dtype):
    return jax.ShapeDtypeStruct(shape, dtype)


def axis_bits(size):
    count = size.bit_length() - 1
    order = list(range(1, count)) + [0]
    other = [order[1], order[0]] + order[2:] if count >= 3 else order
    return order, other


def flipped(index, mask):
    result = index
    bit = 1
    while bit <= mask:
        if mask & bit:
            result = result + bit * (1 - 2 * ((index // bit) % 2))
        bit *= 2
    return result


def gather_weights(
    w_own, st_own, sm_own, w_full, st_full, sm_full,
    local_sem, dp_send, dp_recv, z_send, z_recv, send_sem, recv_sem,
    *, dp, tp, cut
):
    me = lax.axis_index("dp")
    tensor = lax.axis_index("tensor")
    rows, width = w_own.shape
    count = dp.bit_length() - 1

    barrier = pltpu.get_barrier_semaphore()
    for k in range(1, dp):
        pl.semaphore_signal(
            barrier, inc=1, device_id=(flipped(me, k), tensor), device_id_type=MESH
        )
    for k in range(1, tp):
        pl.semaphore_signal(barrier, inc=1, device_id=(me, flipped(tensor, k)), device_id_type=MESH)
    pl.semaphore_wait(barrier, dp + tp - 2)

    orders = axis_bits(dp)
    parts = (pl.ds(0, cut), pl.ds(cut, width - cut))

    def row_of(mask):
        return pl.multiple_of(flipped(me, mask) * rows, 16)

    def full_mask(bits, packed):
        return sum(1 << bits[j] for j in range(count) if packed >> j & 1)

    def move(kind, packed, j):
        bits, columns = orders[kind], parts[kind]
        mask = full_mask(bits, packed)
        slot = packed | (1 << j)
        place = w_full.at[pl.ds(row_of(mask), rows), columns]
        return pltpu.make_async_remote_copy(
            src_ref=w_own.at[:, columns] if mask == 0 else place,
            dst_ref=place,
            send_sem=send_sem.at[kind, slot],
            recv_sem=recv_sem.at[kind, slot],
            device_id=(flipped(me, 1 << bits[j]), tensor),
            device_id_type=MESH,
        )

    smalls = ((st_own, st_full), (sm_own, sm_full))
    direct = [
        pltpu.make_async_remote_copy(
            src_ref=own,
            dst_ref=full.at[tensor, me],
            send_sem=dp_send.at[which, k],
            recv_sem=dp_recv.at[which, k],
            device_id=(flipped(me, k), tensor),
            device_id_type=MESH,
        )
        for k in range(1, dp)
        for which, (own, full) in enumerate(smalls)
    ]
    started = []

    def start(kind, packed, j):
        copy = move(kind, packed, j)
        copy.start()
        started.append(copy)

    kept = [
        pltpu.make_async_copy(own, full.at[tensor, me], local_sem.at[which])
        for which, (own, full) in enumerate(smalls)
    ]
    kept.append(pltpu.make_async_copy(w_own, w_full.at[pl.ds(row_of(0), rows)], local_sem.at[2]))
    for copy in direct:
        copy.start()
    for j in range(count):
        for kind in (0, 1):
            start(kind, 0, j)
    for copy in kept:
        copy.start()
    for copy in kept + direct:
        copy.wait()
    along = [
        pltpu.make_async_remote_copy(
            src_ref=full.at[tensor],
            dst_ref=full.at[tensor],
            send_sem=z_send.at[which, k],
            recv_sem=z_recv.at[which, k],
            device_id=(me, flipped(tensor, k)),
            device_id_type=MESH,
        )
        for k in range(1, tp)
        for which, (own, full) in enumerate(smalls)
    ]
    for copy in along:
        copy.start()
    for packed in range(1, dp):
        top = packed.bit_length() - 1
        for kind in (0, 1):
            move(kind, packed & ~(1 << top), top).wait_recv()
            for j in range(top + 1, count):
                start(kind, packed, j)
    for copy in along:
        copy.wait()
    for copy in started:
        copy.wait_send()


def run_gather(w_own, st_own, sm_own, dp, tp):
    rows, width = w_own.shape
    cut = width // 2 // LANES * LANES
    hbm = pl.BlockSpec(memory_space=pl.ANY)
    dma = pltpu.SemaphoreType.DMA
    return pl.pallas_call(
        functools.partial(gather_weights, dp=dp, tp=tp, cut=cut),
        in_specs=[hbm] * 3,
        out_specs=(hbm,) * 3,
        out_shape=(
            sds((dp * rows, width), BF16),
            sds((tp, dp) + st_own.shape, BF16),
            sds((tp, dp) + sm_own.shape, F32),
        ),
        scratch_shapes=[
            dma((3,)),
            dma((2, dp)),
            dma((2, dp)),
            dma((2, tp)),
            dma((2, tp)),
            dma((2, dp)),
            dma((2, dp)),
        ],
        compiler_params=pltpu.CompilerParams(collective_id=1, has_side_effects=True),
        name="gather_weights",
    )(w_own, st_own, sm_own)


def add_low(a, b):
    return (a.astype(F32) + b.astype(F32)).astype(BF16)


PARTS = 4
PART = SPAN // PARTS


def forward_step(f, x, c, w_v, ws_v, pv, masks, saved, state_v, ext, stage, stats, sizes):
    inner, head_width, heads = sizes
    lower_v, upper_v, marks_v, marks_t_v = masks
    cin_s, pre_s, gate_s, y_s, sp_s, state_s = saved
    states = ws_v.shape[1] // 2
    conv = inner + 2 * states

    x = x[...].astype(F32)
    inv = lax.rsqrt(jnp.mean(x * x, axis=1, keepdims=True) + NORM_EPSILON)
    normed = (x * inv * pv[0:1, :]).astype(BF16)

    step_in = mm(normed, w_v[:, 2 * inner : 2 * inner + LANES])
    sp_s[f] = step_in
    ext[8:, 0:inner] = mm(normed, w_v[:, inner : 2 * inner])
    ext[8:, inner:conv] = mm(normed, ws_v[...])
    gate = mm(normed, w_v[:, 0:inner]).astype(BF16)
    gate_s[f] = gate
    gate = gate.astype(F32)
    cin_s[f] = ext[8:, :].astype(BF16)
    pre = pv[6:7, 0:conv]
    for tap in range(4):
        pre = pre + pv[2 + tap : 3 + tap, 0:conv] * ext[5 + tap : 5 + tap + SPAN, :]
    ext[0:8, :] = ext[SPAN : SPAN + 8, :]
    pre = pre.astype(BF16)
    pre_s[f] = pre
    pre = pre.astype(F32)
    act = pre * sigmoid(pre)

    rate = pv[7:8, 0:LANES]
    dt = softplus(step_in + pv[7:8, LANES : 2 * LANES])
    total = mm_ones(lower_v[...], dt * rate)
    total2 = total * LOG2E
    total2_t = jnp.transpose(total2)
    marks2 = marks_v[...]
    end = total[SPAN - 1 : SPAN, :]
    xc = act[:, 0:inner]
    bmat = act[:, inner : inner + states].astype(BF16)
    cmat = act[:, inner + states :].astype(BF16)
    xd = (xc * spread(dt, marks2)).astype(BF16)
    weighted = (xd.astype(F32) * spread(jnp.exp(end - total), marks2)).astype(BF16)

    state = state_v[...]
    state_low = state.astype(BF16)
    state_s[f] = state_low
    carried = spread(jnp.exp(total), marks2) * mm(cmat, state_low)
    keep = spread(jnp.broadcast_to(jnp.exp(end), (8, LANES)), marks2)[0:1, :]
    state_v[...] = keep * state + mm(jnp.transpose(bmat), weighted)

    inter = mm_nt(cmat, bmat) * lower_v[...].astype(F32)
    first, second = lane_masks()
    skip = pv[1:2, inner : 2 * inner]
    parts = []
    for pair in range(heads // 2):
        lanes = slice(pair * LANES, (pair + 1) * LANES)
        xp = xd[:, lanes].astype(F32)
        within = None
        for side, mask in ((0, first), (1, second)):
            h = 2 * pair + side
            gap = jnp.minimum(total2[:, h : h + 1] - total2_t[h : h + 1, :], 0.0)
            mixing = (jnp.exp2(gap) * inter).astype(BF16)
            term = mm(mixing, (xp * mask).astype(BF16))
            within = term if within is None else within + term
        parts.append(within)
    y = jnp.concatenate(parts, 1) + carried
    y_s[f] = y
    y = y + skip * xc
    gated = y * gate * sigmoid(gate)
    squares = jnp.sum(gated * gated, axis=1, keepdims=True)
    lowered = (gated * pv[1:2, 0:inner]).astype(BF16)
    out = mm_nt(lowered, w_v[:, 2 * inner + LANES :])
    stage[...] = out.astype(BF16).reshape(stage.shape)
    dots = jnp.sum(c[...].astype(F32) * out, axis=1, keepdims=True)
    lane = lax.broadcasted_iota(jnp.int32, (SPAN, LANES), 1)
    both = jnp.where(lane == 0, squares, jnp.where(lane == 1, dots, 0.0))
    stats[...] = jnp.transpose(both)[0:8, :]


def backward_step(
    f, x, c, w_v, ws_v, pv, masks, totals, saved, dst_v, dext, small, grads, lowered_v, turned, put, between, stage, sizes, norm_width
):
    inner, head_width, heads = sizes
    lower_v, upper_v, marks_v, marks_t_v = masks
    cin_s, pre_s, gate_s, y_s, sp_s, state_s = saved
    states = ws_v.shape[1] // 2
    conv = inner + 2 * states
    put_grads, put_lowered, put_branch, put_normed = put

    sums = jnp.transpose(jnp.concatenate([totals] * (LANES // 8), 0))
    scale = lax.rsqrt(sums[:, 0:1] / norm_width + NORM_EPSILON)
    bg = (scale * c[...].astype(F32)).astype(BF16)
    squares_grad = (-0.5 / norm_width) * sums[:, 1:2] * scale * scale * scale
    low_grad = mm(bg, w_v[:, 2 * inner + LANES :])

    pre = pre_s[f].astype(F32)
    sig_pre = sigmoid(pre)
    act = pre * sig_pre
    xc = act[:, 0:inner]
    bmat = act[:, inner : inner + states].astype(BF16)
    cmat = act[:, inner + states :].astype(BF16)

    skip = pv[1:2, inner : 2 * inner]
    gate = gate_s[f].astype(F32)
    sig = sigmoid(gate)
    y_scan = y_s[f]
    y = y_scan + skip * xc
    silu_gate = gate * sig
    gated = y * silu_gate
    gain = pv[1:2, 0:inner]
    lowered_v[...] = (gated * gain).astype(BF16)
    put_lowered.start()
    gated_grad = low_grad * gain + 2.0 * gated * squares_grad
    small[1:2, 0:inner] += jnp.sum(low_grad * gated, axis=0, keepdims=True)
    y_grad = gated_grad * silu_gate
    grads[:, 0:inner] = (gated_grad * y * sig * (1.0 + gate * (1.0 - sig))).astype(BF16)
    small[1:2, inner : 2 * inner] += jnp.sum(y_grad * xc, axis=0, keepdims=True)

    turned[...] = jnp.transpose(bg)
    put_branch.start()

    rate = pv[7:8, 0:LANES]
    step_pre = sp_s[f] + pv[7:8, LANES : 2 * LANES]
    dt = softplus(step_pre)
    total = mm_ones(lower_v[...], dt * rate)
    total2 = total * LOG2E
    total2_t = jnp.transpose(total2)
    marks2 = marks_v[...]
    marks_t2 = marks_t_v[...]
    end = total[SPAN - 1 : SPAN, :]
    dt_wide = spread(dt, marks2)
    xd = (xc * dt_wide).astype(BF16)
    xd_wide = xd.astype(F32)
    end_wide = spread(jnp.exp(end - total), marks2)

    yb = y_grad.astype(BF16)
    yb_wide = yb.astype(F32)
    state_low = state_s[f]
    dst = dst_v[...]
    dst_low = dst.astype(BF16)
    carried_grad = (yb_wide * spread(jnp.exp(total), marks2)).astype(BF16)
    c_grad = mm_nt(carried_grad, state_low)
    b_state = mm(bmat, dst_low) * end_wide
    b_grad = mm_nt((xd_wide * end_wide).astype(BF16), dst_low)
    keep = spread(jnp.broadcast_to(jnp.exp(end), (8, LANES)), marks2)[0:1, :]
    end_row = jnp.sum(xd_wide * b_state, axis=0, keepdims=True) + keep * jnp.sum(
        dst * state_low.astype(F32), axis=0, keepdims=True
    )
    dst_v[...] = keep * dst + mm(jnp.transpose(cmat), carried_grad)

    causal = lower_v[...].astype(F32)
    inter = mm_nt(cmat, bmat) * causal
    first, second = lane_masks()
    inter_grad = jnp.zeros((SPAN, SPAN), F32)
    yb_t = jnp.transpose(yb)
    parts = []
    for pair in range(heads // 2):
        lanes = slice(pair * LANES, (pair + 1) * LANES)
        xp = xd[:, lanes]
        yp = yb_wide[:, lanes]
        for side, mask in ((0, first), (1, second)):
            h = 2 * pair + side
            gap = jnp.minimum(total2[:, h : h + 1] - total2_t[h : h + 1, :], 0.0)
            fade = jnp.exp2(gap)
            mixing = (fade * inter).astype(BF16)
            inter_grad = inter_grad + mm_nt((yp * mask).astype(BF16), xp) * fade
            parts.append(mm(yb_t[h * head_width : (h + 1) * head_width, :], mixing))
        if pair == heads // 4:
            between()
    xd_grad = jnp.transpose(jnp.concatenate(parts, 0)) + b_state
    inter_low = (inter_grad * causal).astype(BF16)
    c_grad = c_grad + mm(inter_low, bmat)
    b_grad = b_grad + mm(jnp.transpose(inter_low), cmat)

    rows = gather_heads(yb_wide * y_scan - xd_wide * xd_grad, marks_t2)
    end_sum = gather_heads(jnp.broadcast_to(end_row, (8, inner)), marks_t2)[0:1, :]
    decay_grad = mm_ones(upper_v[...], rows) + end_sum
    dt_grad = decay_grad * rate + gather_heads(xc * xd_grad, marks_t2)
    small[7:8, 0:LANES] += jnp.sum(decay_grad * dt, axis=0, keepdims=True) * rate
    step_grad = dt_grad * sigmoid(step_pre)
    small[7:8, LANES : 2 * LANES] += jnp.sum(step_grad, axis=0, keepdims=True)
    grads[:, conv + inner :] = step_grad.astype(BF16)

    x_grad = xd_grad * dt_wide + skip * y_grad
    act_grad = jnp.concatenate([x_grad, b_grad, c_grad], 1)
    pre = pre_s[f].astype(F32)
    sig_pre = sigmoid(pre)
    pre_grad = act_grad * sig_pre * (1.0 + pre * (1.0 - sig_pre))
    dext[0:SPAN, :] = pre_grad
    small[6:7, 0:conv] += jnp.sum(pre_grad, axis=0, keepdims=True)
    conv_in = cin_s[f].astype(F32)
    conv_grad = None
    for tap in range(4):
        shifted = dext[3 - tap : 3 - tap + SPAN, :]
        term = pv[2 + tap : 3 + tap, 0:conv] * shifted
        conv_grad = term if conv_grad is None else conv_grad + term
        small[2 + tap : 3 + tap, 0:conv] += jnp.sum(conv_in * shifted, axis=0, keepdims=True)
    dext[SPAN:, :] = dext[0:8, :]
    grads[:, inner : inner + conv] = conv_grad.astype(BF16)

    normed_grad = mm_nt(grads[:, 0 : 2 * inner], w_v[:, 0 : 2 * inner])
    normed_grad = normed_grad + mm_nt(grads[:, 2 * inner : inner + conv], ws_v[...])
    normed_grad = normed_grad + mm_nt(
        grads[:, inner + conv :], w_v[:, 2 * inner : 2 * inner + LANES]
    )
    x = x[...].astype(F32)
    inv = lax.rsqrt(jnp.mean(x * x, axis=1, keepdims=True) + NORM_EPSILON)
    scaled_x = x * inv
    small[0:1, :] += jnp.sum(normed_grad * scaled_x, axis=0, keepdims=True)
    scaled = normed_grad * pv[0:1, :]
    inner_mean = jnp.mean(x * scaled, axis=1, keepdims=True)
    part = inv * scaled - x * (inv * inv * inv * inner_mean)
    stage[...] = part.astype(BF16).reshape(stage.shape)

    put_branch.wait()
    turned[...] = jnp.transpose((scaled_x * pv[0:1, :]).astype(BF16))
    put_normed.start()
    put_grads.start()


def mixer(
    x_hbm,
    c_hbm,
    w_hbm,
    ws_hbm,
    pv,
    edge,
    across,
    mine,
    rs1,
    rs2,
    grads_hbm,
    lowered_hbm,
    branch_hbm,
    normed_hbm,
    own,
    state_sum,
    vectors,
    head_sums,
    totals,
    w_v,
    ws_v,
    xbuf,
    cbuf,
    cin_s,
    pre_s,
    gate_s,
    y_s,
    sp_s,
    state_s,
    state_v,
    dst_v,
    ext,
    wgrad,
    tiles,
    small,
    grads,
    lowered_v,
    turned,
    stage,
    edge_v,
    across_v,
    mine_v,
    pair,
    total_v,
    rsv,
    stat_own,
    stat_in,
    small1,
    small2,
    small3,
    state_in,
    lower_v,
    upper_v,
    marks_v,
    marks_t_v,
    w_sem,
    load_sem,
    edge_send,
    edge_recv,
    across_send,
    across_recv,
    keep_sem,
    mine_sem,
    pump_sem,
    stat_send,
    stat_recv,
    rs1_send,
    rs1_recv,
    rs2_send,
    rs2_recv,
    rs_sem,
    put_sem,
    tile_sem,
    sm_send,
    sm_recv,
    st_send,
    st_recv,
    *,
    dp,
    tp,
    sizes,
    norm_width,
):
    me = lax.axis_index("dp")
    z = lax.axis_index("tensor")
    inner, head_width, heads = sizes
    tokens, depth = x_hbm.shape
    blocks = tokens // SPAN
    per = LENGTH // SPAN
    sequences = blocks // per
    cycle = 2 * per
    pieces = 2 * blocks
    half = dp // 2
    rows = depth // dp
    conv = inner + ws_hbm.shape[1]
    wide = inner + conv + LANES
    saved = (cin_s, pre_s, gate_s, y_s, sp_s, state_s)
    parity = lax.rem(me, 2)
    chip = me // 2
    sibling = me + 1 - 2 * parity
    is_middle = (z == 1) | (z == 2)
    is_end = (z == 0) | (z == 3)
    edge_peer = flipped(z, 1)
    across_peer = 3 - z

    barrier = pltpu.get_barrier_semaphore()
    greet = [(sibling, z)]
    greet += [(2 * lax.rem(chip + k, half) + parity, z) for k in range(1, half)]
    greet += [(me, flipped(z, k)) for k in range(1, tp)]
    for device in greet:
        pl.semaphore_signal(barrier, inc=1, device_id=device, device_id_type=MESH)

    loads_w = [
        pltpu.make_async_copy(w_hbm, w_v, w_sem.at[0]),
        pltpu.make_async_copy(ws_hbm, ws_v, w_sem.at[1]),
    ]
    for copy in loads_w:
        copy.start()

    def block_of(n):
        s, r = n // cycle, lax.rem(n, cycle)
        back = r // per
        pos = lax.rem(r, per)
        return per * s + (1 - back) * pos + back * (per - 1 - pos)

    def slot_of(n):
        return blocks * (lax.rem(n, cycle) // per) + block_of(n)

    def loads(n):
        slot = lax.rem(n, 2)
        at = pl.multiple_of(block_of(n) * SPAN, SPAN)
        return [
            pltpu.make_async_copy(x_hbm.at[pl.ds(at, SPAN)], xbuf.at[slot], load_sem.at[0, slot]),
            pltpu.make_async_copy(c_hbm.at[pl.ds(at, SPAN)], cbuf.at[slot], load_sem.at[1, slot]),
        ]

    def next_block(n):
        for copy in loads(n):
            copy.wait()

        @pl.when(n + 1 < pieces)
        def _():
            for copy in loads(n + 1):
                copy.start()

    def edge_copy(n, h, source):
        slot = slot_of(n)
        return pltpu.make_async_remote_copy(
            src_ref=source,
            dst_ref=edge.at[slot, h],
            send_sem=edge_send.at[slot, h],
            recv_sem=edge_recv.at[slot, h],
            device_id=(me, edge_peer),
            device_id_type=MESH,
        )

    def inward(n, h):
        return edge_copy(n, h, mine.at[slot_of(n), h])

    def outward(n, h):
        return edge_copy(n, h, total_v.at[lax.rem(n, 2), h])

    def kept(n, h):
        slot = slot_of(n)
        return pltpu.make_async_copy(total_v.at[lax.rem(n, 2), h], edge.at[slot, h], keep_sem.at[slot, h])

    def across_copy(n, h):
        slot = slot_of(n)
        return pltpu.make_async_remote_copy(
            src_ref=pair.at[lax.rem(n, 2), h],
            dst_ref=across.at[slot, h],
            send_sem=across_send.at[slot, h],
            recv_sem=across_recv.at[slot, h],
            device_id=(me, across_peer),
            device_id_type=MESH,
        )

    def edge_load(n, h):
        return pltpu.make_async_copy(edge.at[slot_of(n), h], edge_v.at[h], pump_sem.at[0, h])

    def across_load(n, h):
        return pltpu.make_async_copy(across.at[slot_of(n), h], across_v.at[h], pump_sem.at[1, h])

    def mine_load(n, h):
        return pltpu.make_async_copy(mine.at[slot_of(n), h], mine_v.at[h], pump_sem.at[2, h])

    def store_piece(n):
        return pltpu.make_async_copy(stage, mine.at[slot_of(n)], mine_sem.at[0])

    def begin_combine(n, h):
        inward(n, h).wait_recv()
        edge_load(n, h).start()
        mine_load(n, h).start()

    def end_combine(n, h):
        @pl.when(n >= 2)
        def _():
            across_copy(n - 2, h).wait_send()

        edge_load(n, h).wait()
        mine_load(n, h).wait()
        pair[lax.rem(n, 2), h] = add_low(mine_v[h], edge_v[h])
        across_copy(n, h).start()

    def begin_finish(n, h):
        across_copy(n, h).wait_recv()
        across_load(n, h).start()

    def end_finish(n, h):
        @pl.when(n >= 2)
        def _():
            outward(n - 2, h).wait_send()
            kept(n - 2, h).wait()

        across_load(n, h).wait()
        slot = lax.rem(n, 2)
        total_v[slot, h] = add_low(pair[slot, h], across_v[h])
        outward(n, h).start()
        kept(n, h).start()

    ticks = 3 * per + 1

    def made(tick):
        s, q = (tick - 1) // ticks, lax.rem(tick - 1, ticks) + 1
        return cycle * s + jnp.minimum(q, per) + jnp.maximum(q - per - 1, 0) // 2

    def combined(tick):
        return jnp.maximum(2 * tick - 2, 0) // 5

    def finished(tick):
        return combined(jnp.maximum(tick - 3, 0))

    def sent(tick):
        paced = jnp.minimum(made(jnp.maximum(tick, 1)), (3 * tick + 4) // 7)
        return jnp.where(tick == ticks * sequences, pieces, jnp.where(tick < 1, 0, paced))

    def pump(tick):
        @pl.when(is_end)
        def _():
            @pl.loop(sent(tick - 1), sent(tick))
            def _(k):
                for h in range(PARTS):
                    inward(k, h).start()

        @pl.when(is_middle & (finished(tick) > finished(tick - 1)))
        def _():
            finish(finished(tick) - 1)

        @pl.when(is_middle & (combined(tick) > combined(tick - 1)))
        def _():
            combine(combined(tick) - 1)

    def combine(n, apart=False):
        for group in zip(range(PARTS)) if apart else (range(PARTS),):
            for h in group:
                begin_combine(n, h)
            for h in group:
                end_combine(n, h)

    def finish(n, apart=False):
        for group in zip(range(PARTS)) if apart else (range(PARTS),):
            for h in group:
                begin_finish(n, h)
            for h in group:
                end_finish(n, h)

    def free_stage(n):
        @pl.when(is_middle & (n >= 1))
        def _():
            store_piece(n - 1).wait()

    def keep_piece(n):
        store_piece(n).start()

        @pl.when(is_end)
        def _():
            store_piece(n).wait()

    def puts(b, which):
        pairs = (
            (grads, grads_hbm),
            (lowered_v, lowered_hbm),
            (turned, branch_hbm),
            (turned, normed_hbm),
        )
        return [
            pltpu.make_async_copy(pairs[k][0], pairs[k][1].at[b], put_sem.at[k]) for k in which
        ]

    def stat_copy(s, k):
        return pltpu.make_async_remote_copy(
            src_ref=stat_own.at[s],
            dst_ref=stat_in.at[s, k - 1],
            send_sem=stat_send.at[s, k - 1],
            recv_sem=stat_recv.at[s, k - 1],
            device_id=(me, flipped(z, k)),
            device_id_type=MESH,
        )

    for copy in loads(0):
        copy.start()
    small[...] = jnp.zeros_like(small)
    lower_v[...] = causal_ones(True)
    upper_v[...] = causal_ones(False)
    marks_v[0:LANES, :] = head_marks(head_width, inner)
    marks_v[LANES:, :] = head_marks(head_width, inner)
    marks_t_v[0:inner, :] = head_marks_t(head_width, inner)
    marks_t_v[inner:, :] = head_marks_t(head_width, inner)
    masks = (lower_v, upper_v, marks_v, marks_t_v)
    pl.semaphore_wait(barrier, len(greet))
    for copy in loads_w:
        copy.wait()

    @pl.loop(0, sequences)
    def _(s):
        first_n = s * cycle
        ext[0:8, :] = jnp.zeros((8, conv), F32)
        state_v[...] = jnp.zeros_like(state_v)

        @pl.loop(0, per)
        def _(f):
            n = first_n + f
            next_block(n)
            free_stage(n)
            slot = lax.rem(n, 2)
            forward_step(
                f,
                xbuf.at[slot],
                cbuf.at[slot],
                w_v,
                ws_v,
                pv,
                masks,
                saved,
                state_v,
                ext,
                stage,
                stat_own.at[s, f],
                sizes,
            )

            keep_piece(n)

            @pl.when(f == per - 1)
            def _():
                for k in range(1, tp):
                    stat_copy(s, k).start()

            pump(ticks * s + 1 + f)

        for k in range(1, tp):
            stat_copy(s, k).wait()
        pump(ticks * s + per + 1)
        ext[SPAN:, :] = jnp.zeros((8, conv), F32)
        dst_v[...] = jnp.zeros_like(dst_v)
        totals[s] = (stat_own[s] + stat_in[s, 0]) + (stat_in[s, 1] + stat_in[s, 2])

        @pl.loop(0, per)
        def _(j):
            n = first_n + per + j
            f = per - 1 - j
            b = per * s + f
            tick = ticks * s + per + 1 + 2 * j
            next_block(n)
            free_stage(n)

            @pl.when(b != per - 1)
            def _():
                for copy in puts(b, (0, 1, 3)):
                    copy.wait()

            slot = lax.rem(n, 2)
            backward_step(
                f,
                xbuf.at[slot],
                cbuf.at[slot],
                w_v,
                ws_v,
                pv,
                masks,
                totals[s, f],
                saved,
                dst_v,
                ext,
                small,
                grads,
                lowered_v,
                turned,
                puts(b, range(4)),
                lambda: pump(tick + 1),
                stage,
                sizes,
                norm_width,
            )
            keep_piece(n)
            pump(tick + 2)

    groups = ((0, 1024), (1024, wide - 1024), (wide, inner))
    if wide <= 1024:
        groups = ((0, wide), (wide, inner))

    def to_sibling(q, g):
        at = pl.multiple_of((2 * q + 1 - parity) * rows, 16)
        columns = pl.ds(*groups[g])
        return pltpu.make_async_remote_copy(
            src_ref=wgrad.at[pl.ds(at, rows), columns],
            dst_ref=rs1.at[q, :, columns],
            send_sem=rs1_send.at[q, g],
            recv_sem=rs1_recv.at[q, g],
            device_id=(sibling, z),
            device_id_type=MESH,
        )

    def to_owner(k, g):
        q = lax.rem(chip + k, half)
        at = pl.multiple_of((2 * q + parity) * rows, 16)
        columns = pl.ds(*groups[g])
        return pltpu.make_async_remote_copy(
            src_ref=wgrad.at[pl.ds(at, rows), columns],
            dst_ref=rs2.at[chip, :, columns],
            send_sem=rs2_send.at[k, g],
            recv_sem=rs2_recv.at[k, g],
            device_id=(2 * q + parity, z),
            device_id_type=MESH,
        )

    def start_group(g):
        @pl.loop(1, half + 1)
        def _(k):
            to_sibling(lax.rem(chip + k, half), g).start()

    def pass_group(g):
        columns = pl.ds(*groups[g])

        @pl.loop(1, half)
        def _(k):
            q = lax.rem(chip + k, half)
            to_sibling(q, g).wait_recv()
            at = pl.multiple_of((2 * q + parity) * rows, 16)
            block = wgrad[pl.ds(at, rows), columns].astype(F32) + fetch(rs1.at[q], g)
            wgrad[pl.ds(at, rows), columns] = block.astype(BF16)
            to_owner(k, g).start()

        to_sibling(chip, g).wait_recv()
        at = pl.multiple_of(me * rows, 16)
        own[:, columns] = wgrad[pl.ds(at, rows), columns].astype(F32) + fetch(rs1.at[chip], g)

    def small_copy(source, target, index, device):
        return pltpu.make_async_remote_copy(
            src_ref=source,
            dst_ref=target,
            send_sem=sm_send.at[index],
            recv_sem=sm_recv.at[index],
            device_id=device,
            device_id_type=MESH,
        )

    def fetch(source, g):
        columns = pl.ds(*groups[g])
        copy = pltpu.make_async_copy(source.at[:, columns], rsv.at[:, columns], rs_sem.at[0])
        copy.start()
        copy.wait()
        return rsv[:, columns].astype(F32)

    def left_operand(source):
        return [
            pltpu.make_async_copy(source.at[b], w_v.at[:, pl.ds(b * SPAN, SPAN)], tile_sem.at[2 + b])
            for b in range(blocks)
        ]

    def tile_load(source, at, size, slot):
        return pltpu.make_async_copy(
            source.at[:, :, pl.ds(at, size)], tiles.at[slot, :, :, pl.ds(0, size)], tile_sem.at[slot]
        )

    def products(source, first, count, place):
        tile_load(source, first * 256, 256, 0).start()

        @pl.loop(0, count)
        def _(t):
            slot = lax.rem(t, 2)
            at = pl.multiple_of((first + t) * 256, 256)
            tile_load(source, at, 256, slot).wait()

            @pl.when(t + 1 < count)
            def _():
                tile_load(source, pl.multiple_of(at + 256, 256), 256, 1 - slot).start()

            right = tiles[slot].reshape(tokens, 256)
            wgrad[:, pl.ds(pl.multiple_of(place + at, 128), 256)] = mm(
                w_v[:, 0:tokens], right
            ).astype(BF16)

    for copy in puts(per * (sequences - 1), (0, 1, 3)):
        copy.wait()
    last_tick = ticks * sequences
    count = lambda tick: max(2 * tick - 2, 0) // 5
    done_finish, done_combine = count(last_tick - 3), count(last_tick)

    @pl.when(is_middle)
    def _():
        store_piece(pieces - 1).wait()

    for copy in left_operand(normed_hbm):
        copy.start()
    for copy in left_operand(normed_hbm):
        copy.wait()
    whole, rest = wide // 256, wide % 256
    if len(groups) == 3:
        products(grads_hbm, 0, 4, 0)
        start_group(0)
        products(grads_hbm, 4, whole - 4, 0)
    else:
        products(grads_hbm, 0, whole, 0)
    last = tile_load(grads_hbm, wide - rest, rest, 0)
    last.start()
    last.wait()
    wgrad[:, wide - rest : wide] = mm(
        w_v[:, 0:tokens], tiles[0].reshape(tokens, 256)[:, 0:rest]
    ).astype(BF16)
    start_group(len(groups) - 2)
    for copy in left_operand(branch_hbm):
        copy.start()

    steps, behind = [], done_finish
    for n in range(done_combine, pieces):
        while behind <= n - 2:
            steps.append((finish, behind))
            behind += 1
        steps.append((combine, n))
    steps += [(finish, n) for n in range(behind, pieces)]

    def drain(upto):
        count = steps.index((combine, upto)) + 1 if upto < pieces else len(steps)

        @pl.when(is_middle)
        def _():
            for step, n in steps[:count]:
                step(n, n >= pieces - 2)

        del steps[:count]

    drain(done_combine)
    if len(groups) == 3:
        pass_group(0)
    for copy in left_operand(branch_hbm):
        copy.wait()
    products(lowered_hbm, 0, inner // 256, wide)
    start_group(len(groups) - 1)
    first_small = small_copy(small, small1, 0, (sibling, z))
    first_small.start()
    drain(done_combine + 1)
    pass_group(len(groups) - 2)
    first_small.wait()
    small2[chip] = small[...] + small1[...]
    second_small = [
        small_copy(
            small2.at[chip], small2.at[chip], k, (2 * lax.rem(chip + k, half) + parity, z)
        )
        for k in range(1, half)
    ]
    for copy in second_small:
        copy.start()

    pass_group(len(groups) - 1)
    drain(done_combine + 2)
    for copy in second_small:
        copy.wait()
    total = small2[0]
    for q in range(1, half):
        total = total + small2[q]
    small3[z] = total
    third_small = [
        small_copy(small3.at[z], small3.at[z], half + k, (me, flipped(z, k)))
        for k in range(1, tp)
    ]
    for copy in third_small:
        copy.start()
    if done_combine + 2 < pieces - 3:
        drain(pieces - 3)

    @pl.loop(1, half)
    def _(k):
        for g in range(len(groups)):
            to_owner(k, g).wait_recv()
            own[:, pl.ds(*groups[g])] += fetch(rs2.at[lax.rem(chip + half - k, half)], g)

    share = state_sum.shape[0]
    state_columns = pl.ds(2 * inner, conv - inner)

    def state_rows(device):
        return pl.ds(pl.multiple_of(device * share, 8), share)

    state_copies = [] if share * tp != rows else [
        pltpu.make_async_remote_copy(
            src_ref=own.at[state_rows(flipped(z, k)), state_columns],
            dst_ref=state_in.at[k - 1],
            send_sem=st_send.at[k - 1],
            recv_sem=st_recv.at[k - 1],
            device_id=(me, flipped(z, k)),
            device_id_type=MESH,
        )
        for k in range(1, tp)
    ]
    for copy in state_copies:
        copy.start()
    drain(pieces - 1)
    for copy in third_small:
        copy.wait()
    vectors[...] = jnp.zeros_like(vectors)
    both = conv - inner
    shared = small3[0, 2:7, inner:conv]
    before = small3[0, 0:1, :]
    for k in range(1, tp):
        shared = shared + small3[k, 2:7, inner:conv]
        before = before + small3[k, 0:1, :]
    for k in range(tp):
        vectors[0:5, k * inner : (k + 1) * inner] = small3[k, 2:7, 0:inner]
        vectors[5:6, depth + k * inner : depth + (k + 1) * inner] = small3[k, 1:2, 0:inner]
        head_sums[k, 0:1, :] = small3[k, 7:8, 0:LANES]
        head_sums[k, 1:2, :] = small3[k, 7:8, LANES : 2 * LANES]
        skips = gather_heads(
            jnp.broadcast_to(small3[k, 1:2, inner : 2 * inner], (8, inner)), marks_t_v[...]
        )
        head_sums[k, 2:8, :] = skips[2:8, :]
    vectors[0:5, tp * inner : tp * inner + both] = shared
    vectors[5:6, 0:depth] = before

    for copy in state_copies:
        copy.wait()
    if state_copies:
        state_sum[...] = own[state_rows(z), state_columns] + (
            state_in[0] + (state_in[1] + state_in[2])
        )
    else:
        state_sum[...] = jnp.zeros_like(state_sum)
    drain(pieces)

    @pl.loop(0, half)
    def _(q):
        for g in range(len(groups)):
            to_sibling(q, g).wait_send()

    @pl.loop(1, half)
    def _(k):
        for g in range(len(groups)):
            to_owner(k, g).wait_send()

    @pl.when(is_middle)
    def _():
        for n in (pieces - 2, pieces - 1):
            for h in range(PARTS):
                across_copy(n, h).wait_send()
                outward(n, h).wait_send()
                kept(n, h).wait()

    @pl.when(is_end)
    def _():
        @pl.loop(0, pieces)
        def _(n):
            for h in range(PARTS):
                inward(n, h).wait_send()
                outward(n, h).wait_recv()


def finalize(x_ref, c_ref, out_ref, in_ref, totals_ref, block_ref, grad_ref, *, norm_width):
    sums = jnp.transpose(jnp.concatenate([totals_ref[0, 0]] * (LANES // 8), 0))
    scale = lax.rsqrt(sums[:, 0:1] / norm_width + NORM_EPSILON)
    shape = x_ref.shape
    branch = out_ref[0].reshape(shape).astype(F32)
    block_ref[...] = (x_ref[...].astype(F32) + scale * branch).astype(BF16)
    grad_ref[...] = in_ref[0].reshape(shape).astype(F32) + c_ref[...].astype(F32)


def run_finalize(x, c, sums, totals, norm_width):
    tokens, depth = x.shape
    blocks = tokens // SPAN
    per = LENGTH // SPAN
    rows = pl.BlockSpec((SPAN, depth), lambda b: (b, 0))
    return pl.pallas_call(
        functools.partial(finalize, norm_width=norm_width),
        grid=(blocks,),
        in_specs=[
            rows,
            rows,
            pl.BlockSpec((1, PARTS, PART, depth), lambda b: (b, 0, 0, 0)),
            pl.BlockSpec((1, PARTS, PART, depth), lambda b: (blocks + b, 0, 0, 0)),
            pl.BlockSpec((1, 1, 8, SPAN), lambda b: (b // per, b % per, 0, 0)),
        ],
        out_specs=(rows, rows),
        out_shape=(sds((tokens, depth), BF16), sds((tokens, depth), F32)),
        compiler_params=pltpu.CompilerParams(vmem_limit_bytes=60 * 1024 * 1024),
        cost_estimate=pl.CostEstimate(
            flops=6 * tokens * depth, bytes_accessed=14 * tokens * depth, transcendentals=0
        ),
        name="finalize",
    )(x, c, sums, sums, totals)


def run_mixer(x, c, w, ws, pv, dp, tp, sizes, norm_width):
    inner, head_width, heads = sizes
    tokens, depth = x.shape
    conv_states = ws.shape[1]
    conv = inner + conv_states
    states = conv_states // 2
    wide = inner + conv + LANES
    width = w.shape[1]
    blocks = tokens // SPAN
    per = LENGTH // SPAN
    sequences = blocks // per
    pieces = 2 * blocks
    half = dp // 2
    rows = depth // dp
    hbm = pl.BlockSpec(memory_space=pl.ANY)
    vmem = pl.BlockSpec(memory_space=pltpu.VMEM)
    dma = pltpu.SemaphoreType.DMA
    piece = (PARTS, PART, depth)
    rows_of_x = (SPAN, depth)
    share = rows // tp if rows % (8 * tp) == 0 else 8
    flops = tokens * (6 * depth * (2 * inner + conv) + 6 * depth * inner + 80 * heads * SPAN * 64)
    return pl.pallas_call(
        functools.partial(mixer, dp=dp, tp=tp, sizes=sizes, norm_width=norm_width),
        in_specs=[hbm] * 4 + [vmem],
        out_specs=(hbm,) * 9 + (vmem,) * 5,
        out_shape=(
            sds((pieces,) + piece, BF16),
            sds((pieces,) + piece, BF16),
            sds((pieces,) + piece, BF16),
            sds((half, rows, wide + inner), BF16),
            sds((half, rows, wide + inner), BF16),
            sds((blocks, SPAN, wide), BF16),
            sds((blocks, SPAN, inner), BF16),
            sds((blocks, depth, SPAN), BF16),
            sds((blocks, depth, SPAN), BF16),
            sds((rows, wide + inner), F32),
            sds((share, conv_states), F32),
            sds((8, tp * inner + depth), F32),
            sds((tp, 8, LANES), F32),
            sds((sequences, per, 8, SPAN), F32),
        ),
        scratch_shapes=[
            pltpu.VMEM((depth, width), BF16),
            pltpu.VMEM((depth, conv_states), BF16),
            pltpu.VMEM((2,) + rows_of_x, BF16),
            pltpu.VMEM((2,) + rows_of_x, BF16),
            pltpu.VMEM((per, SPAN, conv), BF16),
            pltpu.VMEM((per, SPAN, conv), BF16),
            pltpu.VMEM((per, SPAN, inner), BF16),
            pltpu.VMEM((per, SPAN, inner), F32),
            pltpu.VMEM((per, SPAN, LANES), F32),
            pltpu.VMEM((per, states, inner), BF16),
            pltpu.VMEM((states, inner), F32),
            pltpu.VMEM((states, inner), F32),
            pltpu.VMEM((SPAN + 8, conv), F32),
            pltpu.VMEM((depth, wide + inner), BF16),
            pltpu.VMEM((2, blocks, SPAN, 256), BF16),
            pltpu.VMEM((8, depth), F32),
            pltpu.VMEM((SPAN, wide), BF16),
            pltpu.VMEM((SPAN, inner), BF16),
            pltpu.VMEM((depth, SPAN), BF16),
            pltpu.VMEM(piece, BF16),
            pltpu.VMEM(piece, BF16),
            pltpu.VMEM(piece, BF16),
            pltpu.VMEM(piece, BF16),
            pltpu.VMEM((2,) + piece, BF16),
            pltpu.VMEM((2,) + piece, BF16),
            pltpu.VMEM((rows, wide + inner), BF16),
            pltpu.VMEM((sequences, per, 8, SPAN), F32),
            pltpu.VMEM((sequences, tp - 1, per, 8, SPAN), F32),
            pltpu.VMEM((8, depth), F32),
            pltpu.VMEM((half, 8, depth), F32),
            pltpu.VMEM((tp, 8, depth), F32),
            pltpu.VMEM((tp - 1, share, conv_states), F32),
            pltpu.VMEM((SPAN, SPAN), BF16),
            pltpu.VMEM((SPAN, SPAN), BF16),
            pltpu.VMEM((2 * LANES, inner), BF16),
            pltpu.VMEM((2 * inner, LANES), BF16),
            dma((2,)),
            dma((2, 2)),
            dma((pieces, PARTS)),
            dma((pieces, PARTS)),
            dma((pieces, PARTS)),
            dma((pieces, PARTS)),
            dma((pieces, PARTS)),
            dma((1,)),
            dma((3, PARTS)),
            dma((sequences, tp - 1)),
            dma((sequences, tp - 1)),
            dma((half, 3)),
            dma((half, 3)),
            dma((half, 3)),
            dma((half, 3)),
            dma((1,)),
            dma((4,)),
            dma((2 + blocks,)),
            dma((half + tp,)),
            dma((half + tp,)),
            dma((tp - 1,)),
            dma((tp - 1,)),
        ],
        compiler_params=pltpu.CompilerParams(
            collective_id=2, has_side_effects=True, vmem_limit_bytes=MIXER_VMEM
        ),
        cost_estimate=pl.CostEstimate(flops=flops, bytes_accessed=60_000_000, transcendentals=0),
        name="mixer",
    )(x, c, w, ws, pv)


def adamw_update(weight, gradient, moment, square, step_rate, decay_rate):
    moment = FIRST_DECAY * moment + (1.0 - FIRST_DECAY) * gradient
    square = SECOND_DECAY * square + (1.0 - SECOND_DECAY) * gradient * gradient
    first_fix = 1.0 - FIRST_DECAY**STEP
    second_fix = 1.0 - SECOND_DECAY**STEP
    update = moment / first_fix / (jnp.sqrt(square / second_fix) + ADAM_EPSILON)
    return (weight - step_rate * (update + decay_rate * weight), moment, square)


def swap(values, mask, tp):
    return lax.ppermute(values, "tensor", [(i, i ^ mask) for i in range(tp)])


def pad_to(values, size):
    return jnp.pad(values, [(0, 0)] * (values.ndim - 1) + [(0, size - values.shape[-1])])


def shards(
    dp,
    tp,
    activations,
    cotangent,
    in_weight,
    in_first,
    in_second,
    step_weight,
    step_first,
    step_second,
    out_weight,
    out_first,
    out_second,
    state_weight,
    state_first,
    state_second,
    conv_weight,
    conv_first,
    conv_second,
    conv_bias,
    bias_first,
    bias_second,
    gain_vector,
    gains_first,
    gains_second,
    head_params,
    head_first,
    head_second,
):
    dp_rank = lax.axis_index("dp")
    rank = lax.axis_index("tensor")
    tokens, depth = activations.shape
    shard_rows, _, inner = in_weight.shape
    norm_width = inner * tp
    heads = step_weight.shape[1]
    head_width = inner // heads
    state_rows, conv_states = state_weight.shape
    conv = inner + conv_states
    taps, conv_own = conv_weight.shape
    gains_own = gain_vector.shape[0]
    sizes = (inner, head_width, heads)

    w_own = jnp.concatenate(
        [
            in_weight.reshape(shard_rows, 2 * inner).astype(BF16),
            pad_to(step_weight.astype(BF16), LANES),
            out_weight.astype(BF16).T,
        ],
        1,
    )
    padded_rows = -(-state_rows // 16) * 16
    st_own = jnp.pad(state_weight.astype(BF16), ((0, padded_rows - state_rows), (0, 0)))
    flat = jnp.concatenate([conv_weight.reshape(-1), conv_bias, gain_vector])
    sm_own = pad_to(flat, -(-flat.shape[0] // 1024) * 1024).reshape(-1, LANES)
    w, st_full, sm_full = run_gather(w_own, st_own, sm_own, dp, tp)
    ws = st_full[:, :, :state_rows].swapaxes(0, 1).reshape(depth, conv_states)
    small = sm_full.swapaxes(0, 1).reshape(dp * tp, -1)
    kernel_full = (
        small[:, : taps * conv_own].reshape(-1, taps, conv_own).transpose(1, 0, 2).reshape(taps, -1)
    )
    offsets_full = small[:, taps * conv_own : (taps + 1) * conv_own].reshape(-1)
    gains_full = small[:, (taps + 1) * conv_own : (taps + 1) * conv_own + gains_own].reshape(-1)
    start = rank * inner
    conv_rows = jnp.concatenate([kernel_full, offsets_full[None, :]], 0)
    conv_local = jnp.concatenate(
        [lax.dynamic_slice_in_dim(conv_rows, start, inner, 1), conv_rows[:, norm_width:]], 1
    )
    head_local = lax.dynamic_slice_in_dim(head_params, rank * heads, heads, 1)
    gain_local = lax.dynamic_slice_in_dim(gains_full, depth + start, inner, 0)
    pv = jnp.concatenate(
        [
            gains_full[None, :depth],
            pad_to(jnp.concatenate([gain_local, jnp.repeat(head_local[2], head_width)]), depth)[
                None, :
            ],
            pad_to(conv_local, depth),
            pad_to(
                jnp.concatenate(
                    [pad_to(-jnp.exp(head_local[0]), LANES), pad_to(head_local[1], LANES)]
                ),
                depth,
            )[None, :],
        ],
        0,
    )

    sums, _, _, _, _, _, _, _, _, own, state_sum, vectors, head_sums, totals = run_mixer(
        activations, cotangent, w, ws, pv, dp, tp, sizes, norm_width
    )
    block_output, input_grad = run_finalize(activations, cotangent, sums, totals, norm_width)

    in_owned = own[:, : 2 * inner].reshape(shard_rows, 2, inner)
    state_part = own[:, 2 * inner : inner + conv]
    step_owned = own[:, inner + conv : inner + conv + heads].T
    out_owned = own[:, inner + conv + LANES :].T
    if state_sum.shape[0] == state_rows:
        state_owned = state_sum
    else:
        state_owned = lax.dynamic_slice_in_dim(state_part, rank * state_rows, state_rows, 0)
        for k in range(1, tp):
            theirs = lax.dynamic_slice_in_dim(state_part, (rank ^ k) * state_rows, state_rows, 0)
            state_owned = state_owned + swap(theirs, k, tp)
    head_grad = head_sums[:, :3, :heads].transpose(1, 0, 2).reshape(3, tp * heads)
    device = dp_rank * tp + rank
    conv_owned = lax.dynamic_slice(vectors, (0, device * conv_own), (taps + 1, conv_own))
    gains_owned = lax.dynamic_slice(vectors, (taps + 1, device * gains_own), (1, gains_own))[0]

    in_new = adamw_update(in_weight, in_owned, in_first, in_second, RATE_MATRIX, WEIGHT_DECAY)
    step_new = adamw_update(
        step_weight.T, step_owned, step_first.T, step_second.T, RATE_MATRIX, WEIGHT_DECAY
    )
    step_new = tuple(value.T for value in step_new)
    out_new = adamw_update(out_weight, out_owned, out_first, out_second, RATE_OUTPUT, WEIGHT_DECAY)
    state_new = adamw_update(
        state_weight, state_owned, state_first, state_second, RATE_MATRIX, WEIGHT_DECAY
    )
    conv_new = adamw_update(conv_weight, conv_owned[:taps], conv_first, conv_second, RATE_CONV, 0.0)
    bias_new = adamw_update(conv_bias, conv_owned[taps], bias_first, bias_second, RATE_VECTOR, 0.0)
    gains_new = adamw_update(gain_vector, gains_owned, gains_first, gains_second, RATE_VECTOR, 0.0)
    head_new = adamw_update(head_params, head_grad, head_first, head_second, RATE_HEADS, 0.0)
    return (
        (block_output, input_grad)
        + in_new
        + step_new
        + out_new
        + state_new
        + conv_new
        + bias_new
        + gains_new
        + head_new
    )


def solution(mesh):
    both = ("dp", "tensor")
    rows = P("dp", None)
    projection = P("dp", None, "tensor")
    step = P("dp", "tensor")
    out = P("tensor", "dp")
    state = P(both, None)
    taps = P(None, both)
    vector = P(both)
    parameters = sum(
        ((spec,) * 3 for spec in (projection, step, out, state, taps, vector, vector, P())), ()
    )
    return jax.shard_map(
        functools.partial(shards, mesh.shape["dp"], mesh.shape["tensor"]),
        mesh=mesh,
        in_specs=(rows, rows) + parameters,
        out_specs=(rows, rows) + parameters,
        check_vma=False,
    )
```

```python
import functools

import jax
import jax.numpy as jnp
from jax import lax
from jax.experimental import pallas as pl
from jax.experimental.pallas import tpu as pltpu
from jax.sharding import PartitionSpec as P

F32 = jnp.float32
BF16 = jnp.bfloat16
MESH = pl.DeviceIdType.MESH

SPAN = 256
LENGTH = 1024
STEP = 5
LANES = 128
LOG2E = 1.4426950408889634
NORM_EPSILON = 1e-05
FIRST_DECAY = 0.9
SECOND_DECAY = 0.95
ADAM_EPSILON = 1e-08
WEIGHT_DECAY = 0.1
RATE_MATRIX = 0.05
RATE_OUTPUT = 0.04
RATE_CONV = 1.0
RATE_VECTOR = 0.5
RATE_HEADS = 2.0
MIXER_VMEM = 63 * 1024 * 1024


def mm(a, b):
    return lax.dot_general(a, b, (((1,), (0,)), ((), ())), preferred_element_type=F32)


def mm_nt(a, b):
    return lax.dot_general(a, b, (((1,), (1,)), ((), ())), preferred_element_type=F32)


def mm_ones(ones, v):
    high, low = split_low(v)
    rest = (v - high.astype(F32) - low.astype(F32)).astype(BF16)
    parts = mm(ones, jnp.concatenate([high, low, rest], 1))
    width = v.shape[1]
    return parts[:, 0:width] + parts[:, width : 2 * width] + parts[:, 2 * width :]


def sigmoid(v):
    return 0.5 * jnp.tanh(0.5 * v) + 0.5


def softplus(v):
    return jnp.maximum(v, 0.0) + jnp.log1p(jnp.exp(-jnp.abs(v)))


def split_low(v):
    high = v.astype(BF16)
    return high, (v - high.astype(F32)).astype(BF16)


def head_marks(head_width, channels):
    head = lax.broadcasted_iota(jnp.int32, (LANES, channels), 0)
    channel = lax.broadcasted_iota(jnp.int32, (LANES, channels), 1)
    inside = (channel >= head * head_width) & (channel < (head + 1) * head_width)
    return inside.astype(F32).astype(BF16)


def head_marks_t(head_width, channels):
    head = lax.broadcasted_iota(jnp.int32, (channels, LANES), 1)
    channel = lax.broadcasted_iota(jnp.int32, (channels, LANES), 0)
    inside = (channel >= head * head_width) & (channel < (head + 1) * head_width)
    return inside.astype(F32).astype(BF16)


def spread(v, marks2):
    high, low = split_low(v)
    return mm(jnp.concatenate([high, low], 1), marks2)


def gather_heads(v, marks_t2):
    high, low = split_low(v)
    return mm(jnp.concatenate([high, low], 1), marks_t2)


def causal_ones(lower):
    row = lax.broadcasted_iota(jnp.int32, (SPAN, SPAN), 0)
    col = lax.broadcasted_iota(jnp.int32, (SPAN, SPAN), 1)
    keep = row >= col if lower else row <= col
    return keep.astype(F32).astype(BF16)


def lane_masks():
    lane = lax.broadcasted_iota(jnp.int32, (1, LANES), 1)
    first = (lane < LANES // 2).astype(F32)
    return first, 1.0 - first


def sds(shape, dtype):
    return jax.ShapeDtypeStruct(shape, dtype)


def axis_bits(size):
    count = size.bit_length() - 1
    order = list(range(1, count)) + [0]
    other = [order[1], order[0]] + order[2:] if count >= 3 else order
    return order, other


def flipped(index, mask):
    result = index
    bit = 1
    while bit <= mask:
        if mask & bit:
            result = result + bit * (1 - 2 * ((index // bit) % 2))
        bit *= 2
    return result


def gather_weights(
    w_own, st_own, sm_own, w_full, st_full, sm_full,
    local_sem, dp_send, dp_recv, z_send, z_recv, send_sem, recv_sem,
    *, dp, tp, cut
):
    me = lax.axis_index("dp")
    tensor = lax.axis_index("tensor")
    rows, width = w_own.shape
    count = dp.bit_length() - 1

    barrier = pltpu.get_barrier_semaphore()
    for k in range(1, dp):
        pl.semaphore_signal(
            barrier, inc=1, device_id=(flipped(me, k), tensor), device_id_type=MESH
        )
    for k in range(1, tp):
        pl.semaphore_signal(barrier, inc=1, device_id=(me, flipped(tensor, k)), device_id_type=MESH)
    pl.semaphore_wait(barrier, dp + tp - 2)

    orders = axis_bits(dp)
    parts = ((0, cut), (cut, rows - cut))

    def row_of(mask):
        return pl.multiple_of(flipped(me, mask) * rows, 16)

    def full_mask(bits, packed):
        return sum(1 << bits[j] for j in range(count) if packed >> j & 1)

    def move(kind, packed, j):
        bits, (offset, size) = orders[kind], parts[kind]
        mask = full_mask(bits, packed)
        slot = packed | (1 << j)
        place = w_full.at[pl.ds(pl.multiple_of(row_of(mask) + offset, 16), size)]
        return pltpu.make_async_remote_copy(
            src_ref=w_own.at[pl.ds(offset, size)] if mask == 0 else place,
            dst_ref=place,
            send_sem=send_sem.at[kind, slot],
            recv_sem=recv_sem.at[kind, slot],
            device_id=(flipped(me, 1 << bits[j]), tensor),
            device_id_type=MESH,
        )

    smalls = ((st_own, st_full), (sm_own, sm_full))
    direct = [
        pltpu.make_async_remote_copy(
            src_ref=own,
            dst_ref=full.at[tensor, me],
            send_sem=dp_send.at[which, k],
            recv_sem=dp_recv.at[which, k],
            device_id=(flipped(me, k), tensor),
            device_id_type=MESH,
        )
        for k in range(1, dp)
        for which, (own, full) in enumerate(smalls)
    ]
    started = []

    def start(kind, packed, j):
        copy = move(kind, packed, j)
        copy.start()
        started.append(copy)

    kept = [
        pltpu.make_async_copy(own, full.at[tensor, me], local_sem.at[which])
        for which, (own, full) in enumerate(smalls)
    ]
    kept.append(pltpu.make_async_copy(w_own, w_full.at[pl.ds(row_of(0), rows)], local_sem.at[2]))
    for copy in direct:
        copy.start()
    for j in range(count):
        for kind in (0, 1):
            start(kind, 0, j)
    for copy in kept:
        copy.start()
    for copy in kept + direct:
        copy.wait()
    along = [
        pltpu.make_async_remote_copy(
            src_ref=full.at[tensor],
            dst_ref=full.at[tensor],
            send_sem=z_send.at[which, k],
            recv_sem=z_recv.at[which, k],
            device_id=(me, flipped(tensor, k)),
            device_id_type=MESH,
        )
        for k in range(1, tp)
        for which, (own, full) in enumerate(smalls)
    ]
    for copy in along:
        copy.start()
    for packed in range(1, dp):
        top = packed.bit_length() - 1
        for kind in (0, 1):
            move(kind, packed & ~(1 << top), top).wait_recv()
            for j in range(top + 1, count):
                start(kind, packed, j)
    for copy in along:
        copy.wait()
    for copy in started:
        copy.wait_send()


def run_gather(w_own, st_own, sm_own, dp, tp):
    rows, width = w_own.shape
    cut = rows // 2 // 16 * 16
    hbm = pl.BlockSpec(memory_space=pl.ANY)
    dma = pltpu.SemaphoreType.DMA
    return pl.pallas_call(
        functools.partial(gather_weights, dp=dp, tp=tp, cut=cut),
        in_specs=[hbm] * 3,
        out_specs=(hbm,) * 3,
        out_shape=(
            sds((dp * rows, width), BF16),
            sds((tp, dp) + st_own.shape, BF16),
            sds((tp, dp) + sm_own.shape, F32),
        ),
        scratch_shapes=[
            dma((3,)),
            dma((2, dp)),
            dma((2, dp)),
            dma((2, tp)),
            dma((2, tp)),
            dma((2, dp)),
            dma((2, dp)),
        ],
        compiler_params=pltpu.CompilerParams(collective_id=1, has_side_effects=True),
        name="gather_weights",
    )(w_own, st_own, sm_own)


def add_low(a, b):
    return (a.astype(F32) + b.astype(F32)).astype(BF16)


PARTS = 4
PART = SPAN // PARTS


def forward_step(f, x, c, w_v, ws_v, pv, masks, saved, state_v, ext, stage, stats, sizes):
    inner, head_width, heads = sizes
    lower_v, upper_v, marks_v, marks_t_v = masks
    cin_s, pre_s, gate_s, y_s, sp_s, state_s = saved
    states = ws_v.shape[1] // 2
    conv = inner + 2 * states

    x = x[...].astype(F32)
    inv = lax.rsqrt(jnp.mean(x * x, axis=1, keepdims=True) + NORM_EPSILON)
    normed = (x * inv * pv[0:1, :]).astype(BF16)

    step_in = mm(normed, w_v[:, 2 * inner : 2 * inner + LANES])
    sp_s[f] = step_in
    ext[8:, 0:inner] = mm(normed, w_v[:, inner : 2 * inner])
    ext[8:, inner:conv] = mm(normed, ws_v[...])
    gate = mm(normed, w_v[:, 0:inner]).astype(BF16)
    gate_s[f] = gate
    gate = gate.astype(F32)
    cin_s[f] = ext[8:, :].astype(BF16)
    pre = pv[6:7, 0:conv]
    for tap in range(4):
        pre = pre + pv[2 + tap : 3 + tap, 0:conv] * ext[5 + tap : 5 + tap + SPAN, :]
    ext[0:8, :] = ext[SPAN : SPAN + 8, :]
    pre = pre.astype(BF16)
    pre_s[f] = pre
    pre = pre.astype(F32)
    act = pre * sigmoid(pre)

    rate = pv[7:8, 0:LANES]
    dt = softplus(step_in + pv[7:8, LANES : 2 * LANES])
    total = mm_ones(lower_v[...], dt * rate)
    total2 = total * LOG2E
    total2_t = jnp.transpose(total2)
    marks2 = marks_v[...]
    end = total[SPAN - 1 : SPAN, :]
    xc = act[:, 0:inner]
    bmat = act[:, inner : inner + states].astype(BF16)
    cmat = act[:, inner + states :].astype(BF16)
    xd = (xc * spread(dt, marks2)).astype(BF16)
    weighted = (xd.astype(F32) * spread(jnp.exp(end - total), marks2)).astype(BF16)

    state = state_v[...]
    state_low = state.astype(BF16)
    state_s[f] = state_low
    carried = spread(jnp.exp(total), marks2) * mm(cmat, state_low)
    keep = spread(jnp.broadcast_to(jnp.exp(end), (8, LANES)), marks2)[0:1, :]
    state_v[...] = keep * state + mm(jnp.transpose(bmat), weighted)

    inter = mm_nt(cmat, bmat) * lower_v[...].astype(F32)
    first, second = lane_masks()
    skip = pv[1:2, inner : 2 * inner]
    parts = []
    for pair in range(heads // 2):
        lanes = slice(pair * LANES, (pair + 1) * LANES)
        xp = xd[:, lanes].astype(F32)
        within = None
        for side, mask in ((0, first), (1, second)):
            h = 2 * pair + side
            gap = jnp.minimum(total2[:, h : h + 1] - total2_t[h : h + 1, :], 0.0)
            mixing = (jnp.exp2(gap) * inter).astype(BF16)
            term = mm(mixing, (xp * mask).astype(BF16))
            within = term if within is None else within + term
        parts.append(within)
    y = jnp.concatenate(parts, 1) + carried
    y_s[f] = y
    y = y + skip * xc
    gated = y * gate * sigmoid(gate)
    squares = jnp.sum(gated * gated, axis=1, keepdims=True)
    lowered = (gated * pv[1:2, 0:inner]).astype(BF16)
    out = mm_nt(lowered, w_v[:, 2 * inner + LANES :])
    stage[...] = out.astype(BF16).reshape(stage.shape)
    dots = jnp.sum(c[...].astype(F32) * out, axis=1, keepdims=True)
    lane = lax.broadcasted_iota(jnp.int32, (SPAN, LANES), 1)
    both = jnp.where(lane == 0, squares, jnp.where(lane == 1, dots, 0.0))
    stats[...] = jnp.transpose(both)[0:8, :]


def backward_step(
    f, x, c, w_v, ws_v, pv, masks, totals, saved, dst_v, dext, small, grads, lowered_v, turned, put, between, stage, sizes, norm_width
):
    inner, head_width, heads = sizes
    lower_v, upper_v, marks_v, marks_t_v = masks
    cin_s, pre_s, gate_s, y_s, sp_s, state_s = saved
    states = ws_v.shape[1] // 2
    conv = inner + 2 * states
    put_grads, put_lowered, put_branch, put_normed = put

    sums = jnp.transpose(jnp.concatenate([totals] * (LANES // 8), 0))
    scale = lax.rsqrt(sums[:, 0:1] / norm_width + NORM_EPSILON)
    bg = (scale * c[...].astype(F32)).astype(BF16)
    squares_grad = (-0.5 / norm_width) * sums[:, 1:2] * scale * scale * scale
    low_grad = mm(bg, w_v[:, 2 * inner + LANES :])

    pre = pre_s[f].astype(F32)
    sig_pre = sigmoid(pre)
    act = pre * sig_pre
    xc = act[:, 0:inner]
    bmat = act[:, inner : inner + states].astype(BF16)
    cmat = act[:, inner + states :].astype(BF16)

    skip = pv[1:2, inner : 2 * inner]
    gate = gate_s[f].astype(F32)
    sig = sigmoid(gate)
    y_scan = y_s[f]
    y = y_scan + skip * xc
    silu_gate = gate * sig
    gated = y * silu_gate
    gain = pv[1:2, 0:inner]
    lowered_v[...] = (gated * gain).astype(BF16)
    put_lowered.start()
    gated_grad = low_grad * gain + 2.0 * gated * squares_grad
    small[1:2, 0:inner] += jnp.sum(low_grad * gated, axis=0, keepdims=True)
    y_grad = gated_grad * silu_gate
    grads[:, 0:inner] = (gated_grad * y * sig * (1.0 + gate * (1.0 - sig))).astype(BF16)
    small[1:2, inner : 2 * inner] += jnp.sum(y_grad * xc, axis=0, keepdims=True)

    turned[...] = jnp.transpose(bg)
    put_branch.start()

    rate = pv[7:8, 0:LANES]
    step_pre = sp_s[f] + pv[7:8, LANES : 2 * LANES]
    dt = softplus(step_pre)
    total = mm_ones(lower_v[...], dt * rate)
    total2 = total * LOG2E
    total2_t = jnp.transpose(total2)
    marks2 = marks_v[...]
    marks_t2 = marks_t_v[...]
    end = total[SPAN - 1 : SPAN, :]
    dt_wide = spread(dt, marks2)
    xd = (xc * dt_wide).astype(BF16)
    xd_wide = xd.astype(F32)
    end_wide = spread(jnp.exp(end - total), marks2)

    yb = y_grad.astype(BF16)
    yb_wide = yb.astype(F32)
    state_low = state_s[f]
    dst = dst_v[...]
    dst_low = dst.astype(BF16)
    carried_grad = (yb_wide * spread(jnp.exp(total), marks2)).astype(BF16)
    c_grad = mm_nt(carried_grad, state_low)
    b_state = mm(bmat, dst_low) * end_wide
    b_grad = mm_nt((xd_wide * end_wide).astype(BF16), dst_low)
    keep = spread(jnp.broadcast_to(jnp.exp(end), (8, LANES)), marks2)[0:1, :]
    end_row = jnp.sum(xd_wide * b_state, axis=0, keepdims=True) + keep * jnp.sum(
        dst * state_low.astype(F32), axis=0, keepdims=True
    )
    dst_v[...] = keep * dst + mm(jnp.transpose(cmat), carried_grad)

    causal = lower_v[...].astype(F32)
    inter = mm_nt(cmat, bmat) * causal
    first, second = lane_masks()
    inter_grad = jnp.zeros((SPAN, SPAN), F32)
    yb_t = jnp.transpose(yb)
    parts = []
    for pair in range(heads // 2):
        lanes = slice(pair * LANES, (pair + 1) * LANES)
        xp = xd[:, lanes]
        yp = yb_wide[:, lanes]
        for side, mask in ((0, first), (1, second)):
            h = 2 * pair + side
            gap = jnp.minimum(total2[:, h : h + 1] - total2_t[h : h + 1, :], 0.0)
            fade = jnp.exp2(gap)
            mixing = (fade * inter).astype(BF16)
            inter_grad = inter_grad + mm_nt((yp * mask).astype(BF16), xp) * fade
            parts.append(mm(yb_t[h * head_width : (h + 1) * head_width, :], mixing))
        if pair == heads // 4:
            between()
    xd_grad = jnp.transpose(jnp.concatenate(parts, 0)) + b_state
    inter_low = (inter_grad * causal).astype(BF16)
    c_grad = c_grad + mm(inter_low, bmat)
    b_grad = b_grad + mm(jnp.transpose(inter_low), cmat)

    rows = gather_heads(yb_wide * y_scan - xd_wide * xd_grad, marks_t2)
    end_sum = gather_heads(jnp.broadcast_to(end_row, (8, inner)), marks_t2)[0:1, :]
    decay_grad = mm_ones(upper_v[...], rows) + end_sum
    dt_grad = decay_grad * rate + gather_heads(xc * xd_grad, marks_t2)
    small[7:8, 0:LANES] += jnp.sum(decay_grad * dt, axis=0, keepdims=True) * rate
    step_grad = dt_grad * sigmoid(step_pre)
    small[7:8, LANES : 2 * LANES] += jnp.sum(step_grad, axis=0, keepdims=True)
    grads[:, conv + inner :] = step_grad.astype(BF16)

    x_grad = xd_grad * dt_wide + skip * y_grad
    act_grad = jnp.concatenate([x_grad, b_grad, c_grad], 1)
    pre = pre_s[f].astype(F32)
    sig_pre = sigmoid(pre)
    pre_grad = act_grad * sig_pre * (1.0 + pre * (1.0 - sig_pre))
    dext[0:SPAN, :] = pre_grad
    small[6:7, 0:conv] += jnp.sum(pre_grad, axis=0, keepdims=True)
    conv_in = cin_s[f].astype(F32)
    conv_grad = None
    for tap in range(4):
        shifted = dext[3 - tap : 3 - tap + SPAN, :]
        term = pv[2 + tap : 3 + tap, 0:conv] * shifted
        conv_grad = term if conv_grad is None else conv_grad + term
        small[2 + tap : 3 + tap, 0:conv] += jnp.sum(conv_in * shifted, axis=0, keepdims=True)
    dext[SPAN:, :] = dext[0:8, :]
    grads[:, inner : inner + conv] = conv_grad.astype(BF16)

    normed_grad = mm_nt(grads[:, 0 : 2 * inner], w_v[:, 0 : 2 * inner])
    normed_grad = normed_grad + mm_nt(grads[:, 2 * inner : inner + conv], ws_v[...])
    normed_grad = normed_grad + mm_nt(
        grads[:, inner + conv :], w_v[:, 2 * inner : 2 * inner + LANES]
    )
    x = x[...].astype(F32)
    inv = lax.rsqrt(jnp.mean(x * x, axis=1, keepdims=True) + NORM_EPSILON)
    scaled_x = x * inv
    small[0:1, :] += jnp.sum(normed_grad * scaled_x, axis=0, keepdims=True)
    scaled = normed_grad * pv[0:1, :]
    inner_mean = jnp.mean(x * scaled, axis=1, keepdims=True)
    part = inv * scaled - x * (inv * inv * inv * inner_mean)
    stage[...] = part.astype(BF16).reshape(stage.shape)

    put_branch.wait()
    turned[...] = jnp.transpose((scaled_x * pv[0:1, :]).astype(BF16))
    put_normed.start()
    put_grads.start()


def mixer(
    x_hbm,
    c_hbm,
    w_hbm,
    ws_hbm,
    pv,
    edge,
    across,
    mine,
    rs1,
    rs2,
    grads_hbm,
    lowered_hbm,
    branch_hbm,
    normed_hbm,
    own,
    state_sum,
    vectors,
    head_sums,
    totals,
    w_v,
    ws_v,
    xbuf,
    cbuf,
    cin_s,
    pre_s,
    gate_s,
    y_s,
    sp_s,
    state_s,
    state_v,
    dst_v,
    ext,
    wgrad,
    tiles,
    small,
    grads,
    lowered_v,
    turned,
    stage,
    edge_v,
    across_v,
    mine_v,
    pair,
    total_v,
    rsv,
    stat_own,
    stat_in,
    small1,
    small2,
    small3,
    state_in,
    lower_v,
    upper_v,
    marks_v,
    marks_t_v,
    w_sem,
    load_sem,
    edge_send,
    edge_recv,
    across_send,
    across_recv,
    keep_sem,
    mine_sem,
    pump_sem,
    stat_send,
    stat_recv,
    rs1_send,
    rs1_recv,
    rs2_send,
    rs2_recv,
    rs_sem,
    put_sem,
    tile_sem,
    sm_send,
    sm_recv,
    st_send,
    st_recv,
    *,
    dp,
    tp,
    sizes,
    norm_width,
):
    me = lax.axis_index("dp")
    z = lax.axis_index("tensor")
    inner, head_width, heads = sizes
    tokens, depth = x_hbm.shape
    blocks = tokens // SPAN
    per = LENGTH // SPAN
    sequences = blocks // per
    cycle = 2 * per
    pieces = 2 * blocks
    half = dp // 2
    rows = depth // dp
    conv = inner + ws_hbm.shape[1]
    wide = inner + conv + LANES
    saved = (cin_s, pre_s, gate_s, y_s, sp_s, state_s)
    parity = lax.rem(me, 2)
    chip = me // 2
    sibling = me + 1 - 2 * parity
    is_middle = (z == 1) | (z == 2)
    is_end = (z == 0) | (z == 3)
    edge_peer = flipped(z, 1)
    across_peer = 3 - z

    barrier = pltpu.get_barrier_semaphore()
    greet = [(sibling, z)]
    greet += [(2 * lax.rem(chip + k, half) + parity, z) for k in range(1, half)]
    greet += [(me, flipped(z, k)) for k in range(1, tp)]
    for device in greet:
        pl.semaphore_signal(barrier, inc=1, device_id=device, device_id_type=MESH)

    loads_w = [
        pltpu.make_async_copy(w_hbm, w_v, w_sem.at[0]),
        pltpu.make_async_copy(ws_hbm, ws_v, w_sem.at[1]),
    ]
    for copy in loads_w:
        copy.start()

    def block_of(n):
        s, r = n // cycle, lax.rem(n, cycle)
        back = r // per
        pos = lax.rem(r, per)
        return per * s + (1 - back) * pos + back * (per - 1 - pos)

    def slot_of(n):
        return blocks * (lax.rem(n, cycle) // per) + block_of(n)

    def loads(n):
        slot = lax.rem(n, 2)
        at = pl.multiple_of(block_of(n) * SPAN, SPAN)
        return [
            pltpu.make_async_copy(x_hbm.at[pl.ds(at, SPAN)], xbuf.at[slot], load_sem.at[0, slot]),
            pltpu.make_async_copy(c_hbm.at[pl.ds(at, SPAN)], cbuf.at[slot], load_sem.at[1, slot]),
        ]

    def next_block(n):
        for copy in loads(n):
            copy.wait()

        @pl.when(n + 1 < pieces)
        def _():
            for copy in loads(n + 1):
                copy.start()

    def edge_copy(n, h, source):
        slot = slot_of(n)
        return pltpu.make_async_remote_copy(
            src_ref=source,
            dst_ref=edge.at[slot, h],
            send_sem=edge_send.at[slot, h],
            recv_sem=edge_recv.at[slot, h],
            device_id=(me, edge_peer),
            device_id_type=MESH,
        )

    def inward(n, h):
        return edge_copy(n, h, mine.at[slot_of(n), h])

    def outward(n, h):
        return edge_copy(n, h, total_v.at[lax.rem(n, 2), h])

    def kept(n, h):
        slot = slot_of(n)
        return pltpu.make_async_copy(total_v.at[lax.rem(n, 2), h], edge.at[slot, h], keep_sem.at[slot, h])

    def across_copy(n, h):
        slot = slot_of(n)
        return pltpu.make_async_remote_copy(
            src_ref=pair.at[lax.rem(n, 2), h],
            dst_ref=across.at[slot, h],
            send_sem=across_send.at[slot, h],
            recv_sem=across_recv.at[slot, h],
            device_id=(me, across_peer),
            device_id_type=MESH,
        )

    def edge_load(n, h):
        return pltpu.make_async_copy(edge.at[slot_of(n), h], edge_v.at[h], pump_sem.at[0, h])

    def across_load(n, h):
        return pltpu.make_async_copy(across.at[slot_of(n), h], across_v.at[h], pump_sem.at[1, h])

    def mine_load(n, h):
        return pltpu.make_async_copy(mine.at[slot_of(n), h], mine_v.at[h], pump_sem.at[2, h])

    def store_piece(n):
        return pltpu.make_async_copy(stage, mine.at[slot_of(n)], mine_sem.at[0])

    def begin_combine(n, h):
        inward(n, h).wait_recv()
        edge_load(n, h).start()
        mine_load(n, h).start()

    def end_combine(n, h):
        @pl.when(n >= 2)
        def _():
            across_copy(n - 2, h).wait_send()

        edge_load(n, h).wait()
        mine_load(n, h).wait()
        pair[lax.rem(n, 2), h] = add_low(mine_v[h], edge_v[h])
        across_copy(n, h).start()

    def begin_finish(n, h):
        across_copy(n, h).wait_recv()
        across_load(n, h).start()

    def end_finish(n, h):
        @pl.when(n >= 2)
        def _():
            outward(n - 2, h).wait_send()
            kept(n - 2, h).wait()

        across_load(n, h).wait()
        slot = lax.rem(n, 2)
        total_v[slot, h] = add_low(pair[slot, h], across_v[h])
        outward(n, h).start()
        kept(n, h).start()

    ticks = 3 * per + 1

    def made(tick):
        s, q = (tick - 1) // ticks, lax.rem(tick - 1, ticks) + 1
        return cycle * s + jnp.minimum(q, per) + jnp.maximum(q - per - 1, 0) // 2

    def combined(tick):
        return jnp.maximum(2 * tick - 2, 0) // 5

    def finished(tick):
        return combined(jnp.maximum(tick - 3, 0))

    def sent(tick):
        paced = jnp.minimum(made(jnp.maximum(tick, 1)), (3 * tick + 4) // 7)
        return jnp.where(tick == ticks * sequences, pieces, jnp.where(tick < 1, 0, paced))

    def pump(tick):
        @pl.when(is_end)
        def _():
            @pl.loop(sent(tick - 1), sent(tick))
            def _(k):
                for h in range(PARTS):
                    inward(k, h).start()

        @pl.when(is_middle & (finished(tick) > finished(tick - 1)))
        def _():
            finish(finished(tick) - 1)

        @pl.when(is_middle & (combined(tick) > combined(tick - 1)))
        def _():
            combine(combined(tick) - 1)

    def combine(n, apart=False):
        for group in zip(range(PARTS)) if apart else (range(PARTS),):
            for h in group:
                begin_combine(n, h)
            for h in group:
                end_combine(n, h)

    def finish(n, apart=False):
        for group in zip(range(PARTS)) if apart else (range(PARTS),):
            for h in group:
                begin_finish(n, h)
            for h in group:
                end_finish(n, h)

    def free_stage(n):
        @pl.when(is_middle & (n >= 1))
        def _():
            store_piece(n - 1).wait()

    def keep_piece(n):
        store_piece(n).start()

        @pl.when(is_end)
        def _():
            store_piece(n).wait()

    def puts(b, which):
        pairs = (
            (grads, grads_hbm),
            (lowered_v, lowered_hbm),
            (turned, branch_hbm),
            (turned, normed_hbm),
        )
        return [
            pltpu.make_async_copy(pairs[k][0], pairs[k][1].at[b], put_sem.at[k]) for k in which
        ]

    def stat_copy(s, k):
        return pltpu.make_async_remote_copy(
            src_ref=stat_own.at[s],
            dst_ref=stat_in.at[s, k - 1],
            send_sem=stat_send.at[s, k - 1],
            recv_sem=stat_recv.at[s, k - 1],
            device_id=(me, flipped(z, k)),
            device_id_type=MESH,
        )

    for copy in loads(0):
        copy.start()
    small[...] = jnp.zeros_like(small)
    lower_v[...] = causal_ones(True)
    upper_v[...] = causal_ones(False)
    marks_v[0:LANES, :] = head_marks(head_width, inner)
    marks_v[LANES:, :] = head_marks(head_width, inner)
    marks_t_v[0:inner, :] = head_marks_t(head_width, inner)
    marks_t_v[inner:, :] = head_marks_t(head_width, inner)
    masks = (lower_v, upper_v, marks_v, marks_t_v)
    pl.semaphore_wait(barrier, len(greet))
    for copy in loads_w:
        copy.wait()

    @pl.loop(0, sequences)
    def _(s):
        first_n = s * cycle
        ext[0:8, :] = jnp.zeros((8, conv), F32)
        state_v[...] = jnp.zeros_like(state_v)

        @pl.loop(0, per)
        def _(f):
            n = first_n + f
            next_block(n)
            free_stage(n)
            slot = lax.rem(n, 2)
            forward_step(
                f,
                xbuf.at[slot],
                cbuf.at[slot],
                w_v,
                ws_v,
                pv,
                masks,
                saved,
                state_v,
                ext,
                stage,
                stat_own.at[s, f],
                sizes,
            )

            keep_piece(n)

            @pl.when(f == per - 1)
            def _():
                for k in range(1, tp):
                    stat_copy(s, k).start()

            pump(ticks * s + 1 + f)

        for k in range(1, tp):
            stat_copy(s, k).wait()
        pump(ticks * s + per + 1)
        ext[SPAN:, :] = jnp.zeros((8, conv), F32)
        dst_v[...] = jnp.zeros_like(dst_v)
        totals[s] = (stat_own[s] + stat_in[s, 0]) + (stat_in[s, 1] + stat_in[s, 2])

        @pl.loop(0, per)
        def _(j):
            n = first_n + per + j
            f = per - 1 - j
            b = per * s + f
            tick = ticks * s + per + 1 + 2 * j
            next_block(n)
            free_stage(n)

            @pl.when(b != per - 1)
            def _():
                for copy in puts(b, (0, 1, 3)):
                    copy.wait()

            slot = lax.rem(n, 2)
            backward_step(
                f,
                xbuf.at[slot],
                cbuf.at[slot],
                w_v,
                ws_v,
                pv,
                masks,
                totals[s, f],
                saved,
                dst_v,
                ext,
                small,
                grads,
                lowered_v,
                turned,
                puts(b, range(4)),
                lambda: pump(tick + 1),
                stage,
                sizes,
                norm_width,
            )
            keep_piece(n)
            pump(tick + 2)

    groups = ((0, 1024), (1024, wide - 1024), (wide, inner))
    if wide <= 1024:
        groups = ((0, wide), (wide, inner))

    def to_sibling(q, g):
        at = pl.multiple_of((2 * q + 1 - parity) * rows, 16)
        columns = pl.ds(*groups[g])
        return pltpu.make_async_remote_copy(
            src_ref=wgrad.at[pl.ds(at, rows), columns],
            dst_ref=rs1.at[q, :, columns],
            send_sem=rs1_send.at[q, g],
            recv_sem=rs1_recv.at[q, g],
            device_id=(sibling, z),
            device_id_type=MESH,
        )

    def to_owner(k, g):
        q = lax.rem(chip + k, half)
        at = pl.multiple_of((2 * q + parity) * rows, 16)
        columns = pl.ds(*groups[g])
        return pltpu.make_async_remote_copy(
            src_ref=wgrad.at[pl.ds(at, rows), columns],
            dst_ref=rs2.at[chip, :, columns],
            send_sem=rs2_send.at[k, g],
            recv_sem=rs2_recv.at[k, g],
            device_id=(2 * q + parity, z),
            device_id_type=MESH,
        )

    def start_group(g):
        @pl.loop(1, half + 1)
        def _(k):
            to_sibling(lax.rem(chip + k, half), g).start()

    def pass_group(g):
        columns = pl.ds(*groups[g])

        @pl.loop(1, half)
        def _(k):
            q = lax.rem(chip + k, half)
            to_sibling(q, g).wait_recv()
            at = pl.multiple_of((2 * q + parity) * rows, 16)
            block = wgrad[pl.ds(at, rows), columns].astype(F32) + fetch(rs1.at[q], g)
            wgrad[pl.ds(at, rows), columns] = block.astype(BF16)
            to_owner(k, g).start()

        to_sibling(chip, g).wait_recv()
        at = pl.multiple_of(me * rows, 16)
        own[:, columns] = wgrad[pl.ds(at, rows), columns].astype(F32) + fetch(rs1.at[chip], g)

    def small_copy(source, target, index, device):
        return pltpu.make_async_remote_copy(
            src_ref=source,
            dst_ref=target,
            send_sem=sm_send.at[index],
            recv_sem=sm_recv.at[index],
            device_id=device,
            device_id_type=MESH,
        )

    def fetch(source, g):
        columns = pl.ds(*groups[g])
        copy = pltpu.make_async_copy(source.at[:, columns], rsv.at[:, columns], rs_sem.at[0])
        copy.start()
        copy.wait()
        return rsv[:, columns].astype(F32)

    def left_operand(source):
        return [
            pltpu.make_async_copy(source.at[b], w_v.at[:, pl.ds(b * SPAN, SPAN)], tile_sem.at[2 + b])
            for b in range(blocks)
        ]

    def tile_load(source, at, size, slot):
        return pltpu.make_async_copy(
            source.at[:, :, pl.ds(at, size)], tiles.at[slot, :, :, pl.ds(0, size)], tile_sem.at[slot]
        )

    def products(source, first, count, place):
        tile_load(source, first * 256, 256, 0).start()

        @pl.loop(0, count)
        def _(t):
            slot = lax.rem(t, 2)
            at = pl.multiple_of((first + t) * 256, 256)
            tile_load(source, at, 256, slot).wait()

            @pl.when(t + 1 < count)
            def _():
                tile_load(source, pl.multiple_of(at + 256, 256), 256, 1 - slot).start()

            right = tiles[slot].reshape(tokens, 256)
            wgrad[:, pl.ds(pl.multiple_of(place + at, 128), 256)] = mm(
                w_v[:, 0:tokens], right
            ).astype(BF16)

    for copy in puts(per * (sequences - 1), (0, 1, 3)):
        copy.wait()
    last_tick = ticks * sequences
    count = lambda tick: max(2 * tick - 2, 0) // 5
    done_finish, done_combine = count(last_tick - 3), count(last_tick)

    @pl.when(is_middle)
    def _():
        store_piece(pieces - 1).wait()

    for copy in left_operand(normed_hbm):
        copy.start()
    for copy in left_operand(normed_hbm):
        copy.wait()
    whole, rest = wide // 256, wide % 256
    if len(groups) == 3:
        products(grads_hbm, 0, 4, 0)
        start_group(0)
        products(grads_hbm, 4, whole - 4, 0)
    else:
        products(grads_hbm, 0, whole, 0)
    last = tile_load(grads_hbm, wide - rest, rest, 0)
    last.start()
    last.wait()
    wgrad[:, wide - rest : wide] = mm(
        w_v[:, 0:tokens], tiles[0].reshape(tokens, 256)[:, 0:rest]
    ).astype(BF16)
    start_group(len(groups) - 2)
    for copy in left_operand(branch_hbm):
        copy.start()

    steps, behind = [], done_finish
    for n in range(done_combine, pieces):
        while behind <= n - 2:
            steps.append((finish, behind))
            behind += 1
        steps.append((combine, n))
    steps += [(finish, n) for n in range(behind, pieces)]

    def drain(upto):
        count = steps.index((combine, upto)) + 1 if upto < pieces else len(steps)

        @pl.when(is_middle)
        def _():
            for step, n in steps[:count]:
                step(n, n >= pieces - 2)

        del steps[:count]

    drain(done_combine)
    if len(groups) == 3:
        pass_group(0)
    for copy in left_operand(branch_hbm):
        copy.wait()
    products(lowered_hbm, 0, inner // 256, wide)
    start_group(len(groups) - 1)
    first_small = small_copy(small, small1, 0, (sibling, z))
    first_small.start()
    drain(done_combine + 1)
    pass_group(len(groups) - 2)
    first_small.wait()
    small2[chip] = small[...] + small1[...]
    second_small = [
        small_copy(
            small2.at[chip], small2.at[chip], k, (2 * lax.rem(chip + k, half) + parity, z)
        )
        for k in range(1, half)
    ]
    for copy in second_small:
        copy.start()

    pass_group(len(groups) - 1)
    drain(done_combine + 2)
    for copy in second_small:
        copy.wait()
    total = small2[0]
    for q in range(1, half):
        total = total + small2[q]
    small3[z] = total
    third_small = [
        small_copy(small3.at[z], small3.at[z], half + k, (me, flipped(z, k)))
        for k in range(1, tp)
    ]
    for copy in third_small:
        copy.start()
    if done_combine + 2 < pieces - 3:
        drain(pieces - 3)

    @pl.loop(1, half)
    def _(k):
        for g in range(len(groups)):
            to_owner(k, g).wait_recv()
            own[:, pl.ds(*groups[g])] += fetch(rs2.at[lax.rem(chip + half - k, half)], g)

    share = state_sum.shape[0]
    state_columns = pl.ds(2 * inner, conv - inner)

    def state_rows(device):
        return pl.ds(pl.multiple_of(device * share, 8), share)

    state_copies = [] if share * tp != rows else [
        pltpu.make_async_remote_copy(
            src_ref=own.at[state_rows(flipped(z, k)), state_columns],
            dst_ref=state_in.at[k - 1],
            send_sem=st_send.at[k - 1],
            recv_sem=st_recv.at[k - 1],
            device_id=(me, flipped(z, k)),
            device_id_type=MESH,
        )
        for k in range(1, tp)
    ]
    for copy in state_copies:
        copy.start()
    drain(pieces - 1)
    for copy in third_small:
        copy.wait()
    vectors[...] = jnp.zeros_like(vectors)
    both = conv - inner
    shared = small3[0, 2:7, inner:conv]
    before = small3[0, 0:1, :]
    for k in range(1, tp):
        shared = shared + small3[k, 2:7, inner:conv]
        before = before + small3[k, 0:1, :]
    for k in range(tp):
        vectors[0:5, k * inner : (k + 1) * inner] = small3[k, 2:7, 0:inner]
        vectors[5:6, depth + k * inner : depth + (k + 1) * inner] = small3[k, 1:2, 0:inner]
        head_sums[k, 0:1, :] = small3[k, 7:8, 0:LANES]
        head_sums[k, 1:2, :] = small3[k, 7:8, LANES : 2 * LANES]
        skips = gather_heads(
            jnp.broadcast_to(small3[k, 1:2, inner : 2 * inner], (8, inner)), marks_t_v[...]
        )
        head_sums[k, 2:8, :] = skips[2:8, :]
    vectors[0:5, tp * inner : tp * inner + both] = shared
    vectors[5:6, 0:depth] = before

    for copy in state_copies:
        copy.wait()
    if state_copies:
        state_sum[...] = own[state_rows(z), state_columns] + (
            state_in[0] + (state_in[1] + state_in[2])
        )
    else:
        state_sum[...] = jnp.zeros_like(state_sum)
    drain(pieces)

    @pl.loop(0, half)
    def _(q):
        for g in range(len(groups)):
            to_sibling(q, g).wait_send()

    @pl.loop(1, half)
    def _(k):
        for g in range(len(groups)):
            to_owner(k, g).wait_send()

    @pl.when(is_middle)
    def _():
        for n in (pieces - 2, pieces - 1):
            for h in range(PARTS):
                across_copy(n, h).wait_send()
                outward(n, h).wait_send()
                kept(n, h).wait()

    @pl.when(is_end)
    def _():
        @pl.loop(0, pieces)
        def _(n):
            for h in range(PARTS):
                inward(n, h).wait_send()
                outward(n, h).wait_recv()


def finalize(x_ref, c_ref, out_ref, in_ref, totals_ref, block_ref, grad_ref, *, norm_width):
    sums = jnp.transpose(jnp.concatenate([totals_ref[0, 0]] * (LANES // 8), 0))
    scale = lax.rsqrt(sums[:, 0:1] / norm_width + NORM_EPSILON)
    shape = x_ref.shape
    branch = out_ref[0].reshape(shape).astype(F32)
    block_ref[...] = (x_ref[...].astype(F32) + scale * branch).astype(BF16)
    grad_ref[...] = in_ref[0].reshape(shape).astype(F32) + c_ref[...].astype(F32)


def run_finalize(x, c, sums, totals, norm_width):
    tokens, depth = x.shape
    blocks = tokens // SPAN
    per = LENGTH // SPAN
    rows = pl.BlockSpec((SPAN, depth), lambda b: (b, 0))
    return pl.pallas_call(
        functools.partial(finalize, norm_width=norm_width),
        grid=(blocks,),
        in_specs=[
            rows,
            rows,
            pl.BlockSpec((1, PARTS, PART, depth), lambda b: (b, 0, 0, 0)),
            pl.BlockSpec((1, PARTS, PART, depth), lambda b: (blocks + b, 0, 0, 0)),
            pl.BlockSpec((1, 1, 8, SPAN), lambda b: (b // per, b % per, 0, 0)),
        ],
        out_specs=(rows, rows),
        out_shape=(sds((tokens, depth), BF16), sds((tokens, depth), F32)),
        compiler_params=pltpu.CompilerParams(vmem_limit_bytes=60 * 1024 * 1024),
        cost_estimate=pl.CostEstimate(
            flops=6 * tokens * depth, bytes_accessed=14 * tokens * depth, transcendentals=0
        ),
        name="finalize",
    )(x, c, sums, sums, totals)


def run_mixer(x, c, w, ws, pv, dp, tp, sizes, norm_width):
    inner, head_width, heads = sizes
    tokens, depth = x.shape
    conv_states = ws.shape[1]
    conv = inner + conv_states
    states = conv_states // 2
    wide = inner + conv + LANES
    width = w.shape[1]
    blocks = tokens // SPAN
    per = LENGTH // SPAN
    sequences = blocks // per
    pieces = 2 * blocks
    half = dp // 2
    rows = depth // dp
    hbm = pl.BlockSpec(memory_space=pl.ANY)
    vmem = pl.BlockSpec(memory_space=pltpu.VMEM)
    dma = pltpu.SemaphoreType.DMA
    piece = (PARTS, PART, depth)
    rows_of_x = (SPAN, depth)
    share = rows // tp if rows % (8 * tp) == 0 else 8
    flops = tokens * (6 * depth * (2 * inner + conv) + 6 * depth * inner + 80 * heads * SPAN * 64)
    return pl.pallas_call(
        functools.partial(mixer, dp=dp, tp=tp, sizes=sizes, norm_width=norm_width),
        in_specs=[hbm] * 4 + [vmem],
        out_specs=(hbm,) * 9 + (vmem,) * 5,
        out_shape=(
            sds((pieces,) + piece, BF16),
            sds((pieces,) + piece, BF16),
            sds((pieces,) + piece, BF16),
            sds((half, rows, wide + inner), BF16),
            sds((half, rows, wide + inner), BF16),
            sds((blocks, SPAN, wide), BF16),
            sds((blocks, SPAN, inner), BF16),
            sds((blocks, depth, SPAN), BF16),
            sds((blocks, depth, SPAN), BF16),
            sds((rows, wide + inner), F32),
            sds((share, conv_states), F32),
            sds((8, tp * inner + depth), F32),
            sds((tp, 8, LANES), F32),
            sds((sequences, per, 8, SPAN), F32),
        ),
        scratch_shapes=[
            pltpu.VMEM((depth, width), BF16),
            pltpu.VMEM((depth, conv_states), BF16),
            pltpu.VMEM((2,) + rows_of_x, BF16),
            pltpu.VMEM((2,) + rows_of_x, BF16),
            pltpu.VMEM((per, SPAN, conv), BF16),
            pltpu.VMEM((per, SPAN, conv), BF16),
            pltpu.VMEM((per, SPAN, inner), BF16),
            pltpu.VMEM((per, SPAN, inner), F32),
            pltpu.VMEM((per, SPAN, LANES), F32),
            pltpu.VMEM((per, states, inner), BF16),
            pltpu.VMEM((states, inner), F32),
            pltpu.VMEM((states, inner), F32),
            pltpu.VMEM((SPAN + 8, conv), F32),
            pltpu.VMEM((depth, wide + inner), BF16),
            pltpu.VMEM((2, blocks, SPAN, 256), BF16),
            pltpu.VMEM((8, depth), F32),
            pltpu.VMEM((SPAN, wide), BF16),
            pltpu.VMEM((SPAN, inner), BF16),
            pltpu.VMEM((depth, SPAN), BF16),
            pltpu.VMEM(piece, BF16),
            pltpu.VMEM(piece, BF16),
            pltpu.VMEM(piece, BF16),
            pltpu.VMEM(piece, BF16),
            pltpu.VMEM((2,) + piece, BF16),
            pltpu.VMEM((2,) + piece, BF16),
            pltpu.VMEM((rows, wide + inner), BF16),
            pltpu.VMEM((sequences, per, 8, SPAN), F32),
            pltpu.VMEM((sequences, tp - 1, per, 8, SPAN), F32),
            pltpu.VMEM((8, depth), F32),
            pltpu.VMEM((half, 8, depth), F32),
            pltpu.VMEM((tp, 8, depth), F32),
            pltpu.VMEM((tp - 1, share, conv_states), F32),
            pltpu.VMEM((SPAN, SPAN), BF16),
            pltpu.VMEM((SPAN, SPAN), BF16),
            pltpu.VMEM((2 * LANES, inner), BF16),
            pltpu.VMEM((2 * inner, LANES), BF16),
            dma((2,)),
            dma((2, 2)),
            dma((pieces, PARTS)),
            dma((pieces, PARTS)),
            dma((pieces, PARTS)),
            dma((pieces, PARTS)),
            dma((pieces, PARTS)),
            dma((1,)),
            dma((3, PARTS)),
            dma((sequences, tp - 1)),
            dma((sequences, tp - 1)),
            dma((half, 3)),
            dma((half, 3)),
            dma((half, 3)),
            dma((half, 3)),
            dma((1,)),
            dma((4,)),
            dma((2 + blocks,)),
            dma((half + tp,)),
            dma((half + tp,)),
            dma((tp - 1,)),
            dma((tp - 1,)),
        ],
        compiler_params=pltpu.CompilerParams(
            collective_id=2, has_side_effects=True, vmem_limit_bytes=MIXER_VMEM
        ),
        cost_estimate=pl.CostEstimate(flops=flops, bytes_accessed=60_000_000, transcendentals=0),
        name="mixer",
    )(x, c, w, ws, pv)


def adamw_update(weight, gradient, moment, square, step_rate, decay_rate):
    moment = FIRST_DECAY * moment + (1.0 - FIRST_DECAY) * gradient
    square = SECOND_DECAY * square + (1.0 - SECOND_DECAY) * gradient * gradient
    first_fix = 1.0 - FIRST_DECAY**STEP
    second_fix = 1.0 - SECOND_DECAY**STEP
    update = moment / first_fix / (jnp.sqrt(square / second_fix) + ADAM_EPSILON)
    return (weight - step_rate * (update + decay_rate * weight), moment, square)


def swap(values, mask, tp):
    return lax.ppermute(values, "tensor", [(i, i ^ mask) for i in range(tp)])


def pad_to(values, size):
    return jnp.pad(values, [(0, 0)] * (values.ndim - 1) + [(0, size - values.shape[-1])])


def shards(
    dp,
    tp,
    activations,
    cotangent,
    in_weight,
    in_first,
    in_second,
    step_weight,
    step_first,
    step_second,
    out_weight,
    out_first,
    out_second,
    state_weight,
    state_first,
    state_second,
    conv_weight,
    conv_first,
    conv_second,
    conv_bias,
    bias_first,
    bias_second,
    gain_vector,
    gains_first,
    gains_second,
    head_params,
    head_first,
    head_second,
):
    dp_rank = lax.axis_index("dp")
    rank = lax.axis_index("tensor")
    tokens, depth = activations.shape
    shard_rows, _, inner = in_weight.shape
    norm_width = inner * tp
    heads = step_weight.shape[1]
    head_width = inner // heads
    state_rows, conv_states = state_weight.shape
    conv = inner + conv_states
    taps, conv_own = conv_weight.shape
    gains_own = gain_vector.shape[0]
    sizes = (inner, head_width, heads)

    w_own = jnp.concatenate(
        [
            in_weight.reshape(shard_rows, 2 * inner).astype(BF16),
            pad_to(step_weight.astype(BF16), LANES),
            out_weight.astype(BF16).T,
        ],
        1,
    )
    padded_rows = -(-state_rows // 16) * 16
    st_own = jnp.pad(state_weight.astype(BF16), ((0, padded_rows - state_rows), (0, 0)))
    flat = jnp.concatenate([conv_weight.reshape(-1), conv_bias, gain_vector])
    sm_own = pad_to(flat, -(-flat.shape[0] // 1024) * 1024).reshape(-1, LANES)
    w, st_full, sm_full = run_gather(w_own, st_own, sm_own, dp, tp)
    ws = st_full[:, :, :state_rows].swapaxes(0, 1).reshape(depth, conv_states)
    small = sm_full.swapaxes(0, 1).reshape(dp * tp, -1)
    kernel_full = (
        small[:, : taps * conv_own].reshape(-1, taps, conv_own).transpose(1, 0, 2).reshape(taps, -1)
    )
    offsets_full = small[:, taps * conv_own : (taps + 1) * conv_own].reshape(-1)
    gains_full = small[:, (taps + 1) * conv_own : (taps + 1) * conv_own + gains_own].reshape(-1)
    start = rank * inner
    conv_rows = jnp.concatenate([kernel_full, offsets_full[None, :]], 0)
    conv_local = jnp.concatenate(
        [lax.dynamic_slice_in_dim(conv_rows, start, inner, 1), conv_rows[:, norm_width:]], 1
    )
    head_local = lax.dynamic_slice_in_dim(head_params, rank * heads, heads, 1)
    gain_local = lax.dynamic_slice_in_dim(gains_full, depth + start, inner, 0)
    pv = jnp.concatenate(
        [
            gains_full[None, :depth],
            pad_to(jnp.concatenate([gain_local, jnp.repeat(head_local[2], head_width)]), depth)[
                None, :
            ],
            pad_to(conv_local, depth),
            pad_to(
                jnp.concatenate(
                    [pad_to(-jnp.exp(head_local[0]), LANES), pad_to(head_local[1], LANES)]
                ),
                depth,
            )[None, :],
        ],
        0,
    )

    sums, _, _, _, _, _, _, _, _, own, state_sum, vectors, head_sums, totals = run_mixer(
        activations, cotangent, w, ws, pv, dp, tp, sizes, norm_width
    )
    block_output, input_grad = run_finalize(activations, cotangent, sums, totals, norm_width)

    in_owned = own[:, : 2 * inner].reshape(shard_rows, 2, inner)
    state_part = own[:, 2 * inner : inner + conv]
    step_owned = own[:, inner + conv : inner + conv + heads].T
    out_owned = own[:, inner + conv + LANES :].T
    if state_sum.shape[0] == state_rows:
        state_owned = state_sum
    else:
        state_owned = lax.dynamic_slice_in_dim(state_part, rank * state_rows, state_rows, 0)
        for k in range(1, tp):
            theirs = lax.dynamic_slice_in_dim(state_part, (rank ^ k) * state_rows, state_rows, 0)
            state_owned = state_owned + swap(theirs, k, tp)
    head_grad = head_sums[:, :3, :heads].transpose(1, 0, 2).reshape(3, tp * heads)
    device = dp_rank * tp + rank
    conv_owned = lax.dynamic_slice(vectors, (0, device * conv_own), (taps + 1, conv_own))
    gains_owned = lax.dynamic_slice(vectors, (taps + 1, device * gains_own), (1, gains_own))[0]

    in_new = adamw_update(in_weight, in_owned, in_first, in_second, RATE_MATRIX, WEIGHT_DECAY)
    step_new = adamw_update(
        step_weight.T, step_owned, step_first.T, step_second.T, RATE_MATRIX, WEIGHT_DECAY
    )
    step_new = tuple(value.T for value in step_new)
    out_new = adamw_update(out_weight, out_owned, out_first, out_second, RATE_OUTPUT, WEIGHT_DECAY)
    state_new = adamw_update(
        state_weight, state_owned, state_first, state_second, RATE_MATRIX, WEIGHT_DECAY
    )
    conv_new = adamw_update(conv_weight, conv_owned[:taps], conv_first, conv_second, RATE_CONV, 0.0)
    bias_new = adamw_update(conv_bias, conv_owned[taps], bias_first, bias_second, RATE_VECTOR, 0.0)
    gains_new = adamw_update(gain_vector, gains_owned, gains_first, gains_second, RATE_VECTOR, 0.0)
    head_new = adamw_update(head_params, head_grad, head_first, head_second, RATE_HEADS, 0.0)
    return (
        (block_output, input_grad)
        + in_new
        + step_new
        + out_new
        + state_new
        + conv_new
        + bias_new
        + gains_new
        + head_new
    )


def solution(mesh):
    both = ("dp", "tensor")
    rows = P("dp", None)
    projection = P("dp", None, "tensor")
    step = P("dp", "tensor")
    out = P("tensor", "dp")
    state = P(both, None)
    taps = P(None, both)
    vector = P(both)
    parameters = sum(
        ((spec,) * 3 for spec in (projection, step, out, state, taps, vector, vector, P())), ()
    )
    return jax.shard_map(
        functools.partial(shards, mesh.shape["dp"], mesh.shape["tensor"]),
        mesh=mesh,
        in_specs=(rows, rows) + parameters,
        out_specs=(rows, rows) + parameters,
        check_vma=False,
    )
```
